32 devices in a mesh: groups: 2 (over x), row: 16 (over z, y, core).
Axes of the slice: x: 2, y: 2, z: 4, core: 2. Of those that a mesh axis runs over, the one named last changes fastest.
Arguments:
- pairwise_state: bfloat16 [384, 192, 128], P(('groups', 'row')), parts along dimension 0, may hold values from -6 to 6
- homolog_embedding: bfloat16 [64, 384, 64], P(None, ('groups', 'row')), parts along dimension 1, may hold values from -6 to 6
- alignment_depth: int32 [384], P('groups'), parts along dimension 0, may hold values from 0 to 64
- chain_labels: int32 [384], P('groups'), parts along dimension 0, may hold values from 0 to 7, never falling along the last dimension, each value on 1 to 48 neighbouring positions
- homolog_layer_scale: float32 [64], replicated, may hold values from 0.1 to 1.9
- homolog_layer_shift: float32 [64], replicated, may hold values from -3 to 3
- outer_source_matrix: bfloat16 [64, 32], replicated, may hold values from -0.75 to 0.75
- outer_target_matrix: bfloat16 [64, 32], replicated, may hold values from -0.75 to 0.75
- output_weight: bfloat16 [1024, 128], replicated, may hold values from -0.5 to 0.5
- output_bias: float32 [128], replicated, may hold values from -3 to 3
- chain_match: float32 [128], replicated, may hold values from -3 to 3
- pairwise_norm_gain: float32 [128], replicated, may hold values from 0.1 to 1.9
- pairwise_norm_bias: float32 [128], replicated, may hold values from -3 to 3
- input_projection_weight: bfloat16 [128, 256], replicated, may hold values from -0.5 to 0.5
- input_gate_weight: bfloat16 [128, 256], replicated, may hold values from -0.5 to 0.5
Outputs:
- pair_next: bfloat16 [384, 192, 128], P(('groups', 'row')), parts along dimension 0
- column_inputs: bfloat16 [384, 192, 256], P('groups', 'row'), parts along dimension 0
The draws below stay inside these ranges and needn't reach their ends.
There are 2 independent parts, one for each index of `groups`. The reference program is written for one: setup_inputs(seed, part) draws one part's arguments, and reference() takes and returns one part's arrays. A program takes and returns all parts, laid end to end along the dimension named above; an argument that names none is the same for every part. Nothing has to cross between parts.
Inputs may be any that keep to these rules, and one draw needn't show every extreme that they name: Sequence s is aligned for token n exactly when s < alignment_depth[n]. `chain_labels`: chain ids never fall along the tokens.
All inputs are finite; a program needn't handle non-finite values.
Results may differ from the reference program's by a relative error of at most 0.0074.
Values may be sent and summed in bfloat16 or wider, within the bound.
No kernel may reach another device: no remote copies, remote signals or barrier semaphores. Data moves between devices by JAX's collectives and lax.ppermute only.
A program may use at most 64 MiB of HBM per device.

```python
import math
import jax
import jax.numpy as jnp
import numpy as np
from jax import lax

FEATURE_WIDTH = 64
FACTOR_WIDTH = 32
CZ = 128
TRI = 128
HOMOLOG_NUMBER = 64
BLOCK_TOKENS = 12
RESIDUE_NUMBER = 192
HID = 1024
N_ROW = 16


def set_ends(values, key, low, largest):
    longest = values.shape.index(max(values.shape))
    spots = []
    for shift in (0, 1):
        where = [jax.random.randint(jax.random.fold_in(key, axis), (), 0, length) for axis, length in enumerate(values.shape)]
        where[longest] = (where[longest] + shift) % values.shape[longest]
        spots.append(tuple(where))
    return values.at[spots[0]].set(low).at[spots[1]].set(largest)


def block_levels(rng, dims, split, least, largest):
    factor_of = 1.0
    for axis_at, parts in split:
        draws = jax.random.uniform(jax.random.fold_in(jax.random.fold_in(rng, 6), axis_at), (parts,), jnp.float32, least / len(split), largest / len(split))
        factor_of = factor_of * jnp.repeat(jnp.exp(draws), dims[axis_at] // parts).reshape((-1,) + (1,) * (len(dims) - 1 - axis_at))
    return factor_of


def split_up(number_of, total, limit, slope):
    portions = [(1 << 20) // math.isqrt(standing ** slope) + 1 for standing in range(2, number_of + 1)]
    rest, given = total - limit - (number_of - 1), [1] * (number_of - 1)
    while rest > 0:
        free = [i for i in range(number_of - 1) if given[i] < limit]
        mass, left = sum([portions[i] for i in free]), rest
        for i in free:
            extra = min(limit - given[i], max(1, left * portions[i] // mass), rest)
            given[i] = given[i] + extra
            rest = rest - extra
    return np.array([limit] + given)


def ragged(key, count, total, most, lean):
    if count == 2:
        one = jax.random.randint(key, (), max(1, total - most), min(most, total - 1) + 1)
        return jnp.stack([one, total - one])
    sizes = jnp.asarray(split_up(count, total, most, lean), jnp.int32)
    pairs = (count - 1) // 2
    donor, taker = sizes[1:1 + 2 * pairs:2], sizes[2:2 + 2 * pairs:2]
    room = jnp.minimum(donor - 1, most - taker)
    passed = jax.random.randint(jax.random.fold_in(key, 1), (pairs,), 0, 1 << 20) % (room + 1)
    sizes = sizes.at[1:1 + 2 * pairs:2].set(donor - passed).at[2:2 + 2 * pairs:2].set(taker + passed)
    return sizes[jax.random.permutation(jax.random.fold_in(key, 2), count)]


def bell_draw(own_key, extent, deviation, bound, pieces=(), dtype=jnp.bfloat16):
    level = block_levels(own_key, extent, pieces, -0.22, 0.18) if pieces else 1.0
    array = jax.random.normal(own_key, extent, jnp.float32) * deviation * level
    return jnp.minimum(jnp.maximum(array, -bound), bound).astype(dtype)


def setup_inputs(seed: int = 0, part: int = 0) -> dict:
    arg_keys = jax.random.split(jax.random.key(seed), 16)
    part_splits = jax.random.split(jax.random.fold_in(arg_keys[15], part), 16)
    return {
        "pairwise_state": bell_draw(part_splits[0], (RESIDUE_NUMBER, RESIDUE_NUMBER, CZ), 1.0, 6.0, ((0, 16),)),
        "homolog_embedding": bell_draw(part_splits[1], (HOMOLOG_NUMBER, RESIDUE_NUMBER, FEATURE_WIDTH), 1.0, 6.0, ((1, 16),)),
        "alignment_depth": set_ends(jax.random.randint(part_splits[2], (RESIDUE_NUMBER,), 0, HOMOLOG_NUMBER + 1), jax.random.fold_in(part_splits[2], 1), 0, HOMOLOG_NUMBER).astype(jnp.int32),
        "chain_labels": jnp.searchsorted(jnp.cumsum(ragged(part_splits[3], 8, RESIDUE_NUMBER, RESIDUE_NUMBER // 4, 2)), jnp.arange(RESIDUE_NUMBER), side="right").astype(jnp.int32),
        "homolog_layer_scale": jnp.clip(1.0 + 0.18 * jax.random.normal(arg_keys[4], (FEATURE_WIDTH,), jnp.float32), 0.1, 1.9),
        "homolog_layer_shift": bell_draw(arg_keys[5], (FEATURE_WIDTH,), 0.3, 3.0, (), jnp.float32),
        "outer_source_matrix": bell_draw(arg_keys[6], (FEATURE_WIDTH, FACTOR_WIDTH), FEATURE_WIDTH ** -0.5, 0.75),
        "outer_target_matrix": bell_draw(arg_keys[7], (FEATURE_WIDTH, FACTOR_WIDTH), FEATURE_WIDTH ** -0.5, 0.75),
        "output_weight": bell_draw(arg_keys[8], (HID, CZ), (FACTOR_WIDTH * 4) ** -0.5, 0.5),
        "output_bias": bell_draw(arg_keys[9], (CZ,), 0.5, 3.0, (), jnp.float32),
        "chain_match": bell_draw(arg_keys[10], (CZ,), 0.5, 3.0, (), jnp.float32),
        "pairwise_norm_gain": jnp.clip(1.0 + 0.18 * jax.random.normal(arg_keys[11], (CZ,), jnp.float32), 0.1, 1.9),
        "pairwise_norm_bias": bell_draw(arg_keys[12], (CZ,), 0.3, 3.0, (), jnp.float32),
        "input_projection_weight": bell_draw(arg_keys[13], (CZ, 2 * TRI), CZ ** -0.5, 0.5),
        "input_gate_weight": bell_draw(arg_keys[14], (CZ, 2 * TRI), CZ ** -0.5, 0.5),
    }


def normalized_rows(values, gain, shift):
    centre = values - lax.optimization_barrier(jnp.mean(values, axis=-1, keepdims=True))
    spread = lax.optimization_barrier(jnp.mean(centre * centre, axis=-1, keepdims=True))
    return centre * lax.rsqrt(spread + 1e-05) * gain + shift

def reference(pairwise_state, homolog_embedding, alignment_depth, chain_labels, homolog_layer_scale, homolog_layer_shift, outer_source_matrix, outer_target_matrix, output_weight, output_bias, chain_match, pairwise_norm_gain, pairwise_norm_bias, input_projection_weight, input_gate_weight):
    normalized_input = normalized_rows(homolog_embedding.astype(jnp.float32), homolog_layer_scale, homolog_layer_shift).astype(jnp.bfloat16)
    sequence_index = lax.broadcasted_iota(jnp.int32, (HOMOLOG_NUMBER, RESIDUE_NUMBER), 0)
    sequence_mask = (sequence_index < alignment_depth[None, :].astype(jnp.int32)).astype(jnp.float32)
    left_projected = jnp.einsum('snc,cd->nsd', normalized_input.astype(jnp.float32), outer_source_matrix.astype(jnp.float32)) * sequence_mask.T[:, :, None]
    right_proj = jnp.einsum('snc,cd->nsd', normalized_input.astype(jnp.float32), outer_target_matrix.astype(jnp.float32)) * sequence_mask.T[:, :, None]
    left_projected = left_projected.astype(jnp.bfloat16)
    right_proj = right_proj.astype(jnp.bfloat16)

    def one_block(inputs):
        left_block, block_of_depth = inputs
        shared_terms = jnp.maximum(jnp.minimum(block_of_depth[:, None], alignment_depth[None, :]), 1).astype(jnp.float32)
        outer_sum = jnp.einsum('isc,jsd->ijcd', left_block.astype(jnp.float32), right_proj.astype(jnp.float32))
        outer_sum = (outer_sum / shared_terms[:, :, None, None]).astype(jnp.bfloat16)
        outer_sum = outer_sum.reshape(BLOCK_TOKENS, RESIDUE_NUMBER, HID)
        return jnp.einsum('ijh,he->ije', outer_sum.astype(jnp.float32), output_weight.astype(jnp.float32))
    block_list = (left_projected.reshape(N_ROW, BLOCK_TOKENS, HOMOLOG_NUMBER, FACTOR_WIDTH), alignment_depth.reshape(N_ROW, BLOCK_TOKENS))
    outer_proj = lax.map(one_block, block_list).reshape(RESIDUE_NUMBER, RESIDUE_NUMBER, CZ)
    same = (chain_labels[:, None] == chain_labels[None, :]).astype(jnp.float32)
    pair_next = pairwise_state.astype(jnp.float32) + same[:, :, None] * chain_match + outer_proj + output_bias
    pair_next = pair_next.astype(jnp.bfloat16)
    tri_normed = normalized_rows(pair_next.astype(jnp.float32), pairwise_norm_gain, pairwise_norm_bias).astype(jnp.bfloat16)
    projected = jnp.dot(tri_normed, input_projection_weight, preferred_element_type=jnp.float32)
    gating = jnp.dot(tri_normed, input_gate_weight, preferred_element_type=jnp.float32)
    column_inputs = (projected * jax.nn.sigmoid(gating)).astype(jnp.bfloat16)
    return (pair_next, column_inputs)
```

```python
import functools

import jax
import jax.numpy as jnp
from jax import lax
from jax.experimental import pallas as pl
from jax.experimental.pallas import tpu as pltpu
from jax.sharding import PartitionSpec as P

F32 = jnp.float32
BF16 = jnp.bfloat16
NT = (((1,), (1,)), ((), ()))
VMEM = pltpu.VMEM
SMEM = pltpu.SMEM
LIMIT = 48 * 1024 * 1024


def whole(space):
    return pl.BlockSpec(memory_space=space)


def params(**kw):
    return pltpu.CompilerParams(vmem_limit_bytes=LIMIT, **kw)


def project_kernel(
    row_ref, depth_ref, hom_ref, scale_ref, shift_ref, src_ref, tgt_ref, left_ref, right_ref, packed_ref, tmp_ref
):
    tokens, seqs, feats = hom_ref.shape
    width = src_ref.shape[0]
    half = width // 2
    values = hom_ref[...].astype(F32).reshape(tokens * seqs, feats)
    centre = values - jnp.mean(values, axis=-1, keepdims=True)
    spread = jnp.mean(centre * centre, axis=-1, keepdims=True)
    normed = (centre * lax.rsqrt(spread + 1e-05) * scale_ref[...] + shift_ref[...]).astype(BF16)
    left = lax.dot_general(normed, src_ref[...], NT, preferred_element_type=F32)
    right = lax.dot_general(normed, tgt_ref[...], NT, preferred_element_type=F32)
    both = jnp.concatenate([src_ref[...], tgt_ref[...]], axis=0)
    first = row_ref[0] * tokens
    row_pos = lax.broadcasted_iota(jnp.int32, (seqs, width), 0)
    lane_pos = lax.broadcasted_iota(jnp.int32, (2 * width, seqs), 1)
    tmp_ref[...] = jnp.zeros_like(tmp_ref)
    for n in range(tokens):
        depth = depth_ref[first + n]
        rows = slice(n * seqs, (n + 1) * seqs)
        left_ref[rows] = jnp.where(row_pos < depth, left[rows], 0.0).astype(BF16)
        right_ref[rows] = jnp.where(row_pos < depth, right[rows], 0.0).astype(BF16)
        turned = lax.dot_general(both, normed[rows], NT, preferred_element_type=F32)
        turned = jnp.where(lane_pos < depth, turned, 0.0)
        tmp_ref[n, 0:half] = jnp.concatenate([turned[0:half], turned[half:width]], axis=1)
        tmp_ref[n, half:width] = jnp.concatenate(
            [turned[width : width + half], turned[width + half :]], axis=1
        )
    for q in range(width):
        packed_ref[:, q * 2 * seqs : (q + 1) * 2 * seqs] = tmp_ref[:, q, :].astype(BF16)


def tiles_kernel(row_ref, state_ref, *rest):
    count = (len(rest) - 4) // 1
    outs, (wide_ref, msg_ref, narrow_ref, sems) = rest[:count], rest[count:]
    tokens = state_ref.shape[0]
    wide_ref[...] = state_ref[...].astype(F32)
    for d in range(count):
        for i in range(tokens):
            msg_ref[i * tokens : (i + 1) * tokens] = wide_ref[i, d * tokens : (d + 1) * tokens, :]
        narrow_ref[d] = msg_ref[...].astype(BF16)
    row = row_ref[0]
    copies = [
        pltpu.make_async_copy(narrow_ref.at[row ^ k], outs[k], sems.at[k]) for k in range(count)
    ]
    for copy in copies:
        copy.start()
    for copy in copies:
        copy.wait()


def mix_kernel(left_ref, right_ref, turned_ref, weight_ref, y_ref, z_ref):
    q = pl.program_id(0)
    half = pl.num_programs(0)
    seqs = y_ref.shape[0] // 2
    width = weight_ref.shape[2]
    tokens = left_ref.shape[0] // seqs
    for lhs, w_ref, out_ref in ((left_ref, turned_ref, y_ref), (right_ref, weight_ref, z_ref)):
        pair = jnp.concatenate([w_ref[q], w_ref[q + half]], axis=1)
        mixed = jnp.dot(lhs[...], pair, preferred_element_type=F32).astype(BF16)
        for n in range(tokens):
            rows = slice(n * seqs, (n + 1) * seqs)
            cols = slice(n * width, (n + 1) * width)
            out_ref[0:seqs, cols] = mixed[rows, 0:width]
            out_ref[seqs : 2 * seqs, cols] = mixed[rows, width : 2 * width]


def pair_kernel(row_ref, depth_ref, chain_ref, depth_col, chain_col, match_ref, bias_ref, state_ref, y_ref, z_ref, *rest):
    items, (next_ref, col_ref, all_ref, inv_ref, close_ref, sems) = rest[:-6], rest[-6:]
    step = pl.program_id(0)
    row = row_ref[0]
    count = len(items)
    pad = items[0].shape[0]
    inner = y_ref.shape[0]
    block, total, width = state_ref.shape
    tokens = total // count

    @pl.when(step == 0)
    def _():
        copies = [
            pltpu.make_async_copy(
                items[k], all_ref.at[pl.ds(pl.multiple_of((row ^ k) * pad, pad), pad)], sems.at[k]
            )
            for k in range(count)
        ]
        for copy in copies:
            copy.start()
        inv_ref[...] = 1.0 / jnp.maximum(
            jnp.broadcast_to(depth_col[...], inv_ref.shape).astype(F32), 1.0
        )
        for copy in copies:
            copy.wait()

    for cols, w_ref, out_ref, is_row in (
        (slice(inner, 2 * inner), y_ref, next_ref, True),
        (slice(0, inner), z_ref, col_ref, False),
    ):
        prod = jnp.dot(all_ref[:, cols], w_ref[...], preferred_element_type=F32)
        for t in range(block):
            own = row * tokens + step * block + t
            inv_own = 1.0 / jnp.maximum(jnp.full((1, width), depth_ref[own], jnp.int32).astype(F32), 1.0)
            lanes = slice(t * width, (t + 1) * width)
            for s in range(count):
                close_ref[s * tokens : (s + 1) * tokens] = prod[s * pad : s * pad + tokens, lanes]
            extra = jnp.where(chain_col[...] == chain_ref[own], match_ref[...], 0.0) + bias_ref[...]
            value = close_ref[...] * jnp.maximum(inv_ref[...], inv_own) + extra
            if is_row:
                out_ref[t] = (state_ref[t].astype(F32) + value).astype(BF16)
            else:
                out_ref[t] = value


def gate_kernel(row_ref, col_ref, gain_ref, shift_ref, proj_ref, gate_ref, *rest):
    tiles, (out_ref, msg_ref, wide_ref, sems) = rest[:-4], rest[-4:]
    step = pl.program_id(0)
    row = row_ref[0]
    count = len(tiles)
    rows = tiles[0].shape[0]
    total, width = col_ref.shape[1:]
    tokens = total // count

    @pl.when(step == 0)
    def _():
        copies = [
            pltpu.make_async_copy(tiles[k], msg_ref.at[row ^ k], sems.at[k]) for k in range(count)
        ]
        for copy in copies:
            copy.start()
        for copy in copies:
            copy.wait()
        for s in range(count):
            wide_ref[s * rows : (s + 1) * rows] = msg_ref[s].astype(F32)

    state = wide_ref[pl.ds(step, total, stride=tokens), :]
    pair = (state + col_ref[0]).astype(BF16)
    ones = jnp.full((width, width), 1.0 / width, BF16)
    centre = pair.astype(F32) - jnp.dot(pair, ones, preferred_element_type=F32)
    square = centre * centre
    high = square.astype(BF16)
    low = (square - high.astype(F32)).astype(BF16)
    spread = jnp.dot(
        jnp.concatenate([high, low], axis=1),
        jnp.concatenate([ones, ones], axis=0),
        preferred_element_type=F32,
    )
    normed = (centre * lax.rsqrt(spread + 1e-05) * gain_ref[...] + shift_ref[...]).astype(BF16)
    projected = jnp.dot(normed, proj_ref[...], preferred_element_type=F32)
    gating = jnp.dot(normed, gate_ref[...], preferred_element_type=F32)
    out_ref[0] = (projected * (0.5 + 0.5 * jnp.tanh(0.5 * gating))).astype(BF16)


def body(
    pairwise_state,
    homolog_embedding,
    alignment_depth,
    chain_labels,
    homolog_layer_scale,
    homolog_layer_shift,
    outer_source_matrix,
    outer_target_matrix,
    output_weight,
    output_bias,
    chain_match,
    pairwise_norm_gain,
    pairwise_norm_bias,
    input_projection_weight,
    input_gate_weight,
    *,
    count,
):
    tokens, total, width = pairwise_state.shape
    seqs, _, feats = homolog_embedding.shape
    factor = outer_source_matrix.shape[1]
    half = factor // 2
    pad = -(-tokens // 16) * 16
    inner = factor * seqs
    gated = input_projection_weight.shape[1]
    row = lax.axis_index("row").astype(jnp.int32).reshape(1)

    def swap(array, bit):
        return lax.ppermute(array, "row", [(r, r ^ bit) for r in range(count)])

    left, right, packed = pl.pallas_call(
        project_kernel,
        out_shape=(
            jax.ShapeDtypeStruct((tokens * seqs, factor), BF16),
            jax.ShapeDtypeStruct((tokens * seqs, factor), BF16),
            jax.ShapeDtypeStruct((pad, 2 * inner), BF16),
        ),
        in_specs=[whole(SMEM), whole(SMEM)] + [whole(VMEM)] * 5,
        out_specs=(whole(VMEM),) * 3,
        scratch_shapes=[VMEM((pad, factor, 2 * seqs), F32)],
        compiler_params=params(),
        name="project",
    )(
        row,
        alignment_depth,
        homolog_embedding.transpose(1, 0, 2),
        homolog_layer_scale.reshape(1, feats),
        homolog_layer_shift.reshape(1, feats),
        outer_source_matrix.T,
        outer_target_matrix.T,
    )
    items = {0: packed}
    bit = count // 2
    while bit:
        for k in sorted(items):
            items[k | bit] = swap(items[k], bit)
        bit //= 2

    tiles = pl.pallas_call(
        tiles_kernel,
        out_shape=tuple(jax.ShapeDtypeStruct((tokens * tokens, width), BF16) for _ in range(count)),
        in_specs=[whole(SMEM), whole(VMEM)],
        out_specs=(whole(pl.ANY),) * count,
        scratch_shapes=[
            VMEM((tokens, total, width), F32),
            VMEM((tokens * tokens, width), F32),
            VMEM((count, tokens * tokens, width), BF16),
            pltpu.SemaphoreType.DMA((count,)),
        ],
        compiler_params=params(),
        name="tiles",
    )(row, pairwise_state)
    tiles = [tiles[0]] + [swap(tiles[k], k) for k in range(1, count)]

    weight = output_weight.reshape(factor, factor, width)
    y, z = pl.pallas_call(
        mix_kernel,
        grid=(half,),
        out_shape=(jax.ShapeDtypeStruct((inner, tokens * width), BF16),) * 2,
        in_specs=[whole(VMEM)] * 4,
        out_specs=(pl.BlockSpec((2 * seqs, tokens * width), lambda q: (q, 0)),) * 2,
        compiler_params=params(),
        cost_estimate=pl.CostEstimate(
            flops=4 * tokens * seqs * factor * factor * width,
            bytes_accessed=4 * inner * tokens * width,
            transcendentals=0,
        ),
        name="mix",
    )(left, right, weight.transpose(1, 0, 2), weight)

    block = 2
    steps = tokens // block
    pair_next, columns = pl.pallas_call(
        pair_kernel,
        grid=(steps,),
        out_shape=(
            jax.ShapeDtypeStruct((tokens, total, width), BF16),
            jax.ShapeDtypeStruct((tokens, total, width), F32),
        ),
        in_specs=[whole(SMEM)] * 3
        + [whole(VMEM)] * 4
        + [
            pl.BlockSpec((block, total, width), lambda g: (g, 0, 0)),
            pl.BlockSpec((inner, block * width), lambda g: (0, g)),
            pl.BlockSpec((inner, block * width), lambda g: (0, g)),
        ]
        + [whole(pl.ANY)] * count,
        out_specs=(pl.BlockSpec((block, total, width), lambda g: (g, 0, 0)),) * 2,
        scratch_shapes=[
            VMEM((count * pad, 2 * inner), BF16),
            VMEM((total, width), F32),
            VMEM((total, width), F32),
            pltpu.SemaphoreType.DMA((count,)),
        ],
        compiler_params=params(),
        cost_estimate=pl.CostEstimate(
            flops=4 * count * pad * inner * tokens * width,
            bytes_accessed=4 * inner * tokens * width + 8 * tokens * total * width,
            transcendentals=0,
        ),
        name="pair",
    )(
        row,
        alignment_depth,
        chain_labels,
        alignment_depth.reshape(total, 1),
        chain_labels.reshape(total, 1),
        chain_match.reshape(1, width),
        output_bias.reshape(1, width),
        pairwise_state,
        y,
        z,
        *[items[k] for k in range(count)],
    )

    out = pl.pallas_call(
        gate_kernel,
        grid=(tokens,),
        out_shape=jax.ShapeDtypeStruct((tokens, total, gated), BF16),
        in_specs=[whole(SMEM), pl.BlockSpec((1, total, width), lambda j: (j, 0, 0))]
        + [whole(VMEM)] * 4
        + [whole(pl.ANY)] * count,
        out_specs=pl.BlockSpec((1, total, gated), lambda j: (j, 0, 0)),
        scratch_shapes=[
            VMEM((count, tokens * tokens, width), BF16),
            VMEM((count * tokens * tokens, width), F32),
            pltpu.SemaphoreType.DMA((count,)),
        ],
        compiler_params=params(),
        cost_estimate=pl.CostEstimate(
            flops=4 * tokens * total * width * gated,
            bytes_accessed=tokens * total * (2 * gated + 6 * width),
            transcendentals=tokens * total * gated,
        ),
        name="gate",
    )(
        row,
        columns,
        pairwise_norm_gain.reshape(1, width),
        pairwise_norm_bias.reshape(1, width),
        input_projection_weight,
        input_gate_weight,
        *tiles,
    )
    return pair_next, out.transpose(1, 0, 2)


def solution(mesh):
    return jax.shard_map(
        functools.partial(body, count=mesh.shape["row"]),
        mesh=mesh,
        in_specs=(
            P(("groups", "row"), None, None),
            P(None, ("groups", "row"), None),
            P("groups"),
            P("groups"),
        )
        + (P(),) * 11,
        out_specs=(P(("groups", "row"), None, None), P("groups", "row", None)),
        check_vma=False,
    )
```

```python
import functools

import jax
import jax.numpy as jnp
from jax import lax
from jax.experimental import pallas as pl
from jax.experimental.pallas import tpu as pltpu
from jax.sharding import PartitionSpec as P

F32 = jnp.float32
BF16 = jnp.bfloat16
NT = (((1,), (1,)), ((), ()))
VMEM = pltpu.VMEM
SMEM = pltpu.SMEM
LIMIT = 48 * 1024 * 1024


def whole(space):
    return pl.BlockSpec(memory_space=space)


def params(**kw):
    return pltpu.CompilerParams(vmem_limit_bytes=LIMIT, **kw)


def project_kernel(
    row_ref, depth_ref, hom_ref, scale_ref, shift_ref, src_ref, tgt_ref, left_ref, right_ref, packed_ref, tmp_ref
):
    tokens, seqs, feats = hom_ref.shape
    width = src_ref.shape[0]
    half = width // 2
    values = hom_ref[...].astype(F32).reshape(tokens * seqs, feats)
    centre = values - jnp.mean(values, axis=-1, keepdims=True)
    spread = jnp.mean(centre * centre, axis=-1, keepdims=True)
    normed = (centre * lax.rsqrt(spread + 1e-05) * scale_ref[...] + shift_ref[...]).astype(BF16)
    left = lax.dot_general(normed, src_ref[...], NT, preferred_element_type=F32)
    right = lax.dot_general(normed, tgt_ref[...], NT, preferred_element_type=F32)
    both = jnp.concatenate([src_ref[...], tgt_ref[...]], axis=0)
    first = row_ref[0] * tokens
    row_pos = lax.broadcasted_iota(jnp.int32, (seqs, width), 0)
    lane_pos = lax.broadcasted_iota(jnp.int32, (2 * width, seqs), 1)
    for n in range(tokens):
        depth = depth_ref[first + n]
        rows = slice(n * seqs, (n + 1) * seqs)
        left_ref[rows] = jnp.where(row_pos < depth, left[rows], 0.0).astype(BF16)
        right_ref[rows] = jnp.where(row_pos < depth, right[rows], 0.0).astype(BF16)
        turned = lax.dot_general(both, normed[rows], NT, preferred_element_type=F32)
        turned = jnp.where(lane_pos < depth, turned, 0.0)
        tmp_ref[0, n] = jnp.concatenate([turned[0:half], turned[half:width]], axis=1)
        tmp_ref[1, n] = jnp.concatenate(
            [turned[width : width + half], turned[width + half :]], axis=1
        )
    for q in range(half):
        packed_ref[:, q * 2 * seqs : (q + 1) * 2 * seqs] = jnp.concatenate(
            [tmp_ref[0, :, q, :], tmp_ref[1, :, q, :]], axis=0
        ).astype(BF16)


def tiles_kernel(state_ref, out_ref, wide_ref, msg_ref):
    count = out_ref.shape[0]
    tokens = state_ref.shape[0]
    wide_ref[...] = state_ref[...].astype(F32)
    for d in range(count):
        for i in range(tokens):
            msg_ref[d, i * tokens : (i + 1) * tokens] = wide_ref[i, d * tokens : (d + 1) * tokens, :]
        out_ref[d] = msg_ref[d].astype(BF16)


def mix_kernel(left_ref, right_ref, weight_ref, y_ref, z_ref, wide_ref):
    step = pl.program_id(0)
    factor = left_ref.shape[1]
    half = factor // 2
    seqs = y_ref.shape[0] * pl.num_programs(0) // factor
    width = weight_ref.shape[1]
    per = y_ref.shape[0] // (2 * seqs)
    tokens = left_ref.shape[0] // seqs
    wide_ref[...] = weight_ref[...].astype(F32)
    for p in range(per):
        q = step * per + p
        pairs = (
            [wide_ref[pl.ds(q + t * half, factor, stride=factor), :] for t in (0, 1)],
            [wide_ref[pl.ds(pl.multiple_of((q + t * half) * factor, factor), factor), :] for t in (0, 1)],
        )
        for lhs, pair, out_ref in ((left_ref, pairs[0], y_ref), (right_ref, pairs[1], z_ref)):
            rhs = jnp.concatenate(pair, axis=1).astype(BF16)
            mixed = jnp.dot(lhs[...], rhs, preferred_element_type=F32).astype(BF16)
            for n in range(tokens):
                rows = slice(n * seqs, (n + 1) * seqs)
                cols = slice(n * width, (n + 1) * width)
                low = 2 * p * seqs
                out_ref[low : low + seqs, cols] = mixed[rows, 0:width]
                out_ref[low + seqs : low + 2 * seqs, cols] = mixed[rows, width : 2 * width]


def pair_kernel(
    row_ref, depth_ref, chain_ref, depth_row, chain_row, match_ref, bias_ref, state_ref, lhs_left, lhs_right, y_ref, z_ref,
    next_ref, col_ref, inv_ref, chain_col,
):
    step = pl.program_id(0)
    block, total, width = state_ref.shape
    own_first = row_ref[0] * (block * pl.num_programs(0)) + step * block

    @pl.when(step == 0)
    def _():
        same = lax.broadcasted_iota(jnp.int32, (total, total), 0) == lax.broadcasted_iota(
            jnp.int32, (total, total), 1
        )
        ones = jnp.ones((total, width), BF16)

        def column(ref):
            spread = jnp.where(same, ref[...].astype(F32), 0.0).astype(BF16)
            return jnp.dot(spread, ones, preferred_element_type=F32)

        inv_ref[...] = 1.0 / jnp.maximum(column(depth_row), 1.0)
        chain_col[...] = column(chain_row)

    for lhs, w_ref, out_ref, is_row in (
        (lhs_right, y_ref, next_ref, True),
        (lhs_left, z_ref, col_ref, False),
    ):
        for t in range(block):
            if t % 2 == 0:
                prod = jnp.dot(
                    lhs[...], w_ref[:, t * width : (t + 2) * width], preferred_element_type=F32
                )
            own = own_first + t
            inv_own = 1.0 / jnp.maximum(jnp.full((1, width), depth_ref[own], jnp.int32).astype(F32), 1.0)
            label = jnp.full((1, width), chain_ref[own], jnp.int32).astype(F32)
            extra = jnp.where(chain_col[...] == label, match_ref[...], 0.0) + bias_ref[...]
            value = prod[:, t % 2 * width : (t % 2 + 1) * width] * jnp.maximum(inv_ref[...], inv_own) + extra
            if is_row:
                out_ref[t] = (state_ref[t].astype(F32) + value).astype(BF16)
            else:
                out_ref[t] = value


def gate_kernel(col_ref, gain_ref, shift_ref, proj_ref, gate_ref, tiles_ref, out_ref, wide_ref):
    step = pl.program_id(0)
    count, rows, width = tiles_ref.shape
    block, total = col_ref.shape[:2]
    tokens = total // count

    @pl.when(step == 0)
    def _():
        wide_ref[...] = tiles_ref[...].astype(F32).reshape(count * rows, width)

    ones = jnp.full((width, width), 1.0 / width, BF16)
    none = jnp.zeros((width, width), BF16)
    means = jnp.concatenate(
        [jnp.concatenate([ones, none], axis=1), jnp.concatenate([none, ones], axis=1)], axis=0
    )
    for t in range(0, block, 2):
        halves = []
        for u in (0, 1):
            state = wide_ref[pl.ds(step * block + t + u, total, stride=tokens), :]
            halves.append(state + col_ref[t + u])
        pair = jnp.concatenate(halves, axis=1).astype(BF16)
        centre = pair.astype(F32) - jnp.dot(pair, means, preferred_element_type=F32)
        square = (centre * centre).astype(BF16)
        spread = jnp.dot(square, means, preferred_element_type=F32)
        scaled = centre * lax.rsqrt(spread + 1e-05)
        for u in (0, 1):
            normed = scaled[:, u * width : (u + 1) * width] * gain_ref[...] + shift_ref[...]
            normed = normed.astype(BF16)
            projected = jnp.dot(normed, proj_ref[...], preferred_element_type=F32)
            gating = jnp.dot(normed, gate_ref[...], preferred_element_type=F32)
            out_ref[t + u] = (projected * (0.5 + 0.5 * jnp.tanh(0.5 * gating))).astype(BF16)


def fixed(*shape):
    return pl.BlockSpec(shape, lambda g: (0,) * len(shape))


def body(
    pairwise_state,
    homolog_embedding,
    alignment_depth,
    chain_labels,
    homolog_layer_scale,
    homolog_layer_shift,
    outer_source_matrix,
    outer_target_matrix,
    output_weight,
    output_bias,
    chain_match,
    pairwise_norm_gain,
    pairwise_norm_bias,
    input_projection_weight,
    input_gate_weight,
    *,
    count,
):
    tokens, total, width = pairwise_state.shape
    seqs, _, feats = homolog_embedding.shape
    factor = outer_source_matrix.shape[1]
    half = factor // 2
    inner = factor * seqs
    gated = input_projection_weight.shape[1]
    row = lax.axis_index("row").astype(jnp.int32).reshape(1)

    left, right, packed = pl.pallas_call(
        project_kernel,
        grid=(1,),
        out_shape=(
            jax.ShapeDtypeStruct((tokens * seqs, factor), BF16),
            jax.ShapeDtypeStruct((tokens * seqs, factor), BF16),
            jax.ShapeDtypeStruct((2 * tokens, inner), BF16),
        ),
        in_specs=[
            whole(SMEM),
            whole(SMEM),
            fixed(tokens, seqs, feats),
            fixed(1, feats),
            fixed(1, feats),
            fixed(factor, feats),
            fixed(factor, feats),
        ],
        out_specs=(fixed(tokens * seqs, factor), fixed(tokens * seqs, factor), fixed(2 * tokens, inner)),
        scratch_shapes=[VMEM((2, tokens, half, 2 * seqs), F32)],
        compiler_params=params(),
        name="project",
    )(
        row,
        alignment_depth,
        homolog_embedding.transpose(1, 0, 2),
        homolog_layer_scale.reshape(1, feats),
        homolog_layer_shift.reshape(1, feats),
        outer_source_matrix.T,
        outer_target_matrix.T,
    )
    gathered = lax.all_gather(packed, "row", axis=0, tiled=False)
    all_left = gathered[:, :tokens].reshape(total, inner)
    all_right = gathered[:, tokens:].reshape(total, inner)

    tiles = pl.pallas_call(
        tiles_kernel,
        grid=(1,),
        out_shape=jax.ShapeDtypeStruct((count, tokens * tokens, width), BF16),
        in_specs=[fixed(tokens, total, width)],
        out_specs=fixed(count, tokens * tokens, width),
        scratch_shapes=[
            VMEM((tokens, total, width), F32),
            VMEM((count, tokens * tokens, width), F32),
        ],
        compiler_params=params(),
        name="tiles",
    )(pairwise_state)
    tiles = lax.all_to_all(tiles, "row", split_axis=0, concat_axis=0, tiled=True)

    parts = 4
    y, z = pl.pallas_call(
        mix_kernel,
        grid=(parts,),
        out_shape=(jax.ShapeDtypeStruct((inner, tokens * width), BF16),) * 2,
        in_specs=[
            fixed(tokens * seqs, factor),
            fixed(tokens * seqs, factor),
            fixed(factor * factor, width),
        ],
        out_specs=(pl.BlockSpec((inner // parts, tokens * width), lambda q: (q, 0)),) * 2,
        scratch_shapes=[VMEM((factor * factor, width), F32)],
        compiler_params=params(),
        cost_estimate=pl.CostEstimate(
            flops=4 * tokens * seqs * factor * factor * width,
            bytes_accessed=4 * inner * tokens * width,
            transcendentals=0,
        ),
        name="mix",
    )(left, right, output_weight)

    block = 4
    pair_next, columns = pl.pallas_call(
        pair_kernel,
        grid=(tokens // block,),
        out_shape=(
            jax.ShapeDtypeStruct((tokens, total, width), BF16),
            jax.ShapeDtypeStruct((tokens, total, width), F32),
        ),
        in_specs=[whole(SMEM)] * 3
        + [
            fixed(1, total),
            fixed(1, total),
            fixed(1, width),
            fixed(1, width),
            pl.BlockSpec((block, total, width), lambda g: (g, 0, 0)),
            fixed(total, inner),
            fixed(total, inner),
            pl.BlockSpec((inner, block * width), lambda g: (0, g)),
            pl.BlockSpec((inner, block * width), lambda g: (0, g)),
        ],
        out_specs=(pl.BlockSpec((block, total, width), lambda g: (g, 0, 0)),) * 2,
        scratch_shapes=[VMEM((total, width), F32), VMEM((total, width), F32)],
        compiler_params=params(),
        cost_estimate=pl.CostEstimate(
            flops=4 * total * inner * tokens * width,
            bytes_accessed=4 * inner * tokens * width + 8 * tokens * total * width,
            transcendentals=0,
        ),
        name="pair",
    )(
        row,
        alignment_depth,
        chain_labels,
        alignment_depth.reshape(1, total),
        chain_labels.reshape(1, total),
        chain_match.reshape(1, width),
        output_bias.reshape(1, width),
        pairwise_state,
        all_left,
        all_right,
        y,
        z,
    )

    out = pl.pallas_call(
        gate_kernel,
        grid=(tokens // block,),
        out_shape=jax.ShapeDtypeStruct((tokens, total, gated), BF16),
        in_specs=[
            pl.BlockSpec((block, total, width), lambda j: (j, 0, 0)),
            fixed(1, width),
            fixed(1, width),
            fixed(width, gated),
            fixed(width, gated),
            fixed(count, tokens * tokens, width),
        ],
        out_specs=pl.BlockSpec((block, total, gated), lambda j: (j, 0, 0)),
        scratch_shapes=[VMEM((count * tokens * tokens, width), F32)],
        compiler_params=params(),
        cost_estimate=pl.CostEstimate(
            flops=4 * tokens * total * width * gated,
            bytes_accessed=tokens * total * (2 * gated + 6 * width),
            transcendentals=tokens * total * gated,
        ),
        name="gate",
    )(
        columns,
        pairwise_norm_gain.reshape(1, width),
        pairwise_norm_bias.reshape(1, width),
        input_projection_weight,
        input_gate_weight,
        tiles,
    )
    return pair_next, out.transpose(1, 0, 2)


def solution(mesh):
    return jax.shard_map(
        functools.partial(body, count=mesh.shape["row"]),
        mesh=mesh,
        in_specs=(
            P(("groups", "row"), None, None),
            P(None, ("groups", "row"), None),
            P("groups"),
            P("groups"),
        )
        + (P(),) * 11,
        out_specs=(P(("groups", "row"), None, None), P("groups", "row", None)),
        check_vma=False,
    )
```

```python
import functools

import jax
import jax.numpy as jnp
from jax import lax
from jax.experimental import pallas as pl
from jax.experimental.pallas import tpu as pltpu
from jax.sharding import PartitionSpec as P

F32 = jnp.float32
BF16 = jnp.bfloat16
NT = (((1,), (1,)), ((), ()))
VMEM = pltpu.VMEM
SMEM = pltpu.SMEM
HBM = pltpu.HBM
LANES = 128


def whole(space):
    return pl.BlockSpec(memory_space=space)


def params(mib):
    return pltpu.CompilerParams(vmem_limit_bytes=mib * 1024 * 1024)


def fetch(sems, *pairs):
    copies = [pltpu.make_async_copy(a, b, sems.at[n]) for n, (a, b) in enumerate(pairs)]
    for copy in copies:
        copy.start()
    return copies


def finish(copies):
    for copy in copies:
        copy.wait()


def project_kernel(
    row_ref, depth_hbm, hom_hbm, scale_hbm, shift_hbm, src_hbm, tgt_hbm,
    left_ref, right_ref, item_ref,
    depth_ref, hom_ref, scale_ref, shift_ref, both_ref, sems,
):
    tokens, seqs, feats = hom_ref.shape
    width = src_hbm.shape[0]
    half = width // 2
    finish(
        fetch(
            sems,
            (hom_hbm, hom_ref),
            (depth_hbm, depth_ref),
            (scale_hbm, scale_ref),
            (shift_hbm, shift_ref),
            (src_hbm, both_ref.at[0:width]),
            (tgt_hbm, both_ref.at[width : 2 * width]),
        )
    )
    values = hom_ref[...].reshape(tokens * seqs, feats)
    ones = jnp.full((feats, feats), 1.0 / feats, BF16)
    centre = values.astype(F32) - jnp.dot(values, ones, preferred_element_type=F32)
    square = centre * centre
    high = square.astype(BF16)
    low = (square - high.astype(F32)).astype(BF16)
    spread = jnp.dot(high, ones, preferred_element_type=F32) + jnp.dot(
        low, ones, preferred_element_type=F32
    )
    normed = (centre * lax.rsqrt(spread + 1e-05) * scale_ref[...] + shift_ref[...]).astype(BF16)
    both = both_ref[...]
    turned = lax.dot_general(both, normed, NT, preferred_element_type=F32)
    plain = lax.dot_general(normed, both, NT, preferred_element_type=F32)
    first = row_ref[0] * tokens
    row_pos = lax.broadcasted_iota(jnp.int32, (seqs, width), 0)
    lane = lax.broadcasted_iota(jnp.int32, (half, 2 * seqs), 1)
    front = lane < seqs
    seq_pos = jnp.where(front, lane, lane - seqs)
    for n in range(tokens):
        depth = depth_ref[first + n]
        rows = slice(n * seqs, (n + 1) * seqs)
        left_ref[rows] = jnp.where(row_pos < depth, plain[rows, 0:width], 0.0).astype(BF16)
        right_ref[rows] = jnp.where(row_pos < depth, plain[rows, width : 2 * width], 0.0).astype(BF16)
        keep = seq_pos < depth
        for side in (0, 1):
            upper = turned[side * width : side * width + half, rows]
            lower = turned[side * width + half : (side + 1) * width, rows]
            item_ref[side, n] = jnp.where(keep, jnp.concatenate([upper, lower], axis=1), 0.0).astype(BF16)


def tiles_kernel(state_hbm, out_ref, state_ref, wide_ref, msg_ref, sems):
    count = out_ref.shape[0]
    tokens = state_ref.shape[0]
    finish(fetch(sems, (state_hbm, state_ref)))
    wide_ref[...] = state_ref[...].astype(F32)
    for d in range(count):
        for i in range(tokens):
            msg_ref[d, i * tokens : (i + 1) * tokens] = wide_ref[i, d * tokens : (d + 1) * tokens, :]
        out_ref[d] = msg_ref[d].astype(BF16)


def mix_kernel(left_ref, right_ref, weight_hbm, y_ref, z_ref, weight_ref, wide_ref, sems):
    factor = left_ref.shape[1]
    half = factor // 2
    seqs = y_ref.shape[1] // factor
    width = weight_ref.shape[1]
    tokens = left_ref.shape[0] // seqs
    finish(fetch(sems, (weight_hbm, weight_ref)))
    wide_ref[...] = weight_ref[...].astype(F32)

    def one(q, carry):
        pairs = (
            [wide_ref[pl.ds(q + t * half, factor, stride=factor), :] for t in (0, 1)],
            [wide_ref[pl.ds(pl.multiple_of((q + t * half) * factor, factor), factor), :] for t in (0, 1)],
        )
        for lhs, pair, out_ref in ((left_ref, pairs[0], y_ref), (right_ref, pairs[1], z_ref)):
            rhs = jnp.concatenate(pair, axis=1).astype(BF16)
            mixed = jnp.dot(lhs[...], rhs, preferred_element_type=F32).astype(BF16)
            for n in range(tokens):
                rows = slice(n * seqs, (n + 1) * seqs)
                cols = slice(n % 2 * width, (n % 2 + 1) * width)
                for t in (0, 1):
                    spot = pl.ds(pl.multiple_of((2 * q + t) * seqs, seqs), seqs)
                    out_ref[n // 2, spot, cols] = mixed[rows, t * width : (t + 1) * width]
        return carry

    lax.fori_loop(0, half, one, 0)


def pair_kernel(
    order, row_ref, depth_ref, chain_ref, depth_row, chain_row, match_ref, bias_ref, state_ref, y_ref, z_ref, *rest
):
    pieces, (next_ref, col_ref, wide_ref, lhs_ref, inv_ref, chain_col) = rest[:-6], rest[-6:]
    step = pl.program_id(0)
    block, total, width = state_ref.shape
    row = row_ref[0]
    own_first = row * (block * pl.num_programs(0)) + step * block
    _, _, tokens, groups, lanes = pieces[0].shape

    @pl.when(step == 0)
    def _():
        size = tokens * groups
        for side in (0, 1):
            for piece, ks in zip(pieces, order):
                for m, k in enumerate(ks):
                    spot = pl.ds(pl.multiple_of((row ^ k) * size, size), size)
                    wide_ref[spot, :] = piece[m, side].astype(F32).reshape(size, lanes)
            for q in range(groups):
                lhs_ref[side, :, q * lanes : (q + 1) * lanes] = wide_ref[
                    pl.ds(q, total, stride=groups), :
                ].astype(BF16)
        same = lax.broadcasted_iota(jnp.int32, (total, total), 0) == lax.broadcasted_iota(
            jnp.int32, (total, total), 1
        )
        ones = jnp.ones((total, width), BF16)

        def column(ref):
            spread = jnp.where(same, ref[...].astype(F32), 0.0).astype(BF16)
            return jnp.dot(spread, ones, preferred_element_type=F32)

        inv_ref[...] = 1.0 / jnp.maximum(column(depth_row), 1.0)
        chain_col[...] = column(chain_row)

    for side, w_ref, out_ref in ((1, y_ref, next_ref), (0, z_ref, col_ref)):
        prod = jnp.dot(lhs_ref[side], w_ref[step], preferred_element_type=F32)
        for t in range(block):
            own = own_first + t
            inv_own = 1.0 / jnp.maximum(jnp.full((1, width), depth_ref[own], jnp.int32).astype(F32), 1.0)
            label = jnp.full((1, width), chain_ref[own], jnp.int32).astype(F32)
            extra = jnp.where(chain_col[...] == label, match_ref[...], 0.0) + bias_ref[...]
            value = prod[:, t * width : (t + 1) * width] * jnp.maximum(inv_ref[...], inv_own) + extra
            if side:
                out_ref[t] = (state_ref[t].astype(F32) + value).astype(BF16)
            else:
                out_ref[t] = value


def gate_kernel(
    col_ref, gain_ref, shift_ref, proj_hbm, gate_hbm, tiles_ref, out_ref, proj_ref, gate_ref, wide_ref, sems
):
    step = pl.program_id(0)
    count, rows, width = tiles_ref.shape
    block, total = col_ref.shape[:2]
    tokens = total // count

    @pl.when(step == 0)
    def _():
        copies = fetch(sems, (proj_hbm, proj_ref), (gate_hbm, gate_ref))
        wide_ref[...] = tiles_ref[...].astype(F32).reshape(count * rows, width)
        finish(copies)

    ones = jnp.full((width, width), 1.0 / width, BF16)
    none = jnp.zeros((width, width), BF16)
    means = jnp.concatenate(
        [jnp.concatenate([ones, none], axis=1), jnp.concatenate([none, ones], axis=1)], axis=0
    )
    for t in range(0, block, 2):
        halves = []
        for u in (0, 1):
            state = wide_ref[pl.ds(step * block + t + u, total, stride=tokens), :]
            halves.append(state + col_ref[t + u])
        pair = jnp.concatenate(halves, axis=1).astype(BF16)
        centre = pair.astype(F32) - jnp.dot(pair, means, preferred_element_type=F32)
        square = (centre * centre).astype(BF16)
        spread = jnp.dot(square, means, preferred_element_type=F32)
        scaled = centre * lax.rsqrt(spread + 1e-05)
        for u in (0, 1):
            normed = scaled[:, u * width : (u + 1) * width] * gain_ref[...] + shift_ref[...]
            normed = normed.astype(BF16)
            projected = jnp.dot(normed, proj_ref[...], preferred_element_type=F32)
            gating = jnp.dot(normed, gate_ref[...], preferred_element_type=F32)
            out_ref[t + u] = (projected * (0.5 + 0.5 * jnp.tanh(0.5 * gating))).astype(BF16)


def fixed(*shape):
    return pl.BlockSpec(shape, lambda g: (0,) * len(shape))


def body(
    pairwise_state,
    homolog_embedding,
    alignment_depth,
    chain_labels,
    homolog_layer_scale,
    homolog_layer_shift,
    outer_source_matrix,
    outer_target_matrix,
    output_weight,
    output_bias,
    chain_match,
    pairwise_norm_gain,
    pairwise_norm_bias,
    input_projection_weight,
    input_gate_weight,
    *,
    count,
):
    tokens, total, width = pairwise_state.shape
    seqs, _, feats = homolog_embedding.shape
    factor = outer_source_matrix.shape[1]
    half = factor // 2
    inner = factor * seqs
    gated = input_projection_weight.shape[1]
    row = lax.axis_index("row").astype(jnp.int32).reshape(1)

    def swap(array, bit):
        return lax.ppermute(array, "row", [(r, r ^ bit) for r in range(count)])

    left, right, item = pl.pallas_call(
        project_kernel,
        out_shape=(
            jax.ShapeDtypeStruct((tokens * seqs, factor), BF16),
            jax.ShapeDtypeStruct((tokens * seqs, factor), BF16),
            jax.ShapeDtypeStruct((2, tokens, half, 2 * seqs), BF16),
        ),
        in_specs=[whole(SMEM)] + [whole(HBM)] * 6,
        out_specs=(whole(VMEM),) * 3,
        scratch_shapes=[
            SMEM((total,), jnp.int32),
            VMEM((tokens, seqs, feats), BF16),
            VMEM((1, feats), F32),
            VMEM((1, feats), F32),
            VMEM((2 * factor, feats), BF16),
            pltpu.SemaphoreType.DMA((6,)),
        ],
        name="project",
    )(
        row,
        alignment_depth,
        homolog_embedding.transpose(1, 0, 2),
        homolog_layer_scale.reshape(1, feats),
        homolog_layer_shift.reshape(1, feats),
        outer_source_matrix.T,
        outer_target_matrix.T,
    )
    held, order = item[None], [0]
    bit = count // 2
    while bit > 1:
        came = swap(held, bit)
        new = [k ^ bit for k in order]
        if bit > 2:
            held, order = jnp.concatenate([held, came], axis=0), order + new
        bit //= 2
    pieces = [held, came, swap(held, 1), swap(came, 1)]
    orders = [order, new, [k ^ 1 for k in order], [k ^ 1 for k in new]]

    tiles = pl.pallas_call(
        tiles_kernel,
        out_shape=jax.ShapeDtypeStruct((count, tokens * tokens, width), BF16),
        in_specs=[whole(HBM)],
        out_specs=whole(VMEM),
        scratch_shapes=[
            VMEM((tokens, total, width), BF16),
            VMEM((tokens, total, width), F32),
            VMEM((count, tokens * tokens, width), F32),
            pltpu.SemaphoreType.DMA((1,)),
        ],
        name="tiles",
    )(pairwise_state)
    tiles = lax.all_to_all(tiles, "row", split_axis=0, concat_axis=0, tiled=True)

    y, z = pl.pallas_call(
        mix_kernel,
        out_shape=(jax.ShapeDtypeStruct((tokens // 2, inner, 2 * width), BF16),) * 2,
        in_specs=[whole(VMEM), whole(VMEM), whole(HBM)],
        out_specs=(whole(VMEM),) * 2,
        scratch_shapes=[
            VMEM((factor * factor, width), BF16),
            VMEM((factor * factor, width), F32),
            pltpu.SemaphoreType.DMA((1,)),
        ],
        compiler_params=params(16),
        cost_estimate=pl.CostEstimate(
            flops=4 * tokens * seqs * factor * factor * width,
            bytes_accessed=4 * inner * tokens * width,
            transcendentals=0,
        ),
        name="mix",
    )(left, right, output_weight)

    block = 2
    pair_next, columns = pl.pallas_call(
        functools.partial(pair_kernel, orders),
        grid=(tokens // block,),
        out_shape=(
            jax.ShapeDtypeStruct((tokens, total, width), BF16),
            jax.ShapeDtypeStruct((tokens, total, width), F32),
        ),
        in_specs=[whole(SMEM)] * 3
        + [
            fixed(1, total),
            fixed(1, total),
            fixed(1, width),
            fixed(1, width),
            pl.BlockSpec((block, total, width), lambda g: (g, 0, 0)),
        ]
        + [whole(VMEM)] * 6,
        out_specs=(pl.BlockSpec((block, total, width), lambda g: (g, 0, 0)),) * 2,
        scratch_shapes=[
            VMEM((total * half, 2 * seqs), F32),
            VMEM((2, total, inner), BF16),
            VMEM((total, width), F32),
            VMEM((total, width), F32),
        ],
        compiler_params=params(40),
        cost_estimate=pl.CostEstimate(
            flops=4 * total * inner * tokens * width,
            bytes_accessed=4 * inner * tokens * width + 8 * tokens * total * width,
            transcendentals=0,
        ),
        name="pair",
    )(
        row,
        alignment_depth,
        chain_labels,
        alignment_depth.reshape(1, total),
        chain_labels.reshape(1, total),
        chain_match.reshape(1, width),
        output_bias.reshape(1, width),
        pairwise_state,
        y,
        z,
        *pieces,
    )

    block = 4
    out = pl.pallas_call(
        gate_kernel,
        grid=(tokens // block,),
        out_shape=jax.ShapeDtypeStruct((tokens, total, gated), BF16),
        in_specs=[
            pl.BlockSpec((block, total, width), lambda j: (j, 0, 0)),
            fixed(1, width),
            fixed(1, width),
            whole(HBM),
            whole(HBM),
            fixed(count, tokens * tokens, width),
        ],
        out_specs=pl.BlockSpec((block, total, gated), lambda j: (j, 0, 0)),
        scratch_shapes=[
            VMEM((width, gated), BF16),
            VMEM((width, gated), BF16),
            VMEM((count * tokens * tokens, width), F32),
            pltpu.SemaphoreType.DMA((2,)),
        ],
        cost_estimate=pl.CostEstimate(
            flops=4 * tokens * total * width * gated,
            bytes_accessed=tokens * total * (2 * gated + 6 * width),
            transcendentals=tokens * total * gated,
        ),
        name="gate",
    )(
        columns,
        pairwise_norm_gain.reshape(1, width),
        pairwise_norm_bias.reshape(1, width),
        input_projection_weight,
        input_gate_weight,
        tiles,
    )
    return pair_next, out.transpose(1, 0, 2)


def solution(mesh):
    return jax.shard_map(
        functools.partial(body, count=mesh.shape["row"]),
        mesh=mesh,
        in_specs=(
            P(("groups", "row"), None, None),
            P(None, ("groups", "row"), None),
            P("groups"),
            P("groups"),
        )
        + (P(),) * 11,
        out_specs=(P(("groups", "row"), None, None), P("groups", "row", None)),
        check_vma=False,
    )
```

```python
import functools

import jax
import jax.numpy as jnp
from jax import lax
from jax.experimental import pallas as pl
from jax.experimental.pallas import tpu as pltpu
from jax.sharding import PartitionSpec as P

F32 = jnp.float32
BF16 = jnp.bfloat16
NT = (((1,), (1,)), ((), ()))
VMEM = pltpu.VMEM
SMEM = pltpu.SMEM
HBM = pltpu.HBM
LANES = 128


def whole(space):
    return pl.BlockSpec(memory_space=space)


def params(mib):
    return pltpu.CompilerParams(vmem_limit_bytes=mib * 1024 * 1024)


def fetch(sems, *pairs):
    copies = [pltpu.make_async_copy(a, b, sems.at[n]) for n, (a, b) in enumerate(pairs)]
    for copy in copies:
        copy.start()
    return copies


def finish(copies):
    for copy in copies:
        copy.wait()


def prepare_kernel(
    row_ref, depth_hbm, hom_hbm, scale_hbm, shift_hbm, src_hbm, tgt_hbm, state_hbm, depth_row_hbm, chain_hbm, chain_row_hbm,
    match_hbm, bias_hbm, gain_hbm, move_hbm, proj_hbm, gate_hbm,
    left_ref, right_ref, item_ref, tiles_ref, aux_ref, gates_ref,
    depth_ref, hom_ref, scale_ref, shift_ref, both_ref, state_ref, depth_row_ref, chain_ref, chain_row_ref, vec_ref,
    wide_ref, msg_ref, sems,
):
    tokens, seqs, feats = hom_ref.shape
    count, _, pair_width = tiles_ref.shape
    total = depth_ref.shape[0]
    width = src_hbm.shape[0]
    half = width // 2
    gated = proj_hbm.shape[1]
    first_copies = fetch(
        sems,
        (hom_hbm, hom_ref),
        (depth_hbm, depth_ref),
        (scale_hbm, scale_ref),
        (shift_hbm, shift_ref),
        (src_hbm, both_ref.at[0:width]),
        (tgt_hbm, both_ref.at[width : 2 * width]),
        (state_hbm, state_ref),
        (chain_hbm, chain_ref),
        (depth_row_hbm, depth_row_ref),
        (chain_row_hbm, chain_row_ref),
        (match_hbm, vec_ref.at[0]),
        (bias_hbm, vec_ref.at[1]),
        (gain_hbm, vec_ref.at[2]),
        (move_hbm, vec_ref.at[3]),
        (proj_hbm, gates_ref.at[0]),
        (gate_hbm, gates_ref.at[1]),
    )
    finish(first_copies[:6])
    values = hom_ref[...].reshape(tokens * seqs, feats)
    ones = jnp.full((feats, feats), 1.0 / feats, BF16)
    centre = values.astype(F32) - jnp.dot(values, ones, preferred_element_type=F32)
    square = centre * centre
    high = square.astype(BF16)
    low = (square - high.astype(F32)).astype(BF16)
    spread = jnp.dot(high, ones, preferred_element_type=F32) + jnp.dot(
        low, ones, preferred_element_type=F32
    )
    normed = (centre * lax.rsqrt(spread + 1e-05) * scale_ref[...] + shift_ref[...]).astype(BF16)
    both = both_ref[...]
    turned = lax.dot_general(both, normed, NT, preferred_element_type=F32)
    plain = lax.dot_general(normed, both, NT, preferred_element_type=F32)
    first = row_ref[0] * tokens
    row_pos = lax.broadcasted_iota(jnp.int32, (seqs, width), 0)
    lane = lax.broadcasted_iota(jnp.int32, (half, 2 * seqs), 1)
    front = lane < seqs
    seq_pos = jnp.where(front, lane, lane - seqs)
    for n in range(tokens):
        depth = depth_ref[first + n]
        rows = slice(n * seqs, (n + 1) * seqs)
        left_ref[rows] = jnp.where(row_pos < depth, plain[rows, 0:width], 0.0).astype(BF16)
        right_ref[rows] = jnp.where(row_pos < depth, plain[rows, width : 2 * width], 0.0).astype(BF16)
        keep = seq_pos < depth
        for side in (0, 1):
            upper = turned[side * width : side * width + half, rows]
            lower = turned[side * width + half : (side + 1) * width, rows]
            item_ref[side, n] = jnp.where(keep, jnp.concatenate([upper, lower], axis=1), 0.0).astype(BF16)

    finish(first_copies[6:])
    wide_ref[...] = state_ref[...].astype(F32)
    for d in range(count):
        for i in range(tokens):
            msg_ref[d, i * tokens : (i + 1) * tokens] = wide_ref[i, d * tokens : (d + 1) * tokens, :]
        tiles_ref[d] = msg_ref[d].astype(BF16)

    same = lax.broadcasted_iota(jnp.int32, (total, total), 0) == lax.broadcasted_iota(
        jnp.int32, (total, total), 1
    )
    fill = jnp.ones((total, pair_width), BF16)

    def column(ref):
        diagonal = jnp.where(same, ref[...].astype(F32), 0.0).astype(BF16)
        return jnp.dot(diagonal, fill, preferred_element_type=F32)

    aux_ref[0:total] = 1.0 / jnp.maximum(column(depth_row_ref), 1.0)
    aux_ref[total : 2 * total] = column(chain_row_ref)
    for n in range(tokens):
        own = jnp.full((1, pair_width), depth_ref[first + n], jnp.int32).astype(F32)
        aux_ref[2 * total + n : 2 * total + n + 1] = 1.0 / jnp.maximum(own, 1.0)
        label = jnp.full((1, pair_width), chain_ref[first + n], jnp.int32).astype(F32)
        aux_ref[2 * total + 16 + n : 2 * total + 17 + n] = label
    for n in range(4):
        aux_ref[2 * total + 32 + n : 2 * total + 33 + n] = vec_ref[n]


def mix_kernel(left_ref, right_ref, weight_hbm, y_ref, z_ref, weight_ref, wide_ref, sems):
    factor = left_ref.shape[1]
    half = factor // 2
    seqs = y_ref.shape[1] // factor
    width = weight_ref.shape[1]
    tokens = left_ref.shape[0] // seqs
    finish(fetch(sems, (weight_hbm, weight_ref)))
    wide_ref[...] = weight_ref[...].astype(F32)

    def one(q, carry):
        pairs = (
            [wide_ref[pl.ds(q + t * half, factor, stride=factor), :] for t in (0, 1)],
            [wide_ref[pl.ds(pl.multiple_of((q + t * half) * factor, factor), factor), :] for t in (0, 1)],
        )
        for lhs, pair, out_ref in ((left_ref, pairs[0], y_ref), (right_ref, pairs[1], z_ref)):
            rhs = jnp.concatenate(pair, axis=1).astype(BF16)
            mixed = jnp.dot(lhs[...], rhs, preferred_element_type=F32).astype(BF16)
            for n in range(tokens):
                rows = slice(n * seqs, (n + 1) * seqs)
                cols = slice(n % 2 * width, (n % 2 + 1) * width)
                for t in (0, 1):
                    spot = pl.ds(pl.multiple_of((2 * q + t) * seqs, seqs), seqs)
                    out_ref[n // 2, spot, cols] = mixed[rows, t * width : (t + 1) * width]
        return carry

    lax.fori_loop(0, half, one, 0)


def pair_kernel(order, row_ref, aux_ref, state_ref, y_ref, z_ref, *rest):
    pieces, (next_ref, col_ref, wide_ref, lhs_ref) = rest[:-4], rest[-4:]
    step = pl.program_id(0)
    block, total, width = state_ref.shape
    row = row_ref[0]
    _, _, tokens, groups, lanes = pieces[0].shape

    @pl.when(step == 0)
    def _():
        size = tokens * groups
        for side in (0, 1):
            for piece, ks in zip(pieces, order):
                for m, k in enumerate(ks):
                    spot = pl.ds(pl.multiple_of((row ^ k) * size, size), size)
                    wide_ref[spot, :] = piece[m, side].astype(F32).reshape(size, lanes)
            for q in range(groups):
                lhs_ref[side, :, q * lanes : (q + 1) * lanes] = wide_ref[
                    pl.ds(q, total, stride=groups), :
                ].astype(BF16)

    base = 2 * total
    match = aux_ref[base + 32 : base + 33]
    bias = aux_ref[base + 33 : base + 34]
    for side, w_ref, out_ref in ((1, y_ref, next_ref), (0, z_ref, col_ref)):
        prod = jnp.dot(lhs_ref[side], w_ref[step], preferred_element_type=F32)
        for t in range(block):
            own = step * block + t
            inv_own = aux_ref[pl.ds(base + own, 1)]
            label = aux_ref[pl.ds(base + 16 + own, 1)]
            extra = jnp.where(aux_ref[total:base] == label, match, 0.0) + bias
            value = prod[:, t * width : (t + 1) * width] * jnp.maximum(aux_ref[0:total], inv_own) + extra
            if side:
                out_ref[t] = (state_ref[t].astype(F32) + value).astype(BF16)
            else:
                out_ref[t] = value


def gate_kernel(aux_ref, col_ref, gates_ref, tiles_ref, out_ref, wide_ref):
    step = pl.program_id(0)
    count, rows, width = tiles_ref.shape
    block, total = col_ref.shape[:2]
    tokens = total // count

    @pl.when(step == 0)
    def _():
        wide_ref[...] = tiles_ref[...].astype(F32).reshape(count * rows, width)

    gain = aux_ref[2 * total + 34 : 2 * total + 35]
    shift = aux_ref[2 * total + 35 : 2 * total + 36]
    ones = jnp.full((width, width), 1.0 / width, BF16)
    none = jnp.zeros((width, width), BF16)
    means = jnp.concatenate(
        [jnp.concatenate([ones, none], axis=1), jnp.concatenate([none, ones], axis=1)], axis=0
    )
    for t in range(0, block, 2):
        halves = []
        for u in (0, 1):
            state = wide_ref[pl.ds(step * block + t + u, total, stride=tokens), :]
            halves.append(state + col_ref[t + u])
        pair = jnp.concatenate(halves, axis=1).astype(BF16)
        centre = pair.astype(F32) - jnp.dot(pair, means, preferred_element_type=F32)
        square = (centre * centre).astype(BF16)
        spread = jnp.dot(square, means, preferred_element_type=F32)
        scaled = centre * lax.rsqrt(spread + 1e-05)
        for u in (0, 1):
            normed = scaled[:, u * width : (u + 1) * width] * gain + shift
            normed = normed.astype(BF16)
            projected = jnp.dot(normed, gates_ref[0], preferred_element_type=F32)
            gating = jnp.dot(normed, gates_ref[1], preferred_element_type=F32)
            out_ref[t + u] = (projected * (0.5 + 0.5 * jnp.tanh(0.5 * gating))).astype(BF16)


def fixed(*shape):
    return pl.BlockSpec(shape, lambda g: (0,) * len(shape))


def body(
    pairwise_state,
    homolog_embedding,
    alignment_depth,
    chain_labels,
    homolog_layer_scale,
    homolog_layer_shift,
    outer_source_matrix,
    outer_target_matrix,
    output_weight,
    output_bias,
    chain_match,
    pairwise_norm_gain,
    pairwise_norm_bias,
    input_projection_weight,
    input_gate_weight,
    *,
    count,
):
    tokens, total, width = pairwise_state.shape
    seqs, _, feats = homolog_embedding.shape
    factor = outer_source_matrix.shape[1]
    half = factor // 2
    inner = factor * seqs
    gated = input_projection_weight.shape[1]
    row = lax.axis_index("row").astype(jnp.int32).reshape(1)

    def swap(array, bit):
        return lax.ppermute(array, "row", [(r, r ^ bit) for r in range(count)])

    aux_rows = 2 * total + 40
    left, right, item, tiles, aux, gates = pl.pallas_call(
        prepare_kernel,
        out_shape=(
            jax.ShapeDtypeStruct((tokens * seqs, factor), BF16),
            jax.ShapeDtypeStruct((tokens * seqs, factor), BF16),
            jax.ShapeDtypeStruct((2, tokens, half, 2 * seqs), BF16),
            jax.ShapeDtypeStruct((count, tokens * tokens, width), BF16),
            jax.ShapeDtypeStruct((aux_rows, width), F32),
            jax.ShapeDtypeStruct((2, width, gated), BF16),
        ),
        in_specs=[whole(SMEM)] + [whole(HBM)] * 16,
        out_specs=(whole(VMEM),) * 6,
        scratch_shapes=[
            SMEM((total,), jnp.int32),
            VMEM((tokens, seqs, feats), BF16),
            VMEM((1, feats), F32),
            VMEM((1, feats), F32),
            VMEM((2 * factor, feats), BF16),
            VMEM((tokens, total, width), BF16),
            VMEM((1, total), jnp.int32),
            SMEM((total,), jnp.int32),
            VMEM((1, total), jnp.int32),
            VMEM((4, 1, width), F32),
            VMEM((tokens, total, width), F32),
            VMEM((count, tokens * tokens, width), F32),
            pltpu.SemaphoreType.DMA((16,)),
        ],
        name="prepare",
    )(
        row,
        alignment_depth,
        homolog_embedding.transpose(1, 0, 2),
        homolog_layer_scale.reshape(1, feats),
        homolog_layer_shift.reshape(1, feats),
        outer_source_matrix.T,
        outer_target_matrix.T,
        pairwise_state,
        alignment_depth.reshape(1, total),
        chain_labels,
        chain_labels.reshape(1, total),
        chain_match.reshape(1, width),
        output_bias.reshape(1, width),
        pairwise_norm_gain.reshape(1, width),
        pairwise_norm_bias.reshape(1, width),
        input_projection_weight,
        input_gate_weight,
    )

    y, z = pl.pallas_call(
        mix_kernel,
        out_shape=(jax.ShapeDtypeStruct((tokens // 2, inner, 2 * width), BF16),) * 2,
        in_specs=[whole(VMEM), whole(VMEM), whole(HBM)],
        out_specs=(whole(VMEM),) * 2,
        scratch_shapes=[
            VMEM((factor * factor, width), BF16),
            VMEM((factor * factor, width), F32),
            pltpu.SemaphoreType.DMA((1,)),
        ],
        compiler_params=params(16),
        cost_estimate=pl.CostEstimate(
            flops=4 * tokens * seqs * factor * factor * width,
            bytes_accessed=4 * inner * tokens * width,
            transcendentals=0,
        ),
        name="mix",
    )(left, right, output_weight)

    held, order = item[None], [0]
    bit = count // 2
    while bit > 1:
        came = swap(held, bit)
        new = [k ^ bit for k in order]
        if bit == 4:
            came, y, z = lax.optimization_barrier((came, y, z))
        if bit > 2:
            held, order = jnp.concatenate([held, came], axis=0), order + new
        bit //= 2
    pieces = [held, came, swap(held, 1), swap(came, 1)]
    orders = [order, new, [k ^ 1 for k in order], [k ^ 1 for k in new]]

    tiles = lax.all_to_all(tiles, "row", split_axis=0, concat_axis=0, tiled=True)

    block = 2
    pair_next, columns = pl.pallas_call(
        functools.partial(pair_kernel, orders),
        grid=(tokens // block,),
        out_shape=(
            jax.ShapeDtypeStruct((tokens, total, width), BF16),
            jax.ShapeDtypeStruct((tokens, total, width), F32),
        ),
        in_specs=[whole(SMEM), whole(VMEM), pl.BlockSpec((block, total, width), lambda g: (g, 0, 0))]
        + [whole(VMEM)] * 6,
        out_specs=(pl.BlockSpec((block, total, width), lambda g: (g, 0, 0)),) * 2,
        scratch_shapes=[
            VMEM((total * half, 2 * seqs), F32),
            VMEM((2, total, inner), BF16),
        ],
        compiler_params=params(24),
        cost_estimate=pl.CostEstimate(
            flops=4 * total * inner * tokens * width,
            bytes_accessed=4 * inner * tokens * width + 8 * tokens * total * width,
            transcendentals=0,
        ),
        name="pair",
    )(row, aux, pairwise_state, y, z, *pieces)

    block = 4
    out = pl.pallas_call(
        gate_kernel,
        grid=(tokens // block,),
        out_shape=jax.ShapeDtypeStruct((tokens, total, gated), BF16),
        in_specs=[
            whole(VMEM),
            pl.BlockSpec((block, total, width), lambda j: (j, 0, 0)),
            whole(VMEM),
            whole(VMEM),
        ],
        out_specs=pl.BlockSpec((block, total, gated), lambda j: (j, 0, 0)),
        scratch_shapes=[VMEM((count * tokens * tokens, width), F32)],
        compiler_params=params(24),
        cost_estimate=pl.CostEstimate(
            flops=4 * tokens * total * width * gated,
            bytes_accessed=tokens * total * (2 * gated + 6 * width),
            transcendentals=tokens * total * gated,
        ),
        name="gate",
    )(aux, columns, gates, tiles)
    return pair_next, out.transpose(1, 0, 2)


def solution(mesh):
    return jax.shard_map(
        functools.partial(body, count=mesh.shape["row"]),
        mesh=mesh,
        in_specs=(
            P(("groups", "row"), None, None),
            P(None, ("groups", "row"), None),
            P("groups"),
            P("groups"),
        )
        + (P(),) * 11,
        out_specs=(P(("groups", "row"), None, None), P("groups", "row", None)),
        check_vma=False,
    )
```

```python
import functools

import jax
import jax.numpy as jnp
from jax import lax
from jax.experimental import pallas as pl
from jax.experimental.pallas import tpu as pltpu
from jax.sharding import PartitionSpec as P

F32 = jnp.float32
BF16 = jnp.bfloat16
NT = (((1,), (1,)), ((), ()))
VMEM = pltpu.VMEM
SMEM = pltpu.SMEM
HBM = pltpu.HBM
LANES = 128


def whole(space):
    return pl.BlockSpec(memory_space=space)


def params(mib):
    return pltpu.CompilerParams(vmem_limit_bytes=mib * 1024 * 1024)


def fetch(sems, *pairs):
    copies = [pltpu.make_async_copy(a, b, sems.at[n]) for n, (a, b) in enumerate(pairs)]
    for copy in copies:
        copy.start()
    return copies


def finish(copies):
    for copy in copies:
        copy.wait()


def prepare_kernel(
    row_ref, depth_hbm, hom_hbm, scale_hbm, shift_hbm, src_hbm, tgt_hbm, state_hbm, depth_row_hbm, chain_hbm, chain_row_hbm,
    match_hbm, bias_hbm, gain_hbm, move_hbm, proj_hbm, gate_hbm,
    left_ref, right_ref, item_left, item_right, tiles_ref, aux_ref, gates_ref,
    depth_ref, hom_ref, scale_ref, shift_ref, both_ref, state_ref, depth_row_ref, chain_ref, chain_row_ref, vec_ref,
    wide_ref, msg_ref, sems,
):
    tokens, seqs, feats = hom_ref.shape
    count, _, pair_width = tiles_ref.shape
    total = depth_ref.shape[0]
    width = src_hbm.shape[0]
    half = width // 2
    gated = proj_hbm.shape[1]
    first_copies = fetch(
        sems,
        (hom_hbm, hom_ref),
        (depth_hbm, depth_ref),
        (scale_hbm, scale_ref),
        (shift_hbm, shift_ref),
        (src_hbm, both_ref.at[0:width]),
        (tgt_hbm, both_ref.at[width : 2 * width]),
        (state_hbm, state_ref),
        (chain_hbm, chain_ref),
        (depth_row_hbm, depth_row_ref),
        (chain_row_hbm, chain_row_ref),
        (match_hbm, vec_ref.at[0]),
        (bias_hbm, vec_ref.at[1]),
        (gain_hbm, vec_ref.at[2]),
        (move_hbm, vec_ref.at[3]),
        (proj_hbm, gates_ref.at[0]),
        (gate_hbm, gates_ref.at[1]),
    )
    finish(first_copies[:6])
    values = hom_ref[...].reshape(tokens * seqs, feats)
    ones = jnp.full((feats, feats), 1.0 / feats, BF16)
    centre = values.astype(F32) - jnp.dot(values, ones, preferred_element_type=F32)
    square = centre * centre
    high = square.astype(BF16)
    low = (square - high.astype(F32)).astype(BF16)
    spread = jnp.dot(high, ones, preferred_element_type=F32) + jnp.dot(
        low, ones, preferred_element_type=F32
    )
    normed = (centre * lax.rsqrt(spread + 1e-05) * scale_ref[...] + shift_ref[...]).astype(BF16)
    both = both_ref[...]
    turned = lax.dot_general(both, normed, NT, preferred_element_type=F32)
    plain = lax.dot_general(normed, both, NT, preferred_element_type=F32)
    first = row_ref[0] * tokens
    row_pos = lax.broadcasted_iota(jnp.int32, (seqs, width), 0)
    lane = lax.broadcasted_iota(jnp.int32, (half, 2 * seqs), 1)
    front = lane < seqs
    seq_pos = jnp.where(front, lane, lane - seqs)
    for n in range(tokens):
        depth = depth_ref[first + n]
        rows = slice(n * seqs, (n + 1) * seqs)
        left_ref[rows] = jnp.where(row_pos < depth, plain[rows, 0:width], 0.0).astype(BF16)
        right_ref[rows] = jnp.where(row_pos < depth, plain[rows, width : 2 * width], 0.0).astype(BF16)
        keep = seq_pos < depth
        for side, item_ref in ((0, item_left), (1, item_right)):
            upper = turned[side * width : side * width + half, rows]
            lower = turned[side * width + half : (side + 1) * width, rows]
            item_ref[0, n] = jnp.where(keep, jnp.concatenate([upper, lower], axis=1), 0.0).astype(BF16)

    finish(first_copies[6:])
    wide_ref[...] = state_ref[...].astype(F32)
    for d in range(count):
        for i in range(tokens):
            msg_ref[d, i * tokens : (i + 1) * tokens] = wide_ref[i, d * tokens : (d + 1) * tokens, :]
        tiles_ref[d] = msg_ref[d].astype(BF16)

    same = lax.broadcasted_iota(jnp.int32, (total, total), 0) == lax.broadcasted_iota(
        jnp.int32, (total, total), 1
    )
    fill = jnp.ones((total, pair_width), BF16)

    def column(ref):
        diagonal = jnp.where(same, ref[...].astype(F32), 0.0).astype(BF16)
        return jnp.dot(diagonal, fill, preferred_element_type=F32)

    aux_ref[0:total] = 1.0 / jnp.maximum(column(depth_row_ref), 1.0)
    aux_ref[total : 2 * total] = column(chain_row_ref)
    for n in range(tokens):
        own = jnp.full((1, pair_width), depth_ref[first + n], jnp.int32).astype(F32)
        aux_ref[2 * total + n : 2 * total + n + 1] = 1.0 / jnp.maximum(own, 1.0)
        label = jnp.full((1, pair_width), chain_ref[first + n], jnp.int32).astype(F32)
        aux_ref[2 * total + 16 + n : 2 * total + 17 + n] = label
    for n in range(4):
        aux_ref[2 * total + 32 + n : 2 * total + 33 + n] = vec_ref[n]


def mix_kernel(strided, lhs_ref, weight_ref, out_ref, wide_ref):
    factor = lhs_ref.shape[1]
    half = factor // 2
    seqs = out_ref.shape[1] // factor
    width = weight_ref.shape[1]
    tokens = lhs_ref.shape[0] // seqs
    wide_ref[...] = weight_ref[...].astype(F32)

    def one(q, carry):
        if strided:
            pair = [wide_ref[pl.ds(q + t * half, factor, stride=factor), :] for t in (0, 1)]
        else:
            pair = [
                wide_ref[pl.ds(pl.multiple_of((q + t * half) * factor, factor), factor), :] for t in (0, 1)
            ]
        rhs = jnp.concatenate(pair, axis=1).astype(BF16)
        mixed = jnp.dot(lhs_ref[...], rhs, preferred_element_type=F32).astype(BF16)
        for n in range(tokens):
            rows = slice(n * seqs, (n + 1) * seqs)
            cols = slice(n % 2 * width, (n % 2 + 1) * width)
            for t in (0, 1):
                spot = pl.ds(pl.multiple_of((2 * q + t) * seqs, seqs), seqs)
                out_ref[n // 2, spot, cols] = mixed[rows, t * width : (t + 1) * width]
        return carry

    lax.fori_loop(0, half, one, 0)


def join_kernel(*refs):
    per = (len(refs) - 2) // 2
    for side in (0, 1):
        spot = 0
        for piece in refs[side * per : (side + 1) * per]:
            refs[2 * per + side][spot : spot + piece.shape[0]] = piece[...]
            spot += piece.shape[0]


def spread_items(row, wide_ref, sides):
    for side, pieces in enumerate(sides):
        for piece, ks in pieces:
            _, tokens, groups, lanes = piece.shape
            size = tokens * groups
            for m, k in enumerate(ks):
                spot = pl.ds(pl.multiple_of((row ^ k) * size, size), size)
                wide_ref[side, spot, :] = piece[m].astype(F32).reshape(size, lanes)


def first_half_kernel(orders, row_ref, state_ref, aux_ref, *rest):
    pieces, (wide_ref, state_out, aux_out) = rest[:-3], rest[-3:]
    per = len(pieces) // 2
    state_out[...] = state_ref[...]
    aux_out[...] = aux_ref[...]
    spread_items(
        row_ref[0], wide_ref, [list(zip(pieces[s * per : (s + 1) * per], orders[s])) for s in (0, 1)]
    )


def pair_kernel(orders, row_ref, aux_ref, state_ref, y_ref, z_ref, wide_in, *rest):
    pieces, (next_ref, col_ref, wide_ref, lhs_ref) = rest[:-4], rest[-4:]
    step = pl.program_id(0)
    block, total, width = state_ref.shape
    _, tokens, groups, lanes = pieces[0].shape
    per = len(pieces) // 2

    @pl.when(step == 0)
    def _():
        spread_items(
            row_ref[0], wide_ref, [list(zip(pieces[s * per : (s + 1) * per], orders[s])) for s in (0, 1)]
        )

        def one(q, carry):
            cols = pl.ds(pl.multiple_of(q * lanes, lanes), lanes)
            for side in (0, 1):
                lhs_ref[side, :, cols] = wide_ref[side, pl.ds(q, total, stride=groups), :].astype(BF16)
            return carry

        lax.fori_loop(0, groups, one, 0, unroll=2)

    base = 2 * total
    match = aux_ref[base + 32 : base + 33]
    bias = aux_ref[base + 33 : base + 34]
    for side, w_ref, out_ref in ((1, y_ref, next_ref), (0, z_ref, col_ref)):
        prod = jnp.dot(lhs_ref[side], w_ref[step], preferred_element_type=F32)
        for t in range(block):
            own = step * block + t
            inv_own = aux_ref[pl.ds(base + own, 1)]
            label = aux_ref[pl.ds(base + 16 + own, 1)]
            extra = jnp.where(aux_ref[total:base] == label, match, 0.0) + bias
            value = prod[:, t * width : (t + 1) * width] * jnp.maximum(aux_ref[0:total], inv_own) + extra
            if side:
                out_ref[t] = (state_ref[t].astype(F32) + value).astype(BF16)
            else:
                out_ref[t] = value


def gate_kernel(aux_ref, col_ref, gates_ref, tiles_ref, out_ref, wide_ref):
    step = pl.program_id(0)
    count, rows, width = tiles_ref.shape
    block, total = col_ref.shape[:2]
    tokens = total // count

    @pl.when(step == 0)
    def _():
        wide_ref[...] = tiles_ref[...].astype(F32).reshape(count * rows, width)

    gain = aux_ref[2 * total + 34 : 2 * total + 35]
    shift = aux_ref[2 * total + 35 : 2 * total + 36]
    ones = jnp.full((width, width), 1.0 / width, BF16)
    none = jnp.zeros((width, width), BF16)
    means = jnp.concatenate(
        [jnp.concatenate([ones, none], axis=1), jnp.concatenate([none, ones], axis=1)], axis=0
    )
    for t in range(0, block, 2):
        halves = []
        for u in (0, 1):
            state = wide_ref[pl.ds(step * block + t + u, total, stride=tokens), :]
            halves.append(state + col_ref[t + u])
        pair = jnp.concatenate(halves, axis=1).astype(BF16)
        centre = pair.astype(F32) - jnp.dot(pair, means, preferred_element_type=F32)
        square = (centre * centre).astype(BF16)
        spread = jnp.dot(square, means, preferred_element_type=F32)
        scaled = centre * lax.rsqrt(spread + 1e-05)
        for u in (0, 1):
            normed = scaled[:, u * width : (u + 1) * width] * gain + shift
            normed = normed.astype(BF16)
            projected = jnp.dot(normed, gates_ref[0], preferred_element_type=F32)
            gating = jnp.dot(normed, gates_ref[1], preferred_element_type=F32)
            out_ref[t + u] = (projected * (0.5 + 0.5 * jnp.tanh(0.5 * gating))).astype(BF16)


def fixed(*shape):
    return pl.BlockSpec(shape, lambda g: (0,) * len(shape))


def body(
    pairwise_state,
    homolog_embedding,
    alignment_depth,
    chain_labels,
    homolog_layer_scale,
    homolog_layer_shift,
    outer_source_matrix,
    outer_target_matrix,
    output_weight,
    output_bias,
    chain_match,
    pairwise_norm_gain,
    pairwise_norm_bias,
    input_projection_weight,
    input_gate_weight,
    *,
    count,
):
    tokens, total, width = pairwise_state.shape
    seqs, _, feats = homolog_embedding.shape
    factor = outer_source_matrix.shape[1]
    half = factor // 2
    inner = factor * seqs
    gated = input_projection_weight.shape[1]
    row = lax.axis_index("row").astype(jnp.int32).reshape(1)

    def swap(array, bit):
        return lax.ppermute(array, "row", [(r, r ^ bit) for r in range(count)])

    aux_rows = 2 * total + 40
    left, right, item_left, item_right, tiles, aux, gates = pl.pallas_call(
        prepare_kernel,
        out_shape=(
            jax.ShapeDtypeStruct((tokens * seqs, factor), BF16),
            jax.ShapeDtypeStruct((tokens * seqs, factor), BF16),
            jax.ShapeDtypeStruct((1, tokens, half, 2 * seqs), BF16),
            jax.ShapeDtypeStruct((1, tokens, half, 2 * seqs), BF16),
            jax.ShapeDtypeStruct((count, tokens * tokens, width), BF16),
            jax.ShapeDtypeStruct((aux_rows, width), F32),
            jax.ShapeDtypeStruct((2, width, gated), BF16),
        ),
        in_specs=[whole(SMEM)] + [whole(HBM)] * 16,
        out_specs=(whole(VMEM),) * 7,
        scratch_shapes=[
            SMEM((total,), jnp.int32),
            VMEM((tokens, seqs, feats), BF16),
            VMEM((1, feats), F32),
            VMEM((1, feats), F32),
            VMEM((2 * factor, feats), BF16),
            VMEM((tokens, total, width), BF16),
            VMEM((1, total), jnp.int32),
            SMEM((total,), jnp.int32),
            VMEM((1, total), jnp.int32),
            VMEM((4, 1, width), F32),
            VMEM((tokens, total, width), F32),
            VMEM((count, tokens * tokens, width), F32),
            pltpu.SemaphoreType.DMA((16,)),
        ],
        name="prepare",
    )(
        row,
        alignment_depth,
        homolog_embedding.transpose(1, 0, 2),
        homolog_layer_scale.reshape(1, feats),
        homolog_layer_shift.reshape(1, feats),
        outer_source_matrix.T,
        outer_target_matrix.T,
        pairwise_state,
        alignment_depth.reshape(1, total),
        chain_labels,
        chain_labels.reshape(1, total),
        chain_match.reshape(1, width),
        output_bias.reshape(1, width),
        pairwise_norm_gain.reshape(1, width),
        pairwise_norm_bias.reshape(1, width),
        input_projection_weight,
        input_gate_weight,
    )

    def mixed(lhs, strided):
        return pl.pallas_call(
            functools.partial(mix_kernel, strided),
            out_shape=jax.ShapeDtypeStruct((tokens // 2, inner, 2 * width), BF16),
            in_specs=[whole(VMEM), whole(VMEM)],
            out_specs=whole(VMEM),
            scratch_shapes=[VMEM((factor * factor, width), F32)],
            compiler_params=params(16),
            cost_estimate=pl.CostEstimate(
                flops=2 * tokens * seqs * factor * factor * width,
                bytes_accessed=2 * inner * tokens * width,
                transcendentals=0,
            ),
            name="mix",
        )(lhs, output_weight)

    def joined(lefts, rights):
        shape = (sum(x.shape[0] for x in lefts), tokens, half, 2 * seqs)
        return pl.pallas_call(
            join_kernel,
            out_shape=(jax.ShapeDtypeStruct(shape, BF16),) * 2,
            in_specs=[whole(VMEM)] * (2 * len(lefts)),
            out_specs=(whole(VMEM),) * 2,
            compiler_params=params(16),
            name="join",
        )(*lefts, *rights)

    bits = [1 << n for n in range(1, count.bit_length() - 1)][::-1]
    turns = [bits, bits[-1:] + bits[:-1]]
    own = [item_left, item_right]
    far = [swap(x, t[0]) for x, t in zip(own, turns)]
    near = [swap(x, t[1]) for x, t in zip(own, turns)]
    both = [swap(x, t[1]) for x, t in zip(far, turns)]
    y = mixed(left, True)
    *both, y = lax.optimization_barrier((*both, y))
    held = joined(*[[own[s], far[s], near[s], both[s]] for s in (0, 1)])
    ranks = [[0, t[0], t[1], t[0] ^ t[1]] for t in turns]
    for n in range(2, len(bits)):
        came = [swap(x, t[n]) for x, t in zip(held, turns)]
        new = [[k ^ t[n] for k in r] for r, t in zip(ranks, turns)]
        if n + 1 < len(bits):
            held = joined(*[[held[s], came[s]] for s in (0, 1)])
            ranks = [r + m for r, m in zip(ranks, new)]
    z = mixed(right, False)
    early = [swap(x, 1) for x in held]
    wide, state, aux = pl.pallas_call(
        functools.partial(first_half_kernel, [[r, [k ^ 1 for k in r]] for r in ranks]),
        out_shape=(
            jax.ShapeDtypeStruct((2, total * half, 2 * seqs), F32),
            jax.ShapeDtypeStruct((tokens, total, width), BF16),
            jax.ShapeDtypeStruct((aux_rows, width), F32),
        ),
        in_specs=[whole(SMEM)] + [whole(VMEM)] * 6,
        out_specs=(whole(VMEM),) * 3,
        compiler_params=params(16),
        name="first_half",
    )(row, pairwise_state, aux, held[0], early[0], held[1], early[1])
    *came, z, wide, state, aux = lax.optimization_barrier((*came, z, wide, state, aux))
    late = [swap(x, 1) for x in came]

    tiles = lax.all_to_all(tiles, "row", split_axis=0, concat_axis=0, tiled=True)

    block = 2
    pair_next, columns, _ = pl.pallas_call(
        functools.partial(pair_kernel, [[r, [k ^ 1 for k in r]] for r in new]),
        grid=(tokens // block,),
        out_shape=(
            jax.ShapeDtypeStruct((tokens, total, width), BF16),
            jax.ShapeDtypeStruct((tokens, total, width), F32),
            jax.ShapeDtypeStruct((2, total * half, 2 * seqs), F32),
        ),
        in_specs=[whole(SMEM), whole(VMEM), pl.BlockSpec((block, total, width), lambda g: (g, 0, 0))]
        + [whole(VMEM)] * 7,
        out_specs=(pl.BlockSpec((block, total, width), lambda g: (g, 0, 0)),) * 2 + (whole(VMEM),),
        scratch_shapes=[VMEM((2, total, inner), BF16)],
        input_output_aliases={5: 2},
        compiler_params=params(16),
        cost_estimate=pl.CostEstimate(
            flops=4 * total * inner * tokens * width,
            bytes_accessed=4 * inner * tokens * width + 8 * tokens * total * width,
            transcendentals=0,
        ),
        name="pair",
    )(row, aux, state, y, z, wide, came[0], late[0], came[1], late[1])

    block = 4
    out = pl.pallas_call(
        gate_kernel,
        grid=(tokens // block,),
        out_shape=jax.ShapeDtypeStruct((tokens, total, gated), BF16),
        in_specs=[
            whole(VMEM),
            pl.BlockSpec((block, total, width), lambda j: (j, 0, 0)),
            whole(VMEM),
            whole(VMEM),
        ],
        out_specs=pl.BlockSpec((block, total, gated), lambda j: (j, 0, 0)),
        scratch_shapes=[VMEM((count * tokens * tokens, width), F32)],
        compiler_params=params(24),
        cost_estimate=pl.CostEstimate(
            flops=4 * tokens * total * width * gated,
            bytes_accessed=tokens * total * (2 * gated + 6 * width),
            transcendentals=tokens * total * gated,
        ),
        name="gate",
    )(aux, columns, gates, tiles)
    return pair_next, out.transpose(1, 0, 2)


def solution(mesh):
    return jax.shard_map(
        functools.partial(body, count=mesh.shape["row"]),
        mesh=mesh,
        in_specs=(
            P(("groups", "row"), None, None),
            P(None, ("groups", "row"), None),
            P("groups"),
            P("groups"),
        )
        + (P(),) * 11,
        out_specs=(P(("groups", "row"), None, None), P("groups", "row", None)),
        check_vma=False,
    )
```

```python
import functools

import jax
import jax.numpy as jnp
from jax import lax
from jax.experimental import pallas as pl
from jax.experimental.pallas import tpu as pltpu
from jax.sharding import PartitionSpec as P

F32 = jnp.float32
BF16 = jnp.bfloat16
NT = (((1,), (1,)), ((), ()))
VMEM = pltpu.VMEM
SMEM = pltpu.SMEM
HBM = pltpu.HBM
LANES = 128


def whole(space):
    return pl.BlockSpec(memory_space=space)


def params(mib):
    return pltpu.CompilerParams(vmem_limit_bytes=mib * 1024 * 1024)


def fetch(sems, *pairs):
    copies = [pltpu.make_async_copy(a, b, sems.at[n]) for n, (a, b) in enumerate(pairs)]
    for copy in copies:
        copy.start()
    return copies


def finish(copies):
    for copy in copies:
        copy.wait()


def prepare_kernel(
    row_ref, depth_hbm, hom_hbm, scale_hbm, shift_hbm, src_hbm, tgt_hbm, depth_row_hbm, chain_hbm, chain_row_hbm,
    match_hbm, bias_hbm, gain_hbm, move_hbm, proj_hbm, gate_hbm,
    left_ref, front_ref, back_ref, aux_ref, gates_ref,
    depth_ref, hom_ref, scale_ref, shift_ref, both_ref, depth_row_ref, chain_ref, chain_row_ref, vec_ref, tmp_ref, sems,
):
    tokens, seqs, feats = hom_ref.shape
    pair_width = aux_ref.shape[1]
    total = depth_ref.shape[0]
    width = src_hbm.shape[0]
    half = width // 2
    gated = proj_hbm.shape[1]
    first_copies = fetch(
        sems,
        (hom_hbm, hom_ref),
        (depth_hbm, depth_ref),
        (scale_hbm, scale_ref),
        (shift_hbm, shift_ref),
        (src_hbm, both_ref.at[0:width]),
        (tgt_hbm, both_ref.at[width : 2 * width]),
        (chain_hbm, chain_ref),
        (depth_row_hbm, depth_row_ref),
        (chain_row_hbm, chain_row_ref),
        (match_hbm, vec_ref.at[0]),
        (bias_hbm, vec_ref.at[1]),
        (gain_hbm, vec_ref.at[2]),
        (move_hbm, vec_ref.at[3]),
        (proj_hbm, gates_ref.at[0]),
        (gate_hbm, gates_ref.at[1]),
    )
    finish(first_copies[:6])
    values = hom_ref[...].reshape(tokens * seqs, feats)
    ones = jnp.full((feats, feats), 1.0 / feats, BF16)
    centre = values.astype(F32) - jnp.dot(values, ones, preferred_element_type=F32)
    square = centre * centre
    high = square.astype(BF16)
    low = (square - high.astype(F32)).astype(BF16)
    spread = jnp.dot(high, ones, preferred_element_type=F32) + jnp.dot(
        low, ones, preferred_element_type=F32
    )
    normed = (centre * lax.rsqrt(spread + 1e-05) * scale_ref[...] + shift_ref[...]).astype(BF16)
    turned = lax.dot_general(both_ref[width : 2 * width], normed, NT, preferred_element_type=F32)
    plain = lax.dot_general(normed, both_ref[0:width], NT, preferred_element_type=F32)
    first = row_ref[0] * tokens
    row_pos = lax.broadcasted_iota(jnp.int32, (seqs, width), 0)
    lane = lax.broadcasted_iota(jnp.int32, (half, 2 * seqs), 1)
    seq_pos = jnp.where(lane < seqs, lane, lane - seqs)
    part = half // 2
    for n in range(tokens):
        depth = depth_ref[first + n]
        rows = slice(n * seqs, (n + 1) * seqs)
        left_ref[rows] = jnp.where(row_pos < depth, plain[rows], 0.0).astype(BF16)
        joint = jnp.concatenate([turned[0:half, rows], turned[half:width, rows]], axis=1)
        joint = jnp.where(seq_pos < depth, joint, 0.0)
        for side in (0, 1):
            tmp_ref[side, n * part : (n + 1) * part] = joint[side * part : (side + 1) * part]
    front_ref[0] = tmp_ref[0].astype(BF16)
    back_ref[0] = tmp_ref[1].astype(BF16)

    finish(first_copies[6:])
    same = lax.broadcasted_iota(jnp.int32, (total, total), 0) == lax.broadcasted_iota(
        jnp.int32, (total, total), 1
    )
    fill = jnp.ones((total, pair_width), BF16)

    def column(ref):
        diagonal = jnp.where(same, ref[...].astype(F32), 0.0).astype(BF16)
        return jnp.dot(diagonal, fill, preferred_element_type=F32)

    aux_ref[0:total] = 1.0 / jnp.maximum(column(depth_row_ref), 1.0)
    aux_ref[total : 2 * total] = column(chain_row_ref)
    for n in range(tokens):
        own = jnp.full((1, pair_width), depth_ref[first + n], jnp.int32).astype(F32)
        aux_ref[2 * total + n : 2 * total + n + 1] = 1.0 / jnp.maximum(own, 1.0)
        label = jnp.full((1, pair_width), chain_ref[first + n], jnp.int32).astype(F32)
        aux_ref[2 * total + 16 + n : 2 * total + 17 + n] = label
    for n in range(4):
        aux_ref[2 * total + 32 + n : 2 * total + 33 + n] = vec_ref[n]


def mix_kernel(strided, lhs_ref, weight_ref, out_ref, wide_ref):
    factor = lhs_ref.shape[1]
    half = factor // 2
    seqs = out_ref.shape[1] // factor
    width = weight_ref.shape[1]
    tokens = lhs_ref.shape[0] // seqs
    wide_ref[...] = weight_ref[...].astype(F32)

    def one(q, carry):
        if strided:
            pair = [wide_ref[pl.ds(q + t * half, factor, stride=factor), :] for t in (0, 1)]
        else:
            pair = [
                wide_ref[pl.ds(pl.multiple_of((q + t * half) * factor, factor), factor), :] for t in (0, 1)
            ]
        rhs = jnp.concatenate(pair, axis=1).astype(BF16)
        mixed = jnp.dot(lhs_ref[...], rhs, preferred_element_type=F32).astype(BF16)
        for n in range(tokens):
            rows = slice(n * seqs, (n + 1) * seqs)
            cols = slice(n % 2 * width, (n % 2 + 1) * width)
            for t in (0, 1):
                spot = pl.ds(pl.multiple_of((2 * q + t) * seqs, seqs), seqs)
                out_ref[n // 2, spot, cols] = mixed[rows, t * width : (t + 1) * width]
        return carry

    lax.fori_loop(0, half, one, 0)


def join_kernel(*refs):
    per = (len(refs) - 2) // 2
    for side in (0, 1):
        spot = 0
        for piece in refs[side * per : (side + 1) * per]:
            refs[2 * per + side][spot : spot + piece.shape[0]] = piece[...]
            spot += piece.shape[0]


def spread_items(row, wide_ref, sides):
    for side, pieces in enumerate(sides):
        for piece, ks in pieces:
            size = piece.shape[1]
            for m, k in enumerate(ks):
                spot = pl.ds(pl.multiple_of((row ^ k) * size, size), size)
                wide_ref[side, spot, :] = piece[m].astype(F32)


def first_half_kernel(orders, row_ref, state_ref, aux_ref, *rest):
    pieces, (wide_ref, state_out, aux_out) = rest[:-3], rest[-3:]
    per = len(pieces) // 2
    state_out[...] = state_ref[...]
    aux_out[...] = aux_ref[...]
    spread_items(
        row_ref[0], wide_ref, [list(zip(pieces[s * per : (s + 1) * per], orders[s])) for s in (0, 1)]
    )


def pair_kernel(orders, row_ref, aux_ref, state_ref, y_ref, wide_in, *rest):
    pieces, (next_ref, same_ref, cross_ref, wide_ref, lhs_ref, msg_ref) = rest[:-6], rest[-6:]
    step = pl.program_id(0)
    block, total, width = state_ref.shape
    lanes = pieces[0].shape[2]
    per = len(pieces) // 2
    count = msg_ref.shape[0]
    tokens = total // count
    groups = wide_ref.shape[1] // total

    @pl.when(step == 0)
    def _():
        spread_items(
            row_ref[0], wide_ref, [list(zip(pieces[s * per : (s + 1) * per], orders[s])) for s in (0, 1)]
        )

        def one(q, carry):
            for side in (0, 1):
                cols = pl.ds(pl.multiple_of((side * groups + q) * lanes, lanes), lanes)
                lhs_ref[:, cols] = wide_ref[side, pl.ds(q, total, stride=groups), :].astype(BF16)
            return carry

        lax.fori_loop(0, groups, one, 0, unroll=2)

    base = 2 * total
    match = aux_ref[base + 32 : base + 33]
    bias = aux_ref[base + 33 : base + 34]
    prod = jnp.dot(lhs_ref[...], y_ref[step], preferred_element_type=F32)
    done = []
    for t in range(block):
        own = step * block + t
        inv_own = aux_ref[pl.ds(base + own, 1)]
        label = aux_ref[pl.ds(base + 16 + own, 1)]
        extra = jnp.where(aux_ref[total:base] == label, match, 0.0) + bias
        value = prod[:, t * width : (t + 1) * width] * jnp.maximum(aux_ref[0:total], inv_own) + extra
        value = state_ref[t].astype(F32) + value
        next_ref[t] = value.astype(BF16)
        done.append(value)
    size = block * tokens
    for d in range(count):
        rows = slice(d * tokens, (d + 1) * tokens)
        msg_ref[d, pl.ds(pl.multiple_of(step * size, size), size), :] = jnp.concatenate(
            [value[rows] for value in done], axis=0
        )

    for core in (0, 1):

        @pl.when((step == pl.num_programs(0) - 1) & ((row_ref[0] & 1) == core))
        def _():
            for d in range(count):
                (same_ref if (d & 1) == core else cross_ref)[d // 2] = msg_ref[d].astype(BF16)


def pack_kernel(row_ref, same_ref, crossed_ref, *outs):
    chip = row_ref[0] >> 1
    for core in (0, 1):

        @pl.when((row_ref[0] & 1) == core)
        def _():
            for k, out_ref in enumerate(outs):
                out_ref[core] = same_ref[chip ^ k]
                out_ref[1 - core] = crossed_ref[chip ^ k]


def gate_kernel(row_ref, aux_ref, gates_ref, *rest):
    tiles, (out_ref, wide_ref) = rest[:-2], rest[-2:]
    step = pl.program_id(0)
    block, total = out_ref.shape[:2]
    rows, width = tiles[0].shape[1:]
    tokens = total // (2 * len(tiles))

    @pl.when(step == 0)
    def _():
        chip = row_ref[0] >> 1
        for k, tile in enumerate(tiles):
            for core in (0, 1):
                spot = pl.ds(pl.multiple_of(((chip ^ k) * 2 + core) * rows, rows), rows)
                wide_ref[spot, :] = tile[core].astype(F32)

    gain = aux_ref[2 * total + 34 : 2 * total + 35]
    shift = aux_ref[2 * total + 35 : 2 * total + 36]
    ones = jnp.full((width, width), 1.0 / width, BF16)
    none = jnp.zeros((width, width), BF16)
    means = jnp.concatenate(
        [jnp.concatenate([ones, none], axis=1), jnp.concatenate([none, ones], axis=1)], axis=0
    )
    for t in range(0, block, 2):
        pair = jnp.concatenate(
            [wide_ref[pl.ds(step * block + t + u, total, stride=tokens), :] for u in (0, 1)], axis=1
        )
        centre = pair - jnp.dot(pair.astype(BF16), means, preferred_element_type=F32)
        square = (centre * centre).astype(BF16)
        spread = jnp.dot(square, means, preferred_element_type=F32)
        scaled = centre * lax.rsqrt(spread + 1e-05)
        for u in (0, 1):
            normed = scaled[:, u * width : (u + 1) * width] * gain + shift
            normed = normed.astype(BF16)
            projected = jnp.dot(normed, gates_ref[0], preferred_element_type=F32)
            gating = jnp.dot(normed, gates_ref[1], preferred_element_type=F32)
            out_ref[t + u] = (projected * (0.5 + 0.5 * jnp.tanh(0.5 * gating))).astype(BF16)


def fixed(*shape):
    return pl.BlockSpec(shape, lambda g: (0,) * len(shape))


def body(
    pairwise_state,
    homolog_embedding,
    alignment_depth,
    chain_labels,
    homolog_layer_scale,
    homolog_layer_shift,
    outer_source_matrix,
    outer_target_matrix,
    output_weight,
    output_bias,
    chain_match,
    pairwise_norm_gain,
    pairwise_norm_bias,
    input_projection_weight,
    input_gate_weight,
    *,
    count,
):
    tokens, total, width = pairwise_state.shape
    seqs, _, feats = homolog_embedding.shape
    factor = outer_source_matrix.shape[1]
    half = factor // 2
    inner = factor * seqs
    gated = input_projection_weight.shape[1]
    row = lax.axis_index("row").astype(jnp.int32).reshape(1)

    def swap(array, bit):
        return lax.ppermute(array, "row", [(r, r ^ bit) for r in range(count)])

    aux_rows = 2 * total + 40
    part = tokens * half // 2
    left, front, back, aux, gates = pl.pallas_call(
        prepare_kernel,
        out_shape=(
            jax.ShapeDtypeStruct((tokens * seqs, factor), BF16),
            jax.ShapeDtypeStruct((1, part, 2 * seqs), BF16),
            jax.ShapeDtypeStruct((1, part, 2 * seqs), BF16),
            jax.ShapeDtypeStruct((aux_rows, width), F32),
            jax.ShapeDtypeStruct((2, width, gated), BF16),
        ),
        in_specs=[whole(SMEM)] + [whole(HBM)] * 15,
        out_specs=(whole(VMEM),) * 5,
        scratch_shapes=[
            SMEM((total,), jnp.int32),
            VMEM((tokens, seqs, feats), BF16),
            VMEM((1, feats), F32),
            VMEM((1, feats), F32),
            VMEM((2 * factor, feats), BF16),
            VMEM((1, total), jnp.int32),
            SMEM((total,), jnp.int32),
            VMEM((1, total), jnp.int32),
            VMEM((4, 1, width), F32),
            VMEM((2, part, 2 * seqs), F32),
            pltpu.SemaphoreType.DMA((15,)),
        ],
        name="prepare",
    )(
        row,
        alignment_depth,
        homolog_embedding.transpose(1, 0, 2),
        homolog_layer_scale.reshape(1, feats),
        homolog_layer_shift.reshape(1, feats),
        outer_source_matrix.T,
        outer_target_matrix.T,
        alignment_depth.reshape(1, total),
        chain_labels,
        chain_labels.reshape(1, total),
        chain_match.reshape(1, width),
        output_bias.reshape(1, width),
        pairwise_norm_gain.reshape(1, width),
        pairwise_norm_bias.reshape(1, width),
        input_projection_weight,
        input_gate_weight,
    )

    def joined(fronts, backs):
        shape = (sum(x.shape[0] for x in fronts), part, 2 * seqs)
        return pl.pallas_call(
            join_kernel,
            out_shape=(jax.ShapeDtypeStruct(shape, BF16),) * 2,
            in_specs=[whole(VMEM)] * (2 * len(fronts)),
            out_specs=(whole(VMEM),) * 2,
            compiler_params=params(16),
            name="join",
        )(*fronts, *backs)

    bits = [1 << n for n in range(1, count.bit_length() - 1)][::-1]
    turns = [bits, bits[-1:] + bits[:-1]]
    own = [front, back]
    far = [swap(x, t[0]) for x, t in zip(own, turns)]
    near = [swap(x, t[1]) for x, t in zip(own, turns)]
    both = [swap(x, t[1]) for x, t in zip(far, turns)]
    held = joined(*[[own[s], far[s], near[s], both[s]] for s in (0, 1)])
    ranks = [[0, t[0], t[1], t[0] ^ t[1]] for t in turns]
    for n in range(2, len(bits)):
        came = [swap(x, t[n]) for x, t in zip(held, turns)]
        new = [[k ^ t[n] for k in r] for r, t in zip(ranks, turns)]
        if n + 1 < len(bits):
            held = joined(*[[held[s], came[s]] for s in (0, 1)])
            ranks = [r + m for r, m in zip(ranks, new)]
    early = [swap(x, 1) for x in held]
    y = pl.pallas_call(
        functools.partial(mix_kernel, True),
        out_shape=jax.ShapeDtypeStruct((tokens // 2, inner, 2 * width), BF16),
        in_specs=[whole(VMEM), whole(VMEM)],
        out_specs=whole(VMEM),
        scratch_shapes=[VMEM((factor * factor, width), F32)],
        compiler_params=params(16),
        cost_estimate=pl.CostEstimate(
            flops=2 * tokens * seqs * factor * factor * width,
            bytes_accessed=2 * inner * tokens * width,
            transcendentals=0,
        ),
        name="mix",
    )(left, output_weight)
    wide, state, aux = pl.pallas_call(
        functools.partial(first_half_kernel, [[r, [k ^ 1 for k in r]] for r in ranks]),
        out_shape=(
            jax.ShapeDtypeStruct((2, count * part, 2 * seqs), F32),
            jax.ShapeDtypeStruct((tokens, total, width), BF16),
            jax.ShapeDtypeStruct((aux_rows, width), F32),
        ),
        in_specs=[whole(SMEM)] + [whole(VMEM)] * 6,
        out_specs=(whole(VMEM),) * 3,
        compiler_params=params(16),
        name="first_half",
    )(row, pairwise_state, aux, held[0], early[0], held[1], early[1])
    *came, y, wide, state, aux = lax.optimization_barrier((*came, y, wide, state, aux))
    late = [swap(x, 1) for x in came]

    block = 2
    chips = count // 2
    tile = tokens * tokens
    pair_next, same, cross, _ = pl.pallas_call(
        functools.partial(pair_kernel, [[r, [k ^ 1 for k in r]] for r in new]),
        grid=(tokens // block,),
        out_shape=(
            jax.ShapeDtypeStruct((tokens, total, width), BF16),
            jax.ShapeDtypeStruct((chips, tile, width), BF16),
            jax.ShapeDtypeStruct((chips, tile, width), BF16),
            jax.ShapeDtypeStruct((2, count * part, 2 * seqs), F32),
        ),
        in_specs=[whole(SMEM), whole(VMEM), pl.BlockSpec((block, total, width), lambda g: (g, 0, 0))]
        + [whole(VMEM)] * 6,
        out_specs=(pl.BlockSpec((block, total, width), lambda g: (g, 0, 0)),) + (whole(VMEM),) * 3,
        scratch_shapes=[VMEM((total, inner), BF16), VMEM((count, tile, width), F32)],
        input_output_aliases={4: 3},
        compiler_params=params(16),
        cost_estimate=pl.CostEstimate(
            flops=2 * total * inner * tokens * width,
            bytes_accessed=2 * inner * tokens * width + 8 * tokens * total * width,
            transcendentals=0,
        ),
        name="pair",
    )(row, aux, state, y, wide, came[0], late[0], came[1], late[1])

    crossed = swap(cross, 1)
    tiles = pl.pallas_call(
        pack_kernel,
        out_shape=(jax.ShapeDtypeStruct((2, tile, width), BF16),) * chips,
        in_specs=[whole(SMEM), whole(VMEM), whole(VMEM)],
        out_specs=(whole(VMEM),) * chips,
        compiler_params=params(16),
        name="pack",
    )(row, same, crossed)
    tiles = [tiles[0]] + [swap(tiles[k], 2 * k) for k in range(1, chips)]

    block = 4
    out = pl.pallas_call(
        gate_kernel,
        grid=(tokens // block,),
        out_shape=jax.ShapeDtypeStruct((tokens, total, gated), BF16),
        in_specs=[whole(SMEM)] + [whole(VMEM)] * (2 + chips),
        out_specs=pl.BlockSpec((block, total, gated), lambda j: (j, 0, 0)),
        scratch_shapes=[VMEM((count * tile, width), F32)],
        compiler_params=params(24),
        cost_estimate=pl.CostEstimate(
            flops=4 * tokens * total * width * gated,
            bytes_accessed=tokens * total * (2 * gated + 6 * width),
            transcendentals=tokens * total * gated,
        ),
        name="gate",
    )(row, aux, gates, *tiles)
    return pair_next, out.transpose(1, 0, 2)


def solution(mesh):
    return jax.shard_map(
        functools.partial(body, count=mesh.shape["row"]),
        mesh=mesh,
        in_specs=(
            P(("groups", "row"), None, None),
            P(None, ("groups", "row"), None),
            P("groups"),
            P("groups"),
        )
        + (P(),) * 11,
        out_specs=(P(("groups", "row"), None, None), P("groups", "row", None)),
        check_vma=False,
    )
```

```python
import functools

import jax
import jax.numpy as jnp
from jax import lax
from jax.experimental import pallas as pl
from jax.experimental.pallas import tpu as pltpu
from jax.sharding import PartitionSpec as P

F32 = jnp.float32
BF16 = jnp.bfloat16
NT = (((1,), (1,)), ((), ()))
VMEM = pltpu.VMEM
SMEM = pltpu.SMEM
HBM = pltpu.HBM
LANES = 128


def whole(space):
    return pl.BlockSpec(memory_space=space)


def params(mib):
    return pltpu.CompilerParams(vmem_limit_bytes=mib * 1024 * 1024)


def fetch(sems, *pairs):
    copies = [pltpu.make_async_copy(a, b, sems.at[n]) for n, (a, b) in enumerate(pairs)]
    for copy in copies:
        copy.start()
    return copies


def finish(copies):
    for copy in copies:
        copy.wait()


def prepare_kernel(
    row_ref, depth_hbm, hom_hbm, scale_hbm, shift_hbm, src_hbm, tgt_hbm, depth_row_hbm, chain_hbm, chain_row_hbm,
    match_hbm, bias_hbm, gain_hbm, move_hbm, proj_hbm, gate_hbm, weight_hbm,
    mix_ref, item_ref, aux_ref, gates_ref,
    depth_ref, hom_ref, scale_ref, shift_ref, both_ref, depth_row_ref, chain_ref, chain_row_ref, vec_ref, sems,
):
    tokens, seqs, feats = hom_ref.shape
    pair_width = aux_ref.shape[1]
    total = depth_ref.shape[0]
    width = src_hbm.shape[0]
    half = width // 2
    gated = proj_hbm.shape[1]
    first_copies = fetch(
        sems,
        (hom_hbm, hom_ref),
        (depth_hbm, depth_ref),
        (scale_hbm, scale_ref),
        (shift_hbm, shift_ref),
        (src_hbm, both_ref.at[0:width]),
        (tgt_hbm, both_ref.at[width : 2 * width]),
        (chain_hbm, chain_ref),
        (depth_row_hbm, depth_row_ref),
        (chain_row_hbm, chain_row_ref),
        (match_hbm, vec_ref.at[0]),
        (bias_hbm, vec_ref.at[1]),
        (gain_hbm, vec_ref.at[2]),
        (move_hbm, vec_ref.at[3]),
        (proj_hbm, gates_ref.at[0]),
        (gate_hbm, gates_ref.at[1]),
        (weight_hbm, mix_ref.at[tokens * seqs : tokens * seqs + width * width]),
    )
    finish(first_copies[:6])
    values = hom_ref[...].reshape(tokens * seqs, feats)
    ones = jnp.full((feats, feats), 1.0 / feats, BF16)
    centre = values.astype(F32) - jnp.dot(values, ones, preferred_element_type=F32)
    square = centre * centre
    high = square.astype(BF16)
    low = (square - high.astype(F32)).astype(BF16)
    spread = jnp.dot(high, ones, preferred_element_type=F32) + jnp.dot(
        low, ones, preferred_element_type=F32
    )
    normed = (centre * lax.rsqrt(spread + 1e-05) * scale_ref[...] + shift_ref[...]).astype(BF16)
    turned = lax.dot_general(both_ref[width : 2 * width], normed, NT, preferred_element_type=F32)
    plain = lax.dot_general(normed, both_ref[0:width], NT, preferred_element_type=F32)
    first = row_ref[0] * tokens
    row_pos = lax.broadcasted_iota(jnp.int32, (seqs, width), 0)
    lane = lax.broadcasted_iota(jnp.int32, (half, 2 * seqs), 1)
    seq_pos = jnp.where(lane < seqs, lane, lane - seqs)
    for n in range(tokens):
        depth = depth_ref[first + n]
        rows = slice(n * seqs, (n + 1) * seqs)
        mix_ref[rows, 0:width] = jnp.where(row_pos < depth, plain[rows], 0.0).astype(BF16)
        joint = jnp.concatenate([turned[0:half, rows], turned[half:width, rows]], axis=1)
        item_ref[0, n * half : (n + 1) * half] = jnp.where(seq_pos < depth, joint, 0.0).astype(BF16)

    finish(first_copies[6:])
    same = lax.broadcasted_iota(jnp.int32, (total, total), 0) == lax.broadcasted_iota(
        jnp.int32, (total, total), 1
    )
    fill = jnp.ones((total, pair_width), BF16)

    def column(ref):
        diagonal = jnp.where(same, ref[...].astype(F32), 0.0).astype(BF16)
        return jnp.dot(diagonal, fill, preferred_element_type=F32)

    aux_ref[0:total] = 1.0 / jnp.maximum(column(depth_row_ref), 1.0)
    aux_ref[total : 2 * total] = column(chain_row_ref)
    for n in range(tokens):
        own = jnp.full((1, pair_width), depth_ref[first + n], jnp.int32).astype(F32)
        aux_ref[2 * total + n : 2 * total + n + 1] = 1.0 / jnp.maximum(own, 1.0)
        label = jnp.full((1, pair_width), chain_ref[first + n], jnp.int32).astype(F32)
        aux_ref[2 * total + 16 + n : 2 * total + 17 + n] = label
    for n in range(4):
        aux_ref[2 * total + 32 + n : 2 * total + 33 + n] = vec_ref[n]


def mix_kernel(factor, mix_ref, out_ref, wide_ref):
    half = factor // 2
    seqs = out_ref.shape[1] // factor
    width = mix_ref.shape[1]
    lefts = mix_ref.shape[0] - factor * factor
    tokens = lefts // seqs
    wide_ref[...] = mix_ref[lefts : lefts + factor * factor].astype(F32)

    def one(q, carry):
        pair = [wide_ref[pl.ds(q + t * half, factor, stride=factor), :] for t in (0, 1)]
        rhs = jnp.concatenate(pair, axis=1).astype(BF16)
        mixed = jnp.dot(mix_ref[0:lefts, 0:factor], rhs, preferred_element_type=F32).astype(BF16)
        for n in range(tokens):
            rows = slice(n * seqs, (n + 1) * seqs)
            cols = slice(n % 2 * width, (n % 2 + 1) * width)
            for t in (0, 1):
                spot = pl.ds(pl.multiple_of((2 * q + t) * seqs, seqs), seqs)
                out_ref[n // 2, spot, cols] = mixed[rows, t * width : (t + 1) * width]
        return carry

    lax.fori_loop(0, half, one, 0, unroll=4)


def join_kernel(*refs):
    spot = 0
    for piece in refs[:-1]:
        refs[-1][spot : spot + piece.shape[0]] = piece[...]
        spot += piece.shape[0]


def spread_items(row, wide_ref, pieces, orders):
    for piece, ks in zip(pieces, orders):
        size = piece.shape[1]
        for m, k in enumerate(ks):
            spot = pl.ds(pl.multiple_of((row ^ k) * size, size), size)
            wide_ref[spot, :] = piece[m].astype(F32)


def first_half_kernel(orders, row_ref, state_ref, aux_ref, *rest):
    pieces, (wide_ref, state_out, aux_out) = rest[:-3], rest[-3:]
    state_out[...] = state_ref[...]
    aux_out[...] = aux_ref[...]
    spread_items(row_ref[0], wide_ref, pieces, orders)


def pair_kernel(orders, row_ref, aux_ref, state_ref, y_ref, wide_in, *rest):
    pieces, (next_ref, same_ref, cross_ref, wide_ref, lhs_ref, msg_ref) = rest[:-6], rest[-6:]
    step = pl.program_id(0)
    block, total, width = state_ref.shape
    lanes = pieces[0].shape[2]
    count = msg_ref.shape[0]
    tokens = total // count
    groups = wide_ref.shape[0] // total

    @pl.when(step == 0)
    def _():
        spread_items(row_ref[0], wide_ref, pieces, orders)

        def one(q, carry):
            cols = pl.ds(pl.multiple_of(q * lanes, lanes), lanes)
            lhs_ref[:, cols] = wide_ref[pl.ds(q, total, stride=groups), :].astype(BF16)
            return carry

        lax.fori_loop(0, groups, one, 0, unroll=4)

    base = 2 * total
    match = aux_ref[base + 32 : base + 33]
    bias = aux_ref[base + 33 : base + 34]
    prod = jnp.dot(lhs_ref[...], y_ref[step], preferred_element_type=F32)
    done = []
    for t in range(block):
        own = step * block + t
        inv_own = aux_ref[pl.ds(base + own, 1)]
        label = aux_ref[pl.ds(base + 16 + own, 1)]
        extra = jnp.where(aux_ref[total:base] == label, match, 0.0) + bias
        value = prod[:, t * width : (t + 1) * width] * jnp.maximum(aux_ref[0:total], inv_own) + extra
        value = state_ref[t].astype(F32) + value
        next_ref[t] = value.astype(BF16)
        done.append(value)
    size = block * tokens
    for d in range(count):
        rows = slice(d * tokens, (d + 1) * tokens)
        msg_ref[d, pl.ds(pl.multiple_of(step * size, size), size), :] = jnp.concatenate(
            [value[rows] for value in done], axis=0
        )

    for core in (0, 1):

        @pl.when((step == pl.num_programs(0) - 1) & ((row_ref[0] & 1) == core))
        def _():
            for d in range(count):
                (same_ref if (d & 1) == core else cross_ref)[d // 2] = msg_ref[d].astype(BF16)


def pack_kernel(row_ref, same_ref, crossed_ref, *outs):
    chip = row_ref[0] >> 1
    for core in (0, 1):

        @pl.when((row_ref[0] & 1) == core)
        def _():
            for k, out_ref in enumerate(outs):
                out_ref[core] = same_ref[chip ^ k]
                out_ref[1 - core] = crossed_ref[chip ^ k]


def gate_kernel(row_ref, aux_ref, gates_ref, *rest):
    tiles, (out_ref, wide_ref) = rest[:-2], rest[-2:]
    step = pl.program_id(0)
    block, total = out_ref.shape[:2]
    rows, width = tiles[0].shape[1:]
    tokens = total // (2 * len(tiles))

    @pl.when(step == 0)
    def _():
        chip = row_ref[0] >> 1
        for k, tile in enumerate(tiles):
            for core in (0, 1):
                spot = pl.ds(pl.multiple_of(((chip ^ k) * 2 + core) * rows, rows), rows)
                wide_ref[spot, :] = tile[core].astype(F32)

    gain = aux_ref[2 * total + 34 : 2 * total + 35]
    shift = aux_ref[2 * total + 35 : 2 * total + 36]
    ones = jnp.full((width, width), 1.0 / width, BF16)
    none = jnp.zeros((width, width), BF16)
    means = jnp.concatenate(
        [jnp.concatenate([ones, none], axis=1), jnp.concatenate([none, ones], axis=1)], axis=0
    )
    for t in range(0, block, 2):
        pair = jnp.concatenate(
            [wide_ref[pl.ds(step * block + t + u, total, stride=tokens), :] for u in (0, 1)], axis=1
        )
        centre = pair - jnp.dot(pair.astype(BF16), means, preferred_element_type=F32)
        square = (centre * centre).astype(BF16)
        spread = jnp.dot(square, means, preferred_element_type=F32)
        scaled = centre * lax.rsqrt(spread + 1e-05)
        for u in (0, 1):
            normed = scaled[:, u * width : (u + 1) * width] * gain + shift
            normed = normed.astype(BF16)
            projected = jnp.dot(normed, gates_ref[0], preferred_element_type=F32)
            gating = jnp.dot(normed, gates_ref[1], preferred_element_type=F32)
            out_ref[t + u] = (projected * (0.5 + 0.5 * jnp.tanh(0.5 * gating))).astype(BF16)


def fixed(*shape):
    return pl.BlockSpec(shape, lambda g: (0,) * len(shape))


def body(
    pairwise_state,
    homolog_embedding,
    alignment_depth,
    chain_labels,
    homolog_layer_scale,
    homolog_layer_shift,
    outer_source_matrix,
    outer_target_matrix,
    output_weight,
    output_bias,
    chain_match,
    pairwise_norm_gain,
    pairwise_norm_bias,
    input_projection_weight,
    input_gate_weight,
    *,
    count,
):
    tokens, total, width = pairwise_state.shape
    seqs, _, feats = homolog_embedding.shape
    factor = outer_source_matrix.shape[1]
    half = factor // 2
    inner = factor * seqs
    gated = input_projection_weight.shape[1]
    row = lax.axis_index("row").astype(jnp.int32).reshape(1)

    def swap(array, bit):
        return lax.ppermute(array, "row", [(r, r ^ bit) for r in range(count)])

    aux_rows = 2 * total + 40
    part = tokens * half
    mix_rows = tokens * seqs + factor * factor
    to_mix, item, aux, gates = pl.pallas_call(
        prepare_kernel,
        out_shape=(
            jax.ShapeDtypeStruct((mix_rows, width), BF16),
            jax.ShapeDtypeStruct((1, part, 2 * seqs), BF16),
            jax.ShapeDtypeStruct((aux_rows, width), F32),
            jax.ShapeDtypeStruct((2, width, gated), BF16),
        ),
        in_specs=[whole(SMEM)] + [whole(HBM)] * 16,
        out_specs=(whole(VMEM),) * 4,
        scratch_shapes=[
            SMEM((total,), jnp.int32),
            VMEM((tokens, seqs, feats), BF16),
            VMEM((1, feats), F32),
            VMEM((1, feats), F32),
            VMEM((2 * factor, feats), BF16),
            VMEM((1, total), jnp.int32),
            SMEM((total,), jnp.int32),
            VMEM((1, total), jnp.int32),
            VMEM((4, 1, width), F32),
            pltpu.SemaphoreType.DMA((16,)),
        ],
        name="prepare",
    )(
        row,
        alignment_depth,
        homolog_embedding.transpose(1, 0, 2),
        homolog_layer_scale.reshape(1, feats),
        homolog_layer_shift.reshape(1, feats),
        outer_source_matrix.T,
        outer_target_matrix.T,
        alignment_depth.reshape(1, total),
        chain_labels,
        chain_labels.reshape(1, total),
        chain_match.reshape(1, width),
        output_bias.reshape(1, width),
        pairwise_norm_gain.reshape(1, width),
        pairwise_norm_bias.reshape(1, width),
        input_projection_weight,
        input_gate_weight,
        output_weight,
    )

    y = pl.pallas_call(
        functools.partial(mix_kernel, factor),
        out_shape=jax.ShapeDtypeStruct((tokens // 2, inner, 2 * width), BF16),
        in_specs=[whole(VMEM)],
        out_specs=whole(VMEM),
        scratch_shapes=[VMEM((factor * factor, width), F32)],
        compiler_params=params(16),
        cost_estimate=pl.CostEstimate(
            flops=2 * tokens * seqs * factor * factor * width,
            bytes_accessed=2 * inner * tokens * width,
            transcendentals=0,
        ),
        name="mix",
    )(to_mix)

    def joined(*pieces):
        return pl.pallas_call(
            join_kernel,
            out_shape=jax.ShapeDtypeStruct((sum(x.shape[0] for x in pieces), part, 2 * seqs), BF16),
            in_specs=[whole(VMEM)] * len(pieces),
            out_specs=whole(VMEM),
            compiler_params=params(16),
            name="join",
        )(*pieces)

    held, ranks = item, [0]
    bit = count // 2
    while bit > 1:
        came, new = swap(held, bit), [k ^ bit for k in ranks]
        if bit > 2:
            held, ranks = joined(held, came), ranks + new
        bit //= 2
    early = swap(held, 1)
    wide, state, aux = pl.pallas_call(
        functools.partial(first_half_kernel, [ranks, [k ^ 1 for k in ranks]]),
        out_shape=(
            jax.ShapeDtypeStruct((count * part, 2 * seqs), F32),
            jax.ShapeDtypeStruct((tokens, total, width), BF16),
            jax.ShapeDtypeStruct((aux_rows, width), F32),
        ),
        in_specs=[whole(SMEM)] + [whole(VMEM)] * 4,
        out_specs=(whole(VMEM),) * 3,
        compiler_params=params(16),
        name="first_half",
    )(row, pairwise_state, aux, held, early)
    came, y, wide, state, aux = lax.optimization_barrier((came, y, wide, state, aux))
    late = swap(came, 1)

    block = 2
    chips = count // 2
    tile = tokens * tokens
    pair_next, same, cross, _ = pl.pallas_call(
        functools.partial(pair_kernel, [new, [k ^ 1 for k in new]]),
        grid=(tokens // block,),
        out_shape=(
            jax.ShapeDtypeStruct((tokens, total, width), BF16),
            jax.ShapeDtypeStruct((chips, tile, width), BF16),
            jax.ShapeDtypeStruct((chips, tile, width), BF16),
            jax.ShapeDtypeStruct((count * part, 2 * seqs), F32),
        ),
        in_specs=[whole(SMEM), whole(VMEM), pl.BlockSpec((block, total, width), lambda g: (g, 0, 0))]
        + [whole(VMEM)] * 4,
        out_specs=(pl.BlockSpec((block, total, width), lambda g: (g, 0, 0)),) + (whole(VMEM),) * 3,
        scratch_shapes=[VMEM((total, inner), BF16), VMEM((count, tile, width), F32)],
        input_output_aliases={4: 3},
        compiler_params=params(16),
        cost_estimate=pl.CostEstimate(
            flops=2 * total * inner * tokens * width,
            bytes_accessed=2 * inner * tokens * width + 8 * tokens * total * width,
            transcendentals=0,
        ),
        name="pair",
    )(row, aux, state, y, wide, came, late)

    crossed = swap(cross, 1)
    tiles = pl.pallas_call(
        pack_kernel,
        out_shape=(jax.ShapeDtypeStruct((2, tile, width), BF16),) * chips,
        in_specs=[whole(SMEM), whole(VMEM), whole(VMEM)],
        out_specs=(whole(VMEM),) * chips,
        compiler_params=params(16),
        name="pack",
    )(row, same, crossed)
    moved = {k: swap(tiles[k], 2 * k) for k in range(chips - 1, 0, -1)}
    tiles = [tiles[0]] + [moved[k] for k in range(1, chips)]

    block = 4
    out = pl.pallas_call(
        gate_kernel,
        grid=(tokens // block,),
        out_shape=jax.ShapeDtypeStruct((tokens, total, gated), BF16),
        in_specs=[whole(SMEM)] + [whole(VMEM)] * (2 + chips),
        out_specs=pl.BlockSpec((block, total, gated), lambda j: (j, 0, 0)),
        scratch_shapes=[VMEM((count * tile, width), F32)],
        compiler_params=params(24),
        cost_estimate=pl.CostEstimate(
            flops=4 * tokens * total * width * gated,
            bytes_accessed=tokens * total * (2 * gated + 6 * width),
            transcendentals=tokens * total * gated,
        ),
        name="gate",
    )(row, aux, gates, *tiles)
    return pair_next, out.transpose(1, 0, 2)


def solution(mesh):
    return jax.shard_map(
        functools.partial(body, count=mesh.shape["row"]),
        mesh=mesh,
        in_specs=(
            P(("groups", "row"), None, None),
            P(None, ("groups", "row"), None),
            P("groups"),
            P("groups"),
        )
        + (P(),) * 11,
        out_specs=(P(("groups", "row"), None, None), P("groups", "row", None)),
        check_vma=False,
    )
```

```python
import functools

import jax
import jax.numpy as jnp
from jax import lax
from jax.experimental import pallas as pl
from jax.experimental.pallas import tpu as pltpu
from jax.sharding import PartitionSpec as P

F32 = jnp.float32
BF16 = jnp.bfloat16
NT = (((1,), (1,)), ((), ()))
VMEM = pltpu.VMEM
SMEM = pltpu.SMEM
HBM = pltpu.HBM
LANES = 128


def whole(space):
    return pl.BlockSpec(memory_space=space)


def params(mib):
    return pltpu.CompilerParams(vmem_limit_bytes=mib * 1024 * 1024)


def fetch(sems, *pairs):
    copies = [pltpu.make_async_copy(a, b, sems.at[n]) for n, (a, b) in enumerate(pairs)]
    for copy in copies:
        copy.start()
    return copies


def finish(copies):
    for copy in copies:
        copy.wait()


def prepare_kernel(
    row_ref, depth_hbm, hom_hbm, scale_hbm, shift_hbm, src_hbm, tgt_hbm, depth_row_hbm, chain_hbm, chain_row_hbm,
    match_hbm, bias_hbm, gain_hbm, move_hbm, proj_hbm, gate_hbm, weight_hbm,
    mix_ref, item_ref, aux_ref, gates_ref,
    depth_ref, hom_ref, scale_ref, shift_ref, both_ref, depth_row_ref, chain_ref, chain_row_ref, vec_ref, sems,
):
    tokens, seqs, feats = hom_ref.shape
    pair_width = aux_ref.shape[1]
    total = depth_ref.shape[0]
    width = src_hbm.shape[0]
    half = width // 2
    gated = proj_hbm.shape[1]
    first_copies = fetch(
        sems,
        (hom_hbm, hom_ref),
        (depth_hbm, depth_ref),
        (scale_hbm, scale_ref),
        (shift_hbm, shift_ref),
        (src_hbm, both_ref.at[0:width]),
        (tgt_hbm, both_ref.at[width : 2 * width]),
        (chain_hbm, chain_ref),
        (depth_row_hbm, depth_row_ref),
        (chain_row_hbm, chain_row_ref),
        (match_hbm, vec_ref.at[0]),
        (bias_hbm, vec_ref.at[1]),
        (gain_hbm, vec_ref.at[2]),
        (move_hbm, vec_ref.at[3]),
        (proj_hbm, gates_ref.at[0]),
        (gate_hbm, gates_ref.at[1]),
        (weight_hbm, mix_ref.at[tokens * seqs : tokens * seqs + width * width]),
    )
    finish(first_copies[:6])
    values = hom_ref[...].reshape(tokens * seqs, feats)
    ones = jnp.full((feats, feats), 1.0 / feats, BF16)
    centre = values.astype(F32) - jnp.dot(values, ones, preferred_element_type=F32)
    square = centre * centre
    high = square.astype(BF16)
    low = (square - high.astype(F32)).astype(BF16)
    spread = jnp.dot(high, ones, preferred_element_type=F32) + jnp.dot(
        low, ones, preferred_element_type=F32
    )
    normed = (centre * lax.rsqrt(spread + 1e-05) * scale_ref[...] + shift_ref[...]).astype(BF16)
    turned = lax.dot_general(both_ref[width : 2 * width], normed, NT, preferred_element_type=F32)
    plain = lax.dot_general(normed, both_ref[0:width], NT, preferred_element_type=F32)
    first = row_ref[0] * tokens
    row_pos = lax.broadcasted_iota(jnp.int32, (seqs, width), 0)
    lane = lax.broadcasted_iota(jnp.int32, (half, 2 * seqs), 1)
    seq_pos = jnp.where(lane < seqs, lane, lane - seqs)
    for n in range(tokens):
        depth = depth_ref[first + n]
        rows = slice(n * seqs, (n + 1) * seqs)
        mix_ref[rows, 0:width] = jnp.where(row_pos < depth, plain[rows], 0.0).astype(BF16)
        joint = jnp.concatenate([turned[0:half, rows], turned[half:width, rows]], axis=1)
        item_ref[0, n * half : (n + 1) * half] = jnp.where(seq_pos < depth, joint, 0.0).astype(BF16)

    finish(first_copies[6:])
    same = lax.broadcasted_iota(jnp.int32, (total, total), 0) == lax.broadcasted_iota(
        jnp.int32, (total, total), 1
    )
    fill = jnp.ones((total, pair_width), BF16)

    def column(ref):
        diagonal = jnp.where(same, ref[...].astype(F32), 0.0).astype(BF16)
        return jnp.dot(diagonal, fill, preferred_element_type=F32)

    aux_ref[0:total] = 1.0 / jnp.maximum(column(depth_row_ref), 1.0)
    aux_ref[total : 2 * total] = column(chain_row_ref)
    for n in range(tokens):
        own = jnp.full((1, pair_width), depth_ref[first + n], jnp.int32).astype(F32)
        aux_ref[2 * total + n : 2 * total + n + 1] = 1.0 / jnp.maximum(own, 1.0)
        label = jnp.full((1, pair_width), chain_ref[first + n], jnp.int32).astype(F32)
        aux_ref[2 * total + 16 + n : 2 * total + 17 + n] = label
    for n in range(4):
        aux_ref[2 * total + 32 + n : 2 * total + 33 + n] = vec_ref[n]


def mix_kernel(factor, mix_ref, out_ref, wide_ref):
    half = factor // 2
    seqs = out_ref.shape[1] // factor
    width = mix_ref.shape[1]
    lefts = mix_ref.shape[0] - factor * factor
    tokens = lefts // seqs
    wide_ref[...] = mix_ref[lefts : lefts + factor * factor].astype(F32)

    def one(q, carry):
        pair = [wide_ref[pl.ds(q + t * half, factor, stride=factor), :] for t in (0, 1)]
        rhs = jnp.concatenate(pair, axis=1).astype(BF16)
        mixed = jnp.dot(mix_ref[0:lefts, 0:factor], rhs, preferred_element_type=F32).astype(BF16)
        for n in range(tokens):
            rows = slice(n * seqs, (n + 1) * seqs)
            cols = slice(n % 2 * width, (n % 2 + 1) * width)
            for t in (0, 1):
                spot = pl.ds(pl.multiple_of((2 * q + t) * seqs, seqs), seqs)
                out_ref[n // 2, spot, cols] = mixed[rows, t * width : (t + 1) * width]
        return carry

    lax.fori_loop(0, half, one, 0, unroll=4)


def join_kernel(*refs):
    spot = 0
    for piece in refs[:-1]:
        refs[-1][spot : spot + piece.shape[0]] = piece[...]
        spot += piece.shape[0]


def spread_items(row, wide_ref, pieces, orders):
    for piece, ks in zip(pieces, orders):
        size = piece.shape[1]
        for m, k in enumerate(ks):
            spot = pl.ds(pl.multiple_of((row ^ k) * size, size), size)
            wide_ref[spot, :] = piece[m].astype(F32)


def first_half_kernel(orders, row_ref, state_ref, aux_ref, *rest):
    pieces, (wide_ref, state_out, aux_out) = rest[:-3], rest[-3:]
    state_out[...] = state_ref[...]
    aux_out[...] = aux_ref[...]
    spread_items(row_ref[0], wide_ref, pieces, orders)


def pair_kernel(orders, row_ref, aux_ref, state_ref, y_ref, wide_in, *rest):
    pieces, (next_ref, same_ref, cross_ref, wide_ref, lhs_ref, msg_ref) = rest[:-6], rest[-6:]
    step = pl.program_id(0)
    block, total, width = state_ref.shape
    lanes = pieces[0].shape[2]
    count = msg_ref.shape[0]
    tokens = total // count
    groups = wide_ref.shape[0] // total

    @pl.when(step == 0)
    def _():
        spread_items(row_ref[0], wide_ref, pieces, orders)

        def one(q, carry):
            cols = pl.ds(pl.multiple_of(q * lanes, lanes), lanes)
            lhs_ref[:, cols] = wide_ref[pl.ds(q, total, stride=groups), :].astype(BF16)
            return carry

        lax.fori_loop(0, groups, one, 0, unroll=4)

    base = 2 * total
    match = aux_ref[base + 32 : base + 33]
    bias = aux_ref[base + 33 : base + 34]
    prod = jnp.dot(lhs_ref[...], y_ref[step], preferred_element_type=F32)
    done = []
    for t in range(block):
        own = step * block + t
        inv_own = aux_ref[pl.ds(base + own, 1)]
        label = aux_ref[pl.ds(base + 16 + own, 1)]
        extra = jnp.where(aux_ref[total:base] == label, match, 0.0) + bias
        value = prod[:, t * width : (t + 1) * width] * jnp.maximum(aux_ref[0:total], inv_own) + extra
        value = state_ref[t].astype(F32) + value
        next_ref[t] = value.astype(BF16)
        done.append(value)
    size = block * tokens
    for d in range(count):
        rows = slice(d * tokens, (d + 1) * tokens)
        msg_ref[d, pl.ds(pl.multiple_of(step * size, size), size), :] = jnp.concatenate(
            [value[rows] for value in done], axis=0
        )

    for core in (0, 1):

        @pl.when((step == pl.num_programs(0) - 1) & ((row_ref[0] & 1) == core))
        def _():
            for d in range(count):
                (same_ref if (d & 1) == core else cross_ref)[d // 2] = msg_ref[d].astype(BF16)


def pack_kernel(row_ref, same_ref, crossed_ref, *outs):
    chip = row_ref[0] >> 1
    for core in (0, 1):

        @pl.when((row_ref[0] & 1) == core)
        def _():
            for k, out_ref in enumerate(outs):
                out_ref[core] = same_ref[chip ^ k]
                out_ref[1 - core] = crossed_ref[chip ^ k]


def gate_kernel(row_ref, aux_ref, gates_ref, *rest):
    tiles, (out_ref, wide_ref) = rest[:-2], rest[-2:]
    step = pl.program_id(0)
    block, total = out_ref.shape[:2]
    rows, width = tiles[0].shape[1:]
    tokens = total // (2 * len(tiles))

    @pl.when(step == 0)
    def _():
        chip = row_ref[0] >> 1
        for k, tile in enumerate(tiles):
            for core in (0, 1):
                spot = pl.ds(pl.multiple_of(((chip ^ k) * 2 + core) * rows, rows), rows)
                wide_ref[spot, :] = tile[core].astype(F32)

    gain = aux_ref[2 * total + 34 : 2 * total + 35]
    shift = aux_ref[2 * total + 35 : 2 * total + 36]
    ones = jnp.full((width, width), 1.0 / width, BF16)
    none = jnp.zeros((width, width), BF16)
    means = jnp.concatenate(
        [jnp.concatenate([ones, none], axis=1), jnp.concatenate([none, ones], axis=1)], axis=0
    )
    for t in range(0, block, 2):
        pair = jnp.concatenate(
            [wide_ref[pl.ds(step * block + t + u, total, stride=tokens), :] for u in (0, 1)], axis=1
        )
        centre = pair - jnp.dot(pair.astype(BF16), means, preferred_element_type=F32)
        square = (centre * centre).astype(BF16)
        spread = jnp.dot(square, means, preferred_element_type=F32)
        scaled = centre * lax.rsqrt(spread + 1e-05)
        for u in (0, 1):
            normed = scaled[:, u * width : (u + 1) * width] * gain + shift
            normed = normed.astype(BF16)
            projected = jnp.dot(normed, gates_ref[0], preferred_element_type=F32)
            gating = jnp.dot(normed, gates_ref[1], preferred_element_type=F32)
            out_ref[t + u] = (projected * (0.5 + 0.5 * jnp.tanh(0.5 * gating))).astype(BF16)


def fixed(*shape):
    return pl.BlockSpec(shape, lambda g: (0,) * len(shape))


def body(
    pairwise_state,
    homolog_embedding,
    alignment_depth,
    chain_labels,
    homolog_layer_scale,
    homolog_layer_shift,
    outer_source_matrix,
    outer_target_matrix,
    output_weight,
    output_bias,
    chain_match,
    pairwise_norm_gain,
    pairwise_norm_bias,
    input_projection_weight,
    input_gate_weight,
    *,
    count,
):
    tokens, total, width = pairwise_state.shape
    seqs, _, feats = homolog_embedding.shape
    factor = outer_source_matrix.shape[1]
    half = factor // 2
    inner = factor * seqs
    gated = input_projection_weight.shape[1]
    row = lax.axis_index("row").astype(jnp.int32).reshape(1)

    def swap(array, bit):
        return lax.ppermute(array, "row", [(r, r ^ bit) for r in range(count)])

    aux_rows = 2 * total + 40
    part = tokens * half
    mix_rows = tokens * seqs + factor * factor
    to_mix, item, aux, gates = pl.pallas_call(
        prepare_kernel,
        out_shape=(
            jax.ShapeDtypeStruct((mix_rows, width), BF16),
            jax.ShapeDtypeStruct((1, part, 2 * seqs), BF16),
            jax.ShapeDtypeStruct((aux_rows, width), F32),
            jax.ShapeDtypeStruct((2, width, gated), BF16),
        ),
        in_specs=[whole(SMEM)] + [whole(HBM)] * 16,
        out_specs=(whole(VMEM),) * 4,
        scratch_shapes=[
            SMEM((total,), jnp.int32),
            VMEM((tokens, seqs, feats), BF16),
            VMEM((1, feats), F32),
            VMEM((1, feats), F32),
            VMEM((2 * factor, feats), BF16),
            VMEM((1, total), jnp.int32),
            SMEM((total,), jnp.int32),
            VMEM((1, total), jnp.int32),
            VMEM((4, 1, width), F32),
            pltpu.SemaphoreType.DMA((16,)),
        ],
        name="prepare",
    )(
        row,
        alignment_depth,
        homolog_embedding.transpose(1, 0, 2),
        homolog_layer_scale.reshape(1, feats),
        homolog_layer_shift.reshape(1, feats),
        outer_source_matrix.T,
        outer_target_matrix.T,
        alignment_depth.reshape(1, total),
        chain_labels,
        chain_labels.reshape(1, total),
        chain_match.reshape(1, width),
        output_bias.reshape(1, width),
        pairwise_norm_gain.reshape(1, width),
        pairwise_norm_bias.reshape(1, width),
        input_projection_weight,
        input_gate_weight,
        output_weight,
    )

    y = pl.pallas_call(
        functools.partial(mix_kernel, factor),
        out_shape=jax.ShapeDtypeStruct((tokens // 2, inner, 2 * width), BF16),
        in_specs=[whole(VMEM)],
        out_specs=whole(VMEM),
        scratch_shapes=[VMEM((factor * factor, width), F32)],
        compiler_params=params(16),
        cost_estimate=pl.CostEstimate(
            flops=2 * tokens * seqs * factor * factor * width,
            bytes_accessed=2 * inner * tokens * width,
            transcendentals=0,
        ),
        name="mix",
    )(to_mix)

    def joined(*pieces):
        return pl.pallas_call(
            join_kernel,
            out_shape=jax.ShapeDtypeStruct((sum(x.shape[0] for x in pieces), part, 2 * seqs), BF16),
            in_specs=[whole(VMEM)] * len(pieces),
            out_specs=whole(VMEM),
            compiler_params=params(16),
            name="join",
        )(*pieces)

    chips = count // 2
    turn = [2 * k for k in range(chips - 1, 0, -1)]
    direct = [swap(item, k) for k in turn]
    early = swap(item, 1)
    *direct, y = lax.optimization_barrier((*direct, y))
    held = joined(*direct)
    late = swap(held, 1)
    wide, state, aux = pl.pallas_call(
        functools.partial(first_half_kernel, [turn, [0], [1]]),
        out_shape=(
            jax.ShapeDtypeStruct((count * part, 2 * seqs), F32),
            jax.ShapeDtypeStruct((tokens, total, width), BF16),
            jax.ShapeDtypeStruct((aux_rows, width), F32),
        ),
        in_specs=[whole(SMEM)] + [whole(VMEM)] * 5,
        out_specs=(whole(VMEM),) * 3,
        compiler_params=params(16),
        name="first_half",
    )(row, pairwise_state, aux, held, item, early)

    block = 2
    tile = tokens * tokens
    pair_next, same, cross, _ = pl.pallas_call(
        functools.partial(pair_kernel, [[k ^ 1 for k in turn]]),
        grid=(tokens // block,),
        out_shape=(
            jax.ShapeDtypeStruct((tokens, total, width), BF16),
            jax.ShapeDtypeStruct((chips, tile, width), BF16),
            jax.ShapeDtypeStruct((chips, tile, width), BF16),
            jax.ShapeDtypeStruct((count * part, 2 * seqs), F32),
        ),
        in_specs=[whole(SMEM), whole(VMEM), pl.BlockSpec((block, total, width), lambda g: (g, 0, 0))]
        + [whole(VMEM)] * 3,
        out_specs=(pl.BlockSpec((block, total, width), lambda g: (g, 0, 0)),) + (whole(VMEM),) * 3,
        scratch_shapes=[VMEM((total, inner), BF16), VMEM((count, tile, width), F32)],
        input_output_aliases={4: 3},
        compiler_params=params(16),
        cost_estimate=pl.CostEstimate(
            flops=2 * total * inner * tokens * width,
            bytes_accessed=2 * inner * tokens * width + 8 * tokens * total * width,
            transcendentals=0,
        ),
        name="pair",
    )(row, aux, state, y, wide, late)

    crossed = swap(cross, 1)
    tiles = pl.pallas_call(
        pack_kernel,
        out_shape=(jax.ShapeDtypeStruct((2, tile, width), BF16),) * chips,
        in_specs=[whole(SMEM), whole(VMEM), whole(VMEM)],
        out_specs=(whole(VMEM),) * chips,
        compiler_params=params(16),
        name="pack",
    )(row, same, crossed)
    moved = {k: swap(tiles[k], 2 * k) for k in range(chips - 1, 0, -1)}
    tiles = [tiles[0]] + [moved[k] for k in range(1, chips)]

    block = 4
    out = pl.pallas_call(
        gate_kernel,
        grid=(tokens // block,),
        out_shape=jax.ShapeDtypeStruct((tokens, total, gated), BF16),
        in_specs=[whole(SMEM)] + [whole(VMEM)] * (2 + chips),
        out_specs=pl.BlockSpec((block, total, gated), lambda j: (j, 0, 0)),
        scratch_shapes=[VMEM((count * tile, width), F32)],
        compiler_params=params(24),
        cost_estimate=pl.CostEstimate(
            flops=4 * tokens * total * width * gated,
            bytes_accessed=tokens * total * (2 * gated + 6 * width),
            transcendentals=tokens * total * gated,
        ),
        name="gate",
    )(row, aux, gates, *tiles)
    return pair_next, out.transpose(1, 0, 2)


def solution(mesh):
    return jax.shard_map(
        functools.partial(body, count=mesh.shape["row"]),
        mesh=mesh,
        in_specs=(
            P(("groups", "row"), None, None),
            P(None, ("groups", "row"), None),
            P("groups"),
            P("groups"),
        )
        + (P(),) * 11,
        out_specs=(P(("groups", "row"), None, None), P("groups", "row", None)),
        check_vma=False,
    )
```

```python
import functools

import jax
import jax.numpy as jnp
from jax import lax
from jax.experimental import pallas as pl
from jax.experimental.pallas import tpu as pltpu
from jax.sharding import PartitionSpec as P

F32 = jnp.float32
BF16 = jnp.bfloat16
NT = (((1,), (1,)), ((), ()))
VMEM = pltpu.VMEM
SMEM = pltpu.SMEM
HBM = pltpu.HBM
LANES = 128


def whole(space):
    return pl.BlockSpec(memory_space=space)


def params(mib):
    return pltpu.CompilerParams(vmem_limit_bytes=mib * 1024 * 1024)


def fetch(sems, *pairs):
    copies = [pltpu.make_async_copy(a, b, sems.at[n]) for n, (a, b) in enumerate(pairs)]
    for copy in copies:
        copy.start()
    return copies


def finish(copies):
    for copy in copies:
        copy.wait()


def prepare_kernel(
    row_ref, depth_hbm, hom_hbm, scale_hbm, shift_hbm, src_hbm, tgt_hbm, depth_row_hbm, chain_hbm, chain_row_hbm,
    match_hbm, bias_hbm, gain_hbm, move_hbm, proj_hbm, gate_hbm, weight_hbm,
    mix_ref, item_ref, aux_ref, gates_ref,
    depth_ref, hom_ref, scale_ref, shift_ref, both_ref, depth_row_ref, chain_ref, chain_row_ref, vec_ref, sems,
):
    tokens, seqs, feats = hom_ref.shape
    pair_width = aux_ref.shape[1]
    total = depth_ref.shape[0]
    width = src_hbm.shape[0]
    half = width // 2
    gated = proj_hbm.shape[1]
    first_copies = fetch(
        sems,
        (hom_hbm, hom_ref),
        (depth_hbm, depth_ref),
        (scale_hbm, scale_ref),
        (shift_hbm, shift_ref),
        (src_hbm, both_ref.at[0:width]),
        (tgt_hbm, both_ref.at[width : 2 * width]),
        (chain_hbm, chain_ref),
        (depth_row_hbm, depth_row_ref),
        (chain_row_hbm, chain_row_ref),
        (match_hbm, vec_ref.at[0]),
        (bias_hbm, vec_ref.at[1]),
        (gain_hbm, vec_ref.at[2]),
        (move_hbm, vec_ref.at[3]),
        (proj_hbm, gates_ref.at[0]),
        (gate_hbm, gates_ref.at[1]),
        (weight_hbm, mix_ref.at[tokens * seqs : tokens * seqs + width * width]),
    )
    finish(first_copies[:6])
    values = hom_ref[...].reshape(tokens * seqs, feats)
    ones = jnp.full((feats, feats), 1.0 / feats, BF16)
    centre = values.astype(F32) - jnp.dot(values, ones, preferred_element_type=F32)
    square = centre * centre
    high = square.astype(BF16)
    low = (square - high.astype(F32)).astype(BF16)
    spread = jnp.dot(high, ones, preferred_element_type=F32) + jnp.dot(
        low, ones, preferred_element_type=F32
    )
    normed = (centre * lax.rsqrt(spread + 1e-05) * scale_ref[...] + shift_ref[...]).astype(BF16)
    turned = lax.dot_general(both_ref[width : 2 * width], normed, NT, preferred_element_type=F32)
    plain = lax.dot_general(normed, both_ref[0:width], NT, preferred_element_type=F32)
    first = row_ref[0] * tokens
    row_pos = lax.broadcasted_iota(jnp.int32, (seqs, width), 0)
    lane = lax.broadcasted_iota(jnp.int32, (half, 2 * seqs), 1)
    seq_pos = jnp.where(lane < seqs, lane, lane - seqs)
    for n in range(tokens):
        depth = depth_ref[first + n]
        rows = slice(n * seqs, (n + 1) * seqs)
        mix_ref[rows, 0:width] = jnp.where(row_pos < depth, plain[rows], 0.0).astype(BF16)
        joint = jnp.concatenate([turned[0:half, rows], turned[half:width, rows]], axis=1)
        item_ref[0, n * half : (n + 1) * half] = jnp.where(seq_pos < depth, joint, 0.0).astype(BF16)

    finish(first_copies[6:])
    same = lax.broadcasted_iota(jnp.int32, (total, total), 0) == lax.broadcasted_iota(
        jnp.int32, (total, total), 1
    )
    fill = jnp.ones((total, pair_width), BF16)

    def column(ref):
        diagonal = jnp.where(same, ref[...].astype(F32), 0.0).astype(BF16)
        return jnp.dot(diagonal, fill, preferred_element_type=F32)

    aux_ref[0:total] = 1.0 / jnp.maximum(column(depth_row_ref), 1.0)
    aux_ref[total : 2 * total] = column(chain_row_ref)
    for n in range(tokens):
        own = jnp.full((1, pair_width), depth_ref[first + n], jnp.int32).astype(F32)
        aux_ref[2 * total + n : 2 * total + n + 1] = 1.0 / jnp.maximum(own, 1.0)
        label = jnp.full((1, pair_width), chain_ref[first + n], jnp.int32).astype(F32)
        aux_ref[2 * total + 16 + n : 2 * total + 17 + n] = label
    for n in range(4):
        aux_ref[2 * total + 32 + n : 2 * total + 33 + n] = vec_ref[n]


def mix_kernel(factor, mix_ref, out_ref, wide_ref):
    half = factor // 2
    seqs = out_ref.shape[1] // factor
    width = mix_ref.shape[1]
    lefts = mix_ref.shape[0] - factor * factor
    tokens = lefts // seqs
    wide_ref[...] = mix_ref[lefts : lefts + factor * factor].astype(F32)

    def one(q, carry):
        pair = [wide_ref[pl.ds(q + t * half, factor, stride=factor), :] for t in (0, 1)]
        rhs = jnp.concatenate(pair, axis=1).astype(BF16)
        mixed = jnp.dot(mix_ref[0:lefts, 0:factor], rhs, preferred_element_type=F32).astype(BF16)
        for n in range(tokens):
            rows = slice(n * seqs, (n + 1) * seqs)
            cols = slice(n % 2 * width, (n % 2 + 1) * width)
            for t in (0, 1):
                spot = pl.ds(pl.multiple_of((2 * q + t) * seqs, seqs), seqs)
                out_ref[n // 2, spot, cols] = mixed[rows, t * width : (t + 1) * width]
        return carry

    lax.fori_loop(0, half, one, 0, unroll=4)


def join_kernel(*refs):
    spot = 0
    for piece in refs[:-1]:
        refs[-1][spot : spot + piece.shape[0]] = piece[...]
        spot += piece.shape[0]


def spread_items(row, wide_ref, pieces, orders):
    for piece, ks in zip(pieces, orders):
        size = piece.shape[1]
        for m, k in enumerate(ks):
            spot = pl.ds(pl.multiple_of((row ^ k) * size, size), size)
            wide_ref[spot, :] = piece[m].astype(F32)


def first_half_kernel(orders, row_ref, state_ref, aux_ref, *rest):
    pieces, (wide_ref, state_out, aux_out) = rest[:-3], rest[-3:]
    state_out[...] = state_ref[...]
    aux_out[...] = aux_ref[...]
    spread_items(row_ref[0], wide_ref, pieces, orders)


def pair_kernel(orders, row_ref, aux_ref, state_ref, y_ref, wide_in, *rest):
    pieces, (next_ref, same_ref, cross_ref, wide_ref, lhs_ref) = rest[:-5], rest[-5:]
    step = pl.program_id(0)
    block, total, width = state_ref.shape
    lanes = pieces[0].shape[2]
    count = 2 * same_ref.shape[0]
    tokens = total // count
    groups = wide_ref.shape[0] // total

    @pl.when(step == 0)
    def _():
        spread_items(row_ref[0], wide_ref, pieces, orders)

        def one(q, carry):
            cols = pl.ds(pl.multiple_of(q * lanes, lanes), lanes)
            lhs_ref[:, cols] = wide_ref[pl.ds(q, total, stride=groups), :].astype(BF16)
            return carry

        lax.fori_loop(0, groups, one, 0, unroll=4)

    base = 2 * total
    match = aux_ref[base + 32 : base + 33]
    bias = aux_ref[base + 33 : base + 34]
    done = []
    for t in range(block):
        if t % 2 == 0:
            prod = jnp.dot(lhs_ref[...], y_ref[step * (block // 2) + t // 2], preferred_element_type=F32)
        own = step * block + t
        inv_own = aux_ref[pl.ds(base + own, 1)]
        label = aux_ref[pl.ds(base + 16 + own, 1)]
        extra = jnp.where(aux_ref[total:base] == label, match, 0.0) + bias
        value = prod[:, t % 2 * width : (t % 2 + 1) * width] * jnp.maximum(aux_ref[0:total], inv_own) + extra
        value = state_ref[t].astype(F32) + value
        next_ref[t] = value.astype(BF16)
        done.append(value)
    size = block * tokens
    spot = pl.ds(pl.multiple_of(step * size, size), size)
    for core in (0, 1):

        @pl.when((row_ref[0] & 1) == core)
        def _():
            for d in range(count):
                rows = slice(d * tokens, (d + 1) * tokens)
                tile = jnp.concatenate([value[rows] for value in done], axis=0).astype(BF16)
                (same_ref if (d & 1) == core else cross_ref)[d // 2, spot, :] = tile


def pack_kernel(row_ref, same_ref, crossed_ref, *outs):
    chip = row_ref[0] >> 1
    for core in (0, 1):

        @pl.when((row_ref[0] & 1) == core)
        def _():
            for k, out_ref in enumerate(outs):
                out_ref[core] = same_ref[chip ^ k]
                out_ref[1 - core] = crossed_ref[chip ^ k]


def gate_kernel(row_ref, aux_ref, gates_ref, *rest):
    tiles, (out_ref, wide_ref) = rest[:-2], rest[-2:]
    step = pl.program_id(0)
    block, total = out_ref.shape[:2]
    rows, width = tiles[0].shape[1:]
    tokens = total // (2 * len(tiles))

    @pl.when(step == 0)
    def _():
        chip = row_ref[0] >> 1
        for k, tile in enumerate(tiles):
            for core in (0, 1):
                spot = pl.ds(pl.multiple_of(((chip ^ k) * 2 + core) * rows, rows), rows)
                wide_ref[spot, :] = tile[core].astype(F32)

    gain = aux_ref[2 * total + 34 : 2 * total + 35]
    shift = aux_ref[2 * total + 35 : 2 * total + 36]
    ones = jnp.full((width, width), 1.0 / width, BF16)
    none = jnp.zeros((width, width), BF16)
    means = jnp.concatenate(
        [jnp.concatenate([ones, none], axis=1), jnp.concatenate([none, ones], axis=1)], axis=0
    )
    weights = jnp.concatenate([gates_ref[0], gates_ref[1]], axis=1)
    gated = gates_ref.shape[2]
    pair = jnp.concatenate(
        [
            jnp.concatenate(
                [wide_ref[pl.ds(step * block + t + u, total, stride=tokens), :] for u in (0, 1)], axis=1
            )
            for t in range(0, block, 2)
        ],
        axis=0,
    )
    centre = pair - jnp.dot(pair.astype(BF16), means, preferred_element_type=F32)
    square = (centre * centre).astype(BF16)
    spread = jnp.dot(square, means, preferred_element_type=F32)
    scaled = centre * lax.rsqrt(spread + 1e-05)
    scaled = jnp.concatenate([scaled[:, 0:width], scaled[:, width : 2 * width]], axis=0)
    normed = (scaled * gain + shift).astype(BF16)
    mixed = jnp.dot(normed, weights, preferred_element_type=F32)
    result = (mixed[:, 0:gated] * (0.5 + 0.5 * jnp.tanh(0.5 * mixed[:, gated : 2 * gated]))).astype(BF16)
    for t in range(block):
        first = (t % 2 * (block // 2) + t // 2) * total
        out_ref[t] = result[first : first + total]


def fixed(*shape):
    return pl.BlockSpec(shape, lambda g: (0,) * len(shape))


def body(
    pairwise_state,
    homolog_embedding,
    alignment_depth,
    chain_labels,
    homolog_layer_scale,
    homolog_layer_shift,
    outer_source_matrix,
    outer_target_matrix,
    output_weight,
    output_bias,
    chain_match,
    pairwise_norm_gain,
    pairwise_norm_bias,
    input_projection_weight,
    input_gate_weight,
    *,
    count,
):
    tokens, total, width = pairwise_state.shape
    seqs, _, feats = homolog_embedding.shape
    factor = outer_source_matrix.shape[1]
    half = factor // 2
    inner = factor * seqs
    gated = input_projection_weight.shape[1]
    row = lax.axis_index("row").astype(jnp.int32).reshape(1)

    def swap(array, bit):
        return lax.ppermute(array, "row", [(r, r ^ bit) for r in range(count)])

    aux_rows = 2 * total + 40
    part = tokens * half
    mix_rows = tokens * seqs + factor * factor
    to_mix, item, aux, gates = pl.pallas_call(
        prepare_kernel,
        out_shape=(
            jax.ShapeDtypeStruct((mix_rows, width), BF16),
            jax.ShapeDtypeStruct((1, part, 2 * seqs), BF16),
            jax.ShapeDtypeStruct((aux_rows, width), F32),
            jax.ShapeDtypeStruct((2, width, gated), BF16),
        ),
        in_specs=[whole(SMEM)] + [whole(HBM)] * 16,
        out_specs=(whole(VMEM),) * 4,
        scratch_shapes=[
            SMEM((total,), jnp.int32),
            VMEM((tokens, seqs, feats), BF16),
            VMEM((1, feats), F32),
            VMEM((1, feats), F32),
            VMEM((2 * factor, feats), BF16),
            VMEM((1, total), jnp.int32),
            SMEM((total,), jnp.int32),
            VMEM((1, total), jnp.int32),
            VMEM((4, 1, width), F32),
            pltpu.SemaphoreType.DMA((16,)),
        ],
        name="prepare",
    )(
        row,
        alignment_depth,
        homolog_embedding.transpose(1, 0, 2),
        homolog_layer_scale.reshape(1, feats),
        homolog_layer_shift.reshape(1, feats),
        outer_source_matrix.T,
        outer_target_matrix.T,
        alignment_depth.reshape(1, total),
        chain_labels,
        chain_labels.reshape(1, total),
        chain_match.reshape(1, width),
        output_bias.reshape(1, width),
        pairwise_norm_gain.reshape(1, width),
        pairwise_norm_bias.reshape(1, width),
        input_projection_weight,
        input_gate_weight,
        output_weight,
    )

    y = pl.pallas_call(
        functools.partial(mix_kernel, factor),
        out_shape=jax.ShapeDtypeStruct((tokens // 2, inner, 2 * width), BF16),
        in_specs=[whole(VMEM)],
        out_specs=whole(VMEM),
        scratch_shapes=[VMEM((factor * factor, width), F32)],
        compiler_params=params(16),
        cost_estimate=pl.CostEstimate(
            flops=2 * tokens * seqs * factor * factor * width,
            bytes_accessed=2 * inner * tokens * width,
            transcendentals=0,
        ),
        name="mix",
    )(to_mix)

    def joined(*pieces):
        return pl.pallas_call(
            join_kernel,
            out_shape=jax.ShapeDtypeStruct((sum(x.shape[0] for x in pieces), part, 2 * seqs), BF16),
            in_specs=[whole(VMEM)] * len(pieces),
            out_specs=whole(VMEM),
            compiler_params=params(16),
            name="join",
        )(*pieces)

    chips = count // 2
    turn = [4 * k for k in range(count // 4 - 1, 0, -1)]
    direct = [swap(item, k) for k in turn]
    held = joined(item, *direct)
    turn = [0] + turn
    came = swap(held, 2)
    early = swap(held, 1)
    came, y = lax.optimization_barrier((came, y))
    late = swap(came, 1)
    wide, state, aux = pl.pallas_call(
        functools.partial(first_half_kernel, [turn, [k ^ 1 for k in turn], [k ^ 2 for k in turn]]),
        out_shape=(
            jax.ShapeDtypeStruct((count * part, 2 * seqs), F32),
            jax.ShapeDtypeStruct((tokens, total, width), BF16),
            jax.ShapeDtypeStruct((aux_rows, width), F32),
        ),
        in_specs=[whole(SMEM)] + [whole(VMEM)] * 5,
        out_specs=(whole(VMEM),) * 3,
        compiler_params=params(16),
        name="first_half",
    )(row, pairwise_state, aux, held, early, came)

    block = 4
    tile = tokens * tokens
    pair_next, same, cross, _ = pl.pallas_call(
        functools.partial(pair_kernel, [[k ^ 3 for k in turn]]),
        grid=(tokens // block,),
        out_shape=(
            jax.ShapeDtypeStruct((tokens, total, width), BF16),
            jax.ShapeDtypeStruct((chips, tile, width), BF16),
            jax.ShapeDtypeStruct((chips, tile, width), BF16),
            jax.ShapeDtypeStruct((count * part, 2 * seqs), F32),
        ),
        in_specs=[whole(SMEM), whole(VMEM), pl.BlockSpec((block, total, width), lambda g: (g, 0, 0))]
        + [whole(VMEM)] * 3,
        out_specs=(pl.BlockSpec((block, total, width), lambda g: (g, 0, 0)),) + (whole(VMEM),) * 3,
        scratch_shapes=[VMEM((total, inner), BF16)],
        input_output_aliases={4: 3},
        compiler_params=params(16),
        cost_estimate=pl.CostEstimate(
            flops=2 * total * inner * tokens * width,
            bytes_accessed=2 * inner * tokens * width + 8 * tokens * total * width,
            transcendentals=0,
        ),
        name="pair",
    )(row, aux, state, y, wide, late)

    crossed = swap(cross, 1)
    tiles = pl.pallas_call(
        pack_kernel,
        out_shape=(jax.ShapeDtypeStruct((2, tile, width), BF16),) * chips,
        in_specs=[whole(SMEM), whole(VMEM), whole(VMEM)],
        out_specs=(whole(VMEM),) * chips,
        compiler_params=params(16),
        name="pack",
    )(row, same, crossed)
    moved = {k: swap(tiles[k], 2 * k) for k in range(chips - 1, 0, -1)}
    tiles = [tiles[0]] + [moved[k] for k in range(1, chips)]

    block = 4
    out = pl.pallas_call(
        gate_kernel,
        grid=(tokens // block,),
        out_shape=jax.ShapeDtypeStruct((tokens, total, gated), BF16),
        in_specs=[whole(SMEM)] + [whole(VMEM)] * (2 + chips),
        out_specs=pl.BlockSpec((block, total, gated), lambda j: (j, 0, 0)),
        scratch_shapes=[VMEM((count * tile, width), F32)],
        compiler_params=params(24),
        cost_estimate=pl.CostEstimate(
            flops=4 * tokens * total * width * gated,
            bytes_accessed=tokens * total * (2 * gated + 6 * width),
            transcendentals=tokens * total * gated,
        ),
        name="gate",
    )(row, aux, gates, *tiles)
    return pair_next, out.transpose(1, 0, 2)


def solution(mesh):
    return jax.shard_map(
        functools.partial(body, count=mesh.shape["row"]),
        mesh=mesh,
        in_specs=(
            P(("groups", "row"), None, None),
            P(None, ("groups", "row"), None),
            P("groups"),
            P("groups"),
        )
        + (P(),) * 11,
        out_specs=(P(("groups", "row"), None, None), P("groups", "row", None)),
        check_vma=False,
    )
```

```python
import functools

import jax
import jax.numpy as jnp
from jax import lax
from jax.experimental import pallas as pl
from jax.experimental.pallas import tpu as pltpu
from jax.sharding import PartitionSpec as P

F32 = jnp.float32
BF16 = jnp.bfloat16
NT = (((1,), (1,)), ((), ()))
VMEM = pltpu.VMEM
SMEM = pltpu.SMEM
HBM = pltpu.HBM
LANES = 128


def whole(space):
    return pl.BlockSpec(memory_space=space)


def params(mib):
    return pltpu.CompilerParams(vmem_limit_bytes=mib * 1024 * 1024)


def fetch(sems, *pairs):
    copies = [pltpu.make_async_copy(a, b, sems.at[n]) for n, (a, b) in enumerate(pairs)]
    for copy in copies:
        copy.start()
    return copies


def finish(copies):
    for copy in copies:
        copy.wait()


def prepare_kernel(
    row_ref, depth_hbm, hom_hbm, scale_hbm, shift_hbm, src_hbm, tgt_hbm, depth_row_hbm, chain_hbm, chain_row_hbm,
    match_hbm, bias_hbm, gain_hbm, move_hbm, proj_hbm, gate_hbm,
    left_ref, item_ref, aux_ref, gates_ref,
    depth_ref, hom_ref, scale_ref, shift_ref, both_ref, depth_row_ref, chain_ref, chain_row_ref, vec_ref, sems,
):
    tokens, seqs, feats = hom_ref.shape
    pair_width = aux_ref.shape[1]
    total = depth_ref.shape[0]
    width = src_hbm.shape[0]
    half = width // 2
    gated = proj_hbm.shape[1]
    first_copies = fetch(
        sems,
        (hom_hbm, hom_ref),
        (depth_hbm, depth_ref),
        (scale_hbm, scale_ref),
        (shift_hbm, shift_ref),
        (src_hbm, both_ref.at[0:width]),
        (tgt_hbm, both_ref.at[width : 2 * width]),
        (chain_hbm, chain_ref),
        (depth_row_hbm, depth_row_ref),
        (chain_row_hbm, chain_row_ref),
        (match_hbm, vec_ref.at[0]),
        (bias_hbm, vec_ref.at[1]),
        (gain_hbm, vec_ref.at[2]),
        (move_hbm, vec_ref.at[3]),
        (proj_hbm, gates_ref.at[0]),
        (gate_hbm, gates_ref.at[1]),
    )
    finish(first_copies[:6])
    values = hom_ref[...].reshape(tokens * seqs, feats)
    ones = jnp.full((feats, feats), 1.0 / feats, BF16)
    centre = values.astype(F32) - jnp.dot(values, ones, preferred_element_type=F32)
    square = centre * centre
    high = square.astype(BF16)
    low = (square - high.astype(F32)).astype(BF16)
    spread = jnp.dot(high, ones, preferred_element_type=F32) + jnp.dot(
        low, ones, preferred_element_type=F32
    )
    normed = (centre * lax.rsqrt(spread + 1e-05) * scale_ref[...] + shift_ref[...]).astype(BF16)
    turned = lax.dot_general(both_ref[width : 2 * width], normed, NT, preferred_element_type=F32)
    plain = lax.dot_general(normed, both_ref[0:width], NT, preferred_element_type=F32)
    first = row_ref[0] * tokens
    row_pos = lax.broadcasted_iota(jnp.int32, (seqs, width), 0)
    lane = lax.broadcasted_iota(jnp.int32, (half, 2 * seqs), 1)
    seq_pos = jnp.where(lane < seqs, lane, lane - seqs)
    for n in range(tokens):
        depth = depth_ref[first + n]
        rows = slice(n * seqs, (n + 1) * seqs)
        left_ref[rows] = jnp.where(row_pos < depth, plain[rows], 0.0).astype(BF16)
        joint = jnp.concatenate([turned[0:half, rows], turned[half:width, rows]], axis=1)
        item_ref[0, n * half : (n + 1) * half] = jnp.where(seq_pos < depth, joint, 0.0).astype(BF16)

    finish(first_copies[6:])
    same = lax.broadcasted_iota(jnp.int32, (total, total), 0) == lax.broadcasted_iota(
        jnp.int32, (total, total), 1
    )
    fill = jnp.ones((total, pair_width), BF16)

    def column(ref):
        diagonal = jnp.where(same, ref[...].astype(F32), 0.0).astype(BF16)
        return jnp.dot(diagonal, fill, preferred_element_type=F32)

    aux_ref[0:total] = 1.0 / jnp.maximum(column(depth_row_ref), 1.0)
    aux_ref[total : 2 * total] = column(chain_row_ref)
    for n in range(tokens):
        own = jnp.full((1, pair_width), depth_ref[first + n], jnp.int32).astype(F32)
        aux_ref[2 * total + n : 2 * total + n + 1] = 1.0 / jnp.maximum(own, 1.0)
        label = jnp.full((1, pair_width), chain_ref[first + n], jnp.int32).astype(F32)
        aux_ref[2 * total + 16 + n : 2 * total + 17 + n] = label
    for n in range(4):
        aux_ref[2 * total + 32 + n : 2 * total + 33 + n] = vec_ref[n]


def mix_kernel(left_ref, weight_ref, out_ref, wide_ref):
    factor = left_ref.shape[1]
    half = factor // 2
    seqs = out_ref.shape[1] // factor
    width = weight_ref.shape[1]
    tokens = left_ref.shape[0] // seqs
    wide_ref[...] = weight_ref[...].astype(F32)

    def one(q, carry):
        pair = [wide_ref[pl.ds(q + t * half, factor, stride=factor), :] for t in (0, 1)]
        rhs = jnp.concatenate(pair, axis=1).astype(BF16)
        mixed = jnp.dot(left_ref[...], rhs, preferred_element_type=F32).astype(BF16)
        for n in range(tokens):
            rows = slice(n * seqs, (n + 1) * seqs)
            cols = slice(n % 2 * width, (n % 2 + 1) * width)
            for t in (0, 1):
                spot = pl.ds(pl.multiple_of((2 * q + t) * seqs, seqs), seqs)
                out_ref[n // 2, spot, cols] = mixed[rows, t * width : (t + 1) * width]
        return carry

    lax.fori_loop(0, half, one, 0, unroll=4)


def join_kernel(*refs):
    spot = 0
    for piece in refs[:-1]:
        refs[-1][spot : spot + piece.shape[0]] = piece[...]
        spot += piece.shape[0]


def spread_items(row, wide_ref, pieces, orders):
    for piece, ks in zip(pieces, orders):
        size = piece.shape[1]
        for m, k in enumerate(ks):
            spot = pl.ds(pl.multiple_of((row ^ k) * size, size), size)
            wide_ref[spot, :] = piece[m].astype(F32)


def first_half_kernel(orders, row_ref, state_ref, aux_ref, *rest):
    pieces, (wide_ref, state_out, aux_out) = rest[:-3], rest[-3:]
    state_out[...] = state_ref[...]
    aux_out[...] = aux_ref[...]
    spread_items(row_ref[0], wide_ref, pieces, orders)


def pair_kernel(orders, row_ref, aux_ref, state_ref, y_ref, wide_in, *rest):
    pieces, (next_ref, same_ref, cross_ref, wide_ref, lhs_ref) = rest[:-5], rest[-5:]
    step = pl.program_id(0)
    block, total, width = state_ref.shape
    lanes = pieces[0].shape[2]
    count = 2 * same_ref.shape[0]
    tokens = total // count
    groups = wide_ref.shape[0] // total

    @pl.when(step == 0)
    def _():
        spread_items(row_ref[0], wide_ref, pieces, orders)

        def one(q, carry):
            cols = pl.ds(pl.multiple_of(q * lanes, lanes), lanes)
            lhs_ref[:, cols] = wide_ref[pl.ds(q, total, stride=groups), :].astype(BF16)
            return carry

        lax.fori_loop(0, groups, one, 0, unroll=4)

    base = 2 * total
    match = aux_ref[base + 32 : base + 33]
    bias = aux_ref[base + 33 : base + 34]
    done = []
    for t in range(block):
        if t % 2 == 0:
            prod = jnp.dot(lhs_ref[...], y_ref[step * (block // 2) + t // 2], preferred_element_type=F32)
        own = step * block + t
        inv_own = aux_ref[pl.ds(base + own, 1)]
        label = aux_ref[pl.ds(base + 16 + own, 1)]
        extra = jnp.where(aux_ref[total:base] == label, match, 0.0) + bias
        value = prod[:, t % 2 * width : (t % 2 + 1) * width] * jnp.maximum(aux_ref[0:total], inv_own) + extra
        value = state_ref[t].astype(F32) + value
        next_ref[t] = value.astype(BF16)
        done.append(value)
    size = block * tokens
    spot = pl.ds(pl.multiple_of(step * size, size), size)
    for core in (0, 1):

        @pl.when((row_ref[0] & 1) == core)
        def _():
            for d in range(count):
                rows = slice(d * tokens, (d + 1) * tokens)
                tile = jnp.concatenate([value[rows] for value in done], axis=0).astype(BF16)
                (same_ref if (d & 1) == core else cross_ref)[d // 2, spot, :] = tile


def pack_kernel(row_ref, same_ref, crossed_ref, *outs):
    chip = row_ref[0] >> 1
    for core in (0, 1):

        @pl.when((row_ref[0] & 1) == core)
        def _():
            for k, out_ref in enumerate(outs):
                out_ref[core] = same_ref[chip ^ k]
                out_ref[1 - core] = crossed_ref[chip ^ k]


def gate_kernel(row_ref, aux_ref, gates_ref, *rest):
    tiles, (out_ref, wide_ref) = rest[:-2], rest[-2:]
    step = pl.program_id(0)
    block, total = out_ref.shape[:2]
    rows, width = tiles[0].shape[1:]
    tokens = total // (2 * len(tiles))

    @pl.when(step == 0)
    def _():
        chip = row_ref[0] >> 1
        for k, tile in enumerate(tiles):
            for core in (0, 1):
                spot = pl.ds(pl.multiple_of(((chip ^ k) * 2 + core) * rows, rows), rows)
                wide_ref[spot, :] = tile[core].astype(F32)

    gain = aux_ref[2 * total + 34 : 2 * total + 35]
    shift = aux_ref[2 * total + 35 : 2 * total + 36]
    ones = jnp.full((width, width), 1.0 / width, BF16)
    none = jnp.zeros((width, width), BF16)
    means = jnp.concatenate(
        [jnp.concatenate([ones, none], axis=1), jnp.concatenate([none, ones], axis=1)], axis=0
    )
    weights = jnp.concatenate([gates_ref[0], gates_ref[1]], axis=1)
    gated = gates_ref.shape[2]
    pair = jnp.concatenate(
        [
            jnp.concatenate(
                [wide_ref[pl.ds(step * block + t + u, total, stride=tokens), :] for u in (0, 1)], axis=1
            )
            for t in range(0, block, 2)
        ],
        axis=0,
    )
    centre = pair - jnp.dot(pair.astype(BF16), means, preferred_element_type=F32)
    square = (centre * centre).astype(BF16)
    spread = jnp.dot(square, means, preferred_element_type=F32)
    scaled = centre * lax.rsqrt(spread + 1e-05)
    scaled = jnp.concatenate([scaled[:, 0:width], scaled[:, width : 2 * width]], axis=0)
    normed = (scaled * gain + shift).astype(BF16)
    mixed = jnp.dot(normed, weights, preferred_element_type=F32)
    result = (mixed[:, 0:gated] * (0.5 + 0.5 * jnp.tanh(0.5 * mixed[:, gated : 2 * gated]))).astype(BF16)
    for t in range(block):
        first = (t % 2 * (block // 2) + t // 2) * total
        out_ref[t] = result[first : first + total]


def fixed(*shape):
    return pl.BlockSpec(shape, lambda g: (0,) * len(shape))


def body(
    pairwise_state,
    homolog_embedding,
    alignment_depth,
    chain_labels,
    homolog_layer_scale,
    homolog_layer_shift,
    outer_source_matrix,
    outer_target_matrix,
    output_weight,
    output_bias,
    chain_match,
    pairwise_norm_gain,
    pairwise_norm_bias,
    input_projection_weight,
    input_gate_weight,
    *,
    count,
):
    tokens, total, width = pairwise_state.shape
    seqs, _, feats = homolog_embedding.shape
    factor = outer_source_matrix.shape[1]
    half = factor // 2
    inner = factor * seqs
    gated = input_projection_weight.shape[1]
    row = lax.axis_index("row").astype(jnp.int32).reshape(1)

    def swap(array, bit):
        return lax.ppermute(array, "row", [(r, r ^ bit) for r in range(count)])

    aux_rows = 2 * total + 40
    part = tokens * half
    left, item, aux, gates = pl.pallas_call(
        prepare_kernel,
        out_shape=(
            jax.ShapeDtypeStruct((tokens * seqs, factor), BF16),
            jax.ShapeDtypeStruct((1, part, 2 * seqs), BF16),
            jax.ShapeDtypeStruct((aux_rows, width), F32),
            jax.ShapeDtypeStruct((2, width, gated), BF16),
        ),
        in_specs=[whole(SMEM)] + [whole(HBM)] * 15,
        out_specs=(whole(VMEM),) * 4,
        scratch_shapes=[
            SMEM((total,), jnp.int32),
            VMEM((tokens, seqs, feats), BF16),
            VMEM((1, feats), F32),
            VMEM((1, feats), F32),
            VMEM((2 * factor, feats), BF16),
            VMEM((1, total), jnp.int32),
            SMEM((total,), jnp.int32),
            VMEM((1, total), jnp.int32),
            VMEM((4, 1, width), F32),
            pltpu.SemaphoreType.DMA((15,)),
        ],
        name="prepare",
    )(
        row,
        alignment_depth,
        homolog_embedding.transpose(1, 0, 2),
        homolog_layer_scale.reshape(1, feats),
        homolog_layer_shift.reshape(1, feats),
        outer_source_matrix.T,
        outer_target_matrix.T,
        alignment_depth.reshape(1, total),
        chain_labels,
        chain_labels.reshape(1, total),
        chain_match.reshape(1, width),
        output_bias.reshape(1, width),
        pairwise_norm_gain.reshape(1, width),
        pairwise_norm_bias.reshape(1, width),
        input_projection_weight,
        input_gate_weight,
    )

    y = pl.pallas_call(
        mix_kernel,
        out_shape=jax.ShapeDtypeStruct((tokens // 2, inner, 2 * width), BF16),
        in_specs=[whole(VMEM)] * 2,
        out_specs=whole(VMEM),
        scratch_shapes=[VMEM((factor * factor, width), F32)],
        compiler_params=params(16),
        cost_estimate=pl.CostEstimate(
            flops=2 * tokens * seqs * factor * factor * width,
            bytes_accessed=2 * inner * tokens * width,
            transcendentals=0,
        ),
        name="mix",
    )(left, output_weight)

    def joined(*pieces):
        return pl.pallas_call(
            join_kernel,
            out_shape=jax.ShapeDtypeStruct((sum(x.shape[0] for x in pieces), part, 2 * seqs), BF16),
            in_specs=[whole(VMEM)] * len(pieces),
            out_specs=whole(VMEM),
            compiler_params=params(16),
            name="join",
        )(*pieces)

    chips = count // 2
    turn = [4 * k for k in range(count // 4 - 1, 0, -1)]
    direct = [swap(item, k) for k in turn]
    own_came = swap(item, 2)
    own_early = swap(item, 1)
    *direct, own_came, own_early = lax.optimization_barrier((*direct, own_came, own_early))
    held = joined(*direct)
    came = swap(held, 2)
    early = swap(held, 1)
    came, y = lax.optimization_barrier((came, y))
    own_late = swap(own_came, 1)
    late = swap(came, 1)
    wide, state, aux = pl.pallas_call(
        functools.partial(
            first_half_kernel, [[0], [1], [2], turn, [k ^ 1 for k in turn], [k ^ 2 for k in turn]]
        ),
        out_shape=(
            jax.ShapeDtypeStruct((count * part, 2 * seqs), F32),
            jax.ShapeDtypeStruct((tokens, total, width), BF16),
            jax.ShapeDtypeStruct((aux_rows, width), F32),
        ),
        in_specs=[whole(SMEM)] + [whole(VMEM)] * 8,
        out_specs=(whole(VMEM),) * 3,
        compiler_params=params(16),
        name="first_half",
    )(row, pairwise_state, aux, item, own_early, own_came, held, early, came)

    block = 4
    tile = tokens * tokens
    pair_next, same, cross, _ = pl.pallas_call(
        functools.partial(pair_kernel, [[3], [k ^ 3 for k in turn]]),
        grid=(tokens // block,),
        out_shape=(
            jax.ShapeDtypeStruct((tokens, total, width), BF16),
            jax.ShapeDtypeStruct((chips, tile, width), BF16),
            jax.ShapeDtypeStruct((chips, tile, width), BF16),
            jax.ShapeDtypeStruct((count * part, 2 * seqs), F32),
        ),
        in_specs=[whole(SMEM), whole(VMEM), pl.BlockSpec((block, total, width), lambda g: (g, 0, 0))]
        + [whole(VMEM)] * 4,
        out_specs=(pl.BlockSpec((block, total, width), lambda g: (g, 0, 0)),) + (whole(VMEM),) * 3,
        scratch_shapes=[VMEM((total, inner), BF16)],
        input_output_aliases={4: 3},
        compiler_params=params(16),
        cost_estimate=pl.CostEstimate(
            flops=2 * total * inner * tokens * width,
            bytes_accessed=2 * inner * tokens * width + 8 * tokens * total * width,
            transcendentals=0,
        ),
        name="pair",
    )(row, aux, state, y, wide, own_late, late)

    crossed = swap(cross, 1)
    tiles = pl.pallas_call(
        pack_kernel,
        out_shape=(jax.ShapeDtypeStruct((2, tile, width), BF16),) * chips,
        in_specs=[whole(SMEM), whole(VMEM), whole(VMEM)],
        out_specs=(whole(VMEM),) * chips,
        compiler_params=params(16),
        name="pack",
    )(row, same, crossed)
    moved = {k: swap(tiles[k], 2 * k) for k in range(chips - 1, 0, -1)}
    tiles = [tiles[0]] + [moved[k] for k in range(1, chips)]

    block = 4
    out = pl.pallas_call(
        gate_kernel,
        grid=(tokens // block,),
        out_shape=jax.ShapeDtypeStruct((tokens, total, gated), BF16),
        in_specs=[whole(SMEM)] + [whole(VMEM)] * (2 + chips),
        out_specs=pl.BlockSpec((block, total, gated), lambda j: (j, 0, 0)),
        scratch_shapes=[VMEM((count * tile, width), F32)],
        compiler_params=params(24),
        cost_estimate=pl.CostEstimate(
            flops=4 * tokens * total * width * gated,
            bytes_accessed=tokens * total * (2 * gated + 6 * width),
            transcendentals=tokens * total * gated,
        ),
        name="gate",
    )(row, aux, gates, *tiles)
    return pair_next, out.transpose(1, 0, 2)


def solution(mesh):
    return jax.shard_map(
        functools.partial(body, count=mesh.shape["row"]),
        mesh=mesh,
        in_specs=(
            P(("groups", "row"), None, None),
            P(None, ("groups", "row"), None),
            P("groups"),
            P("groups"),
        )
        + (P(),) * 11,
        out_specs=(P(("groups", "row"), None, None), P("groups", "row", None)),
        check_vma=False,
    )
```

```python
import functools

import jax
import jax.numpy as jnp
from jax import lax
from jax.experimental import pallas as pl
from jax.experimental.pallas import tpu as pltpu
from jax.sharding import PartitionSpec as P

F32 = jnp.float32
BF16 = jnp.bfloat16
NT = (((1,), (1,)), ((), ()))
VMEM = pltpu.VMEM
SMEM = pltpu.SMEM
HBM = pltpu.HBM
LANES = 128


def whole(space):
    return pl.BlockSpec(memory_space=space)


def params(mib):
    return pltpu.CompilerParams(vmem_limit_bytes=mib * 1024 * 1024)


def fetch(sems, *pairs):
    copies = [pltpu.make_async_copy(a, b, sems.at[n]) for n, (a, b) in enumerate(pairs)]
    for copy in copies:
        copy.start()
    return copies


def finish(copies):
    for copy in copies:
        copy.wait()


def prepare_kernel(
    row_ref, depth_hbm, hom_hbm, scale_hbm, shift_hbm, src_hbm, tgt_hbm, depth_row_hbm, chain_hbm, chain_row_hbm,
    match_hbm, bias_hbm, gain_hbm, move_hbm, proj_hbm, gate_hbm, weight_hbm,
    mix_ref, item_ref, aux_ref, gates_ref,
    depth_ref, hom_ref, scale_ref, shift_ref, both_ref, depth_row_ref, chain_ref, chain_row_ref, vec_ref, sems,
):
    tokens, seqs, feats = hom_ref.shape
    pair_width = aux_ref.shape[1]
    total = depth_ref.shape[0]
    width = src_hbm.shape[0]
    half = width // 2
    gated = proj_hbm.shape[1]
    first_copies = fetch(
        sems,
        (hom_hbm, hom_ref),
        (depth_hbm, depth_ref),
        (scale_hbm, scale_ref),
        (shift_hbm, shift_ref),
        (src_hbm, both_ref.at[0:width]),
        (tgt_hbm, both_ref.at[width : 2 * width]),
        (chain_hbm, chain_ref),
        (depth_row_hbm, depth_row_ref),
        (chain_row_hbm, chain_row_ref),
        (match_hbm, vec_ref.at[0]),
        (bias_hbm, vec_ref.at[1]),
        (gain_hbm, vec_ref.at[2]),
        (move_hbm, vec_ref.at[3]),
        (proj_hbm, gates_ref.at[0]),
        (gate_hbm, gates_ref.at[1]),
        (weight_hbm, mix_ref.at[tokens * seqs : tokens * seqs + width * width]),
    )
    finish(first_copies[:6])
    values = hom_ref[...].reshape(tokens * seqs, feats)
    ones = jnp.full((feats, feats), 1.0 / feats, BF16)
    centre = values.astype(F32) - jnp.dot(values, ones, preferred_element_type=F32)
    square = centre * centre
    high = square.astype(BF16)
    low = (square - high.astype(F32)).astype(BF16)
    spread = jnp.dot(high, ones, preferred_element_type=F32) + jnp.dot(
        low, ones, preferred_element_type=F32
    )
    normed = (centre * lax.rsqrt(spread + 1e-05) * scale_ref[...] + shift_ref[...]).astype(BF16)
    turned = lax.dot_general(both_ref[width : 2 * width], normed, NT, preferred_element_type=F32)
    plain = lax.dot_general(normed, both_ref[0:width], NT, preferred_element_type=F32)
    first = row_ref[0] * tokens
    row_pos = lax.broadcasted_iota(jnp.int32, (seqs, width), 0)
    lane = lax.broadcasted_iota(jnp.int32, (half, 2 * seqs), 1)
    seq_pos = jnp.where(lane < seqs, lane, lane - seqs)
    for n in range(tokens):
        depth = depth_ref[first + n]
        rows = slice(n * seqs, (n + 1) * seqs)
        mix_ref[rows, 0:width] = jnp.where(row_pos < depth, plain[rows], 0.0).astype(BF16)
        joint = jnp.concatenate([turned[0:half, rows], turned[half:width, rows]], axis=1)
        item_ref[0, n * half : (n + 1) * half] = jnp.where(seq_pos < depth, joint, 0.0).astype(BF16)

    finish(first_copies[6:])
    same = lax.broadcasted_iota(jnp.int32, (total, total), 0) == lax.broadcasted_iota(
        jnp.int32, (total, total), 1
    )
    fill = jnp.ones((total, pair_width), BF16)

    def column(ref):
        diagonal = jnp.where(same, ref[...].astype(F32), 0.0).astype(BF16)
        return jnp.dot(diagonal, fill, preferred_element_type=F32)

    aux_ref[0:total] = 1.0 / jnp.maximum(column(depth_row_ref), 1.0)
    aux_ref[total : 2 * total] = column(chain_row_ref)
    for n in range(tokens):
        own = jnp.full((1, pair_width), depth_ref[first + n], jnp.int32).astype(F32)
        aux_ref[2 * total + n : 2 * total + n + 1] = 1.0 / jnp.maximum(own, 1.0)
        label = jnp.full((1, pair_width), chain_ref[first + n], jnp.int32).astype(F32)
        aux_ref[2 * total + 16 + n : 2 * total + 17 + n] = label
    for n in range(4):
        aux_ref[2 * total + 32 + n : 2 * total + 33 + n] = vec_ref[n]


def mix_kernel(factor, mix_ref, out_ref, wide_ref):
    half = factor // 2
    seqs = out_ref.shape[1] // factor
    width = mix_ref.shape[1]
    lefts = mix_ref.shape[0] - factor * factor
    tokens = lefts // seqs
    wide_ref[...] = mix_ref[lefts : lefts + factor * factor].astype(F32)

    def one(q, carry):
        pair = [wide_ref[pl.ds(q + t * half, factor, stride=factor), :] for t in (0, 1)]
        rhs = jnp.concatenate(pair, axis=1).astype(BF16)
        mixed = jnp.dot(mix_ref[0:lefts, 0:factor], rhs, preferred_element_type=F32).astype(BF16)
        for n in range(tokens):
            rows = slice(n * seqs, (n + 1) * seqs)
            cols = slice(n % 2 * width, (n % 2 + 1) * width)
            for t in (0, 1):
                spot = pl.ds(pl.multiple_of((2 * q + t) * seqs, seqs), seqs)
                out_ref[n // 2, spot, cols] = mixed[rows, t * width : (t + 1) * width]
        return carry

    lax.fori_loop(0, half, one, 0, unroll=4)


def join_kernel(*refs):
    spot = 0
    for piece in refs[:-1]:
        refs[-1][spot : spot + piece.shape[0]] = piece[...]
        spot += piece.shape[0]


def by_core(row, pair):
    return jnp.where((row & 1) == 1, pair[1], pair[0])


def spread_items(row, wide_ref, pieces, orders):
    for piece, pairs in zip(pieces, orders):
        size = piece.shape[1]
        for m, pair in enumerate(pairs):
            spot = pl.ds(pl.multiple_of((row ^ by_core(row, pair)) * size, size), size)
            wide_ref[spot, :] = piece[m].astype(F32)


def first_half_kernel(orders, row_ref, state_ref, aux_ref, *rest):
    pieces, (wide_ref, state_out, aux_out) = rest[:-3], rest[-3:]
    state_out[...] = state_ref[...]
    aux_out[...] = aux_ref[...]
    spread_items(row_ref[0], wide_ref, pieces, orders)


def pair_kernel(orders, row_ref, aux_ref, state_ref, y_ref, wide_in, *rest):
    pieces, (next_ref, same_ref, cross_ref, wide_ref, lhs_ref) = rest[:-5], rest[-5:]
    step = pl.program_id(0)
    block, total, width = state_ref.shape
    lanes = pieces[0].shape[2]
    count = 2 * same_ref.shape[0]
    tokens = total // count
    groups = wide_ref.shape[0] // total

    @pl.when(step == 0)
    def _():
        spread_items(row_ref[0], wide_ref, pieces, orders)

        def one(q, carry):
            cols = pl.ds(pl.multiple_of(q * lanes, lanes), lanes)
            lhs_ref[:, cols] = wide_ref[pl.ds(q, total, stride=groups), :].astype(BF16)
            return carry

        lax.fori_loop(0, groups, one, 0, unroll=4)

    base = 2 * total
    match = aux_ref[base + 32 : base + 33]
    bias = aux_ref[base + 33 : base + 34]
    done = []
    for t in range(block):
        if t % 2 == 0:
            prod = jnp.dot(lhs_ref[...], y_ref[step * (block // 2) + t // 2], preferred_element_type=F32)
        own = step * block + t
        inv_own = aux_ref[pl.ds(base + own, 1)]
        label = aux_ref[pl.ds(base + 16 + own, 1)]
        extra = jnp.where(aux_ref[total:base] == label, match, 0.0) + bias
        value = prod[:, t % 2 * width : (t % 2 + 1) * width] * jnp.maximum(aux_ref[0:total], inv_own) + extra
        value = state_ref[t].astype(F32) + value
        next_ref[t] = value.astype(BF16)
        done.append(value)
    size = block * tokens
    spot = pl.ds(pl.multiple_of(step * size, size), size)
    for core in (0, 1):

        @pl.when((row_ref[0] & 1) == core)
        def _():
            for d in range(count):
                rows = slice(d * tokens, (d + 1) * tokens)
                tile = jnp.concatenate([value[rows] for value in done], axis=0).astype(BF16)
                (same_ref if (d & 1) == core else cross_ref)[d // 2, spot, :] = tile


def pack_kernel(pairs, row_ref, same_ref, crossed_ref, *outs):
    chip = row_ref[0] >> 1
    for core in (0, 1):

        @pl.when((row_ref[0] & 1) == core)
        def _():
            for pair, out_ref in zip(pairs, outs):
                out_ref[core] = same_ref[chip ^ pair[core]]
                out_ref[1 - core] = crossed_ref[chip ^ pair[core]]


def gate_kernel(pairs, row_ref, aux_ref, gates_ref, *rest):
    tiles, (out_ref, wide_ref) = rest[:-2], rest[-2:]
    step = pl.program_id(0)
    block, total = out_ref.shape[:2]
    rows, width = tiles[0].shape[1:]
    tokens = total // (2 * len(tiles))

    @pl.when(step == 0)
    def _():
        chip = row_ref[0] >> 1
        for pair, tile in zip(pairs, tiles):
            source = chip ^ by_core(row_ref[0], pair)
            for core in (0, 1):
                spot = pl.ds(pl.multiple_of((source * 2 + core) * rows, rows), rows)
                wide_ref[spot, :] = tile[core].astype(F32)

    gain = aux_ref[2 * total + 34 : 2 * total + 35]
    shift = aux_ref[2 * total + 35 : 2 * total + 36]
    ones = jnp.full((width, width), 1.0 / width, BF16)
    none = jnp.zeros((width, width), BF16)
    means = jnp.concatenate(
        [jnp.concatenate([ones, none], axis=1), jnp.concatenate([none, ones], axis=1)], axis=0
    )
    weights = jnp.concatenate([gates_ref[0], gates_ref[1]], axis=1)
    gated = gates_ref.shape[2]
    pair = jnp.concatenate(
        [
            jnp.concatenate(
                [wide_ref[pl.ds(step * block + t + u, total, stride=tokens), :] for u in (0, 1)], axis=1
            )
            for t in range(0, block, 2)
        ],
        axis=0,
    )
    centre = pair - jnp.dot(pair.astype(BF16), means, preferred_element_type=F32)
    square = (centre * centre).astype(BF16)
    spread = jnp.dot(square, means, preferred_element_type=F32)
    scaled = centre * lax.rsqrt(spread + 1e-05)
    scaled = jnp.concatenate([scaled[:, 0:width], scaled[:, width : 2 * width]], axis=0)
    normed = (scaled * gain + shift).astype(BF16)
    mixed = jnp.dot(normed, weights, preferred_element_type=F32)
    result = (mixed[:, 0:gated] * (0.5 + 0.5 * jnp.tanh(0.5 * mixed[:, gated : 2 * gated]))).astype(BF16)
    for t in range(block):
        first = (t % 2 * (block // 2) + t // 2) * total
        out_ref[t] = result[first : first + total]


def fixed(*shape):
    return pl.BlockSpec(shape, lambda g: (0,) * len(shape))


def body(
    pairwise_state,
    homolog_embedding,
    alignment_depth,
    chain_labels,
    homolog_layer_scale,
    homolog_layer_shift,
    outer_source_matrix,
    outer_target_matrix,
    output_weight,
    output_bias,
    chain_match,
    pairwise_norm_gain,
    pairwise_norm_bias,
    input_projection_weight,
    input_gate_weight,
    *,
    count,
):
    tokens, total, width = pairwise_state.shape
    seqs, _, feats = homolog_embedding.shape
    factor = outer_source_matrix.shape[1]
    half = factor // 2
    inner = factor * seqs
    gated = input_projection_weight.shape[1]
    row = lax.axis_index("row").astype(jnp.int32).reshape(1)

    def swap(array, bits):
        bits = bits if isinstance(bits, tuple) else (bits, bits)
        return lax.ppermute(array, "row", [(r, r ^ bits[r & 1]) for r in range(count)])

    def staggered(items):
        cut = (len(items) + 1) // 2
        return list(zip(items, items[cut:] + items[:cut]))

    aux_rows = 2 * total + 40
    part = tokens * half
    mix_rows = tokens * seqs + factor * factor
    to_mix, item, aux, gates = pl.pallas_call(
        prepare_kernel,
        out_shape=(
            jax.ShapeDtypeStruct((mix_rows, width), BF16),
            jax.ShapeDtypeStruct((1, part, 2 * seqs), BF16),
            jax.ShapeDtypeStruct((aux_rows, width), F32),
            jax.ShapeDtypeStruct((2, width, gated), BF16),
        ),
        in_specs=[whole(SMEM)] + [whole(HBM)] * 16,
        out_specs=(whole(VMEM),) * 4,
        scratch_shapes=[
            SMEM((total,), jnp.int32),
            VMEM((tokens, seqs, feats), BF16),
            VMEM((1, feats), F32),
            VMEM((1, feats), F32),
            VMEM((2 * factor, feats), BF16),
            VMEM((1, total), jnp.int32),
            SMEM((total,), jnp.int32),
            VMEM((1, total), jnp.int32),
            VMEM((4, 1, width), F32),
            pltpu.SemaphoreType.DMA((16,)),
        ],
        name="prepare",
    )(
        row,
        alignment_depth,
        homolog_embedding.transpose(1, 0, 2),
        homolog_layer_scale.reshape(1, feats),
        homolog_layer_shift.reshape(1, feats),
        outer_source_matrix.T,
        outer_target_matrix.T,
        alignment_depth.reshape(1, total),
        chain_labels,
        chain_labels.reshape(1, total),
        chain_match.reshape(1, width),
        output_bias.reshape(1, width),
        pairwise_norm_gain.reshape(1, width),
        pairwise_norm_bias.reshape(1, width),
        input_projection_weight,
        input_gate_weight,
        output_weight,
    )

    y = pl.pallas_call(
        functools.partial(mix_kernel, factor),
        out_shape=jax.ShapeDtypeStruct((tokens // 2, inner, 2 * width), BF16),
        in_specs=[whole(VMEM)],
        out_specs=whole(VMEM),
        scratch_shapes=[VMEM((factor * factor, width), F32)],
        compiler_params=params(16),
        cost_estimate=pl.CostEstimate(
            flops=2 * tokens * seqs * factor * factor * width,
            bytes_accessed=2 * inner * tokens * width,
            transcendentals=0,
        ),
        name="mix",
    )(to_mix)

    def joined(*pieces):
        return pl.pallas_call(
            join_kernel,
            out_shape=jax.ShapeDtypeStruct((sum(x.shape[0] for x in pieces), part, 2 * seqs), BF16),
            in_specs=[whole(VMEM)] * len(pieces),
            out_specs=whole(VMEM),
            compiler_params=params(16),
            name="join",
        )(*pieces)

    chips = count // 2
    turn = staggered([4 * k for k in range(count // 4 - 1, 0, -1)])
    direct = [swap(item, pair) for pair in turn]
    own_came = swap(item, 2)
    own_early = swap(item, 1)
    *direct, own_came, own_early = lax.optimization_barrier((*direct, own_came, own_early))
    held = joined(*direct)
    came = swap(held, 2)
    kept, y = lax.optimization_barrier((held, y))
    early = swap(kept, 1)
    came, y = lax.optimization_barrier((came, y))
    own_late = swap(own_came, 1)
    late = swap(came, 1)

    def ranks(bits):
        return [(a ^ bits, b ^ bits) if bits in (0, 2) else (b ^ bits, a ^ bits) for a, b in turn]

    wide, state, aux = pl.pallas_call(
        functools.partial(
            first_half_kernel, [[(0, 0)], [(1, 1)], [(2, 2)], ranks(0), ranks(1), ranks(2)]
        ),
        out_shape=(
            jax.ShapeDtypeStruct((count * part, 2 * seqs), F32),
            jax.ShapeDtypeStruct((tokens, total, width), BF16),
            jax.ShapeDtypeStruct((aux_rows, width), F32),
        ),
        in_specs=[whole(SMEM)] + [whole(VMEM)] * 8,
        out_specs=(whole(VMEM),) * 3,
        compiler_params=params(16),
        name="first_half",
    )(row, pairwise_state, aux, item, own_early, own_came, held, early, came)

    block = 4
    tile = tokens * tokens
    pair_next, same, cross, _ = pl.pallas_call(
        functools.partial(pair_kernel, [[(3, 3)], ranks(3)]),
        grid=(tokens // block,),
        out_shape=(
            jax.ShapeDtypeStruct((tokens, total, width), BF16),
            jax.ShapeDtypeStruct((chips, tile, width), BF16),
            jax.ShapeDtypeStruct((chips, tile, width), BF16),
            jax.ShapeDtypeStruct((count * part, 2 * seqs), F32),
        ),
        in_specs=[whole(SMEM), whole(VMEM), pl.BlockSpec((block, total, width), lambda g: (g, 0, 0))]
        + [whole(VMEM)] * 4,
        out_specs=(pl.BlockSpec((block, total, width), lambda g: (g, 0, 0)),) + (whole(VMEM),) * 3,
        scratch_shapes=[VMEM((total, inner), BF16)],
        input_output_aliases={4: 3},
        compiler_params=params(16),
        cost_estimate=pl.CostEstimate(
            flops=2 * total * inner * tokens * width,
            bytes_accessed=2 * inner * tokens * width + 8 * tokens * total * width,
            transcendentals=0,
        ),
        name="pair",
    )(row, aux, state, y, wide, own_late, late)

    crossed = swap(cross, 1)
    sends = [(0, 0)] + staggered(list(range(chips - 1, 0, -1)))
    tiles = pl.pallas_call(
        functools.partial(pack_kernel, sends),
        out_shape=(jax.ShapeDtypeStruct((2, tile, width), BF16),) * chips,
        in_specs=[whole(SMEM), whole(VMEM), whole(VMEM)],
        out_specs=(whole(VMEM),) * chips,
        compiler_params=params(16),
        name="pack",
    )(row, same, crossed)
    tiles = [tiles[0]] + [swap(t, (2 * a, 2 * b)) for t, (a, b) in zip(tiles[1:], sends[1:])]

    block = 4
    out = pl.pallas_call(
        functools.partial(gate_kernel, sends),
        grid=(tokens // block,),
        out_shape=jax.ShapeDtypeStruct((tokens, total, gated), BF16),
        in_specs=[whole(SMEM)] + [whole(VMEM)] * (2 + chips),
        out_specs=pl.BlockSpec((block, total, gated), lambda j: (j, 0, 0)),
        scratch_shapes=[VMEM((count * tile, width), F32)],
        compiler_params=params(24),
        cost_estimate=pl.CostEstimate(
            flops=4 * tokens * total * width * gated,
            bytes_accessed=tokens * total * (2 * gated + 6 * width),
            transcendentals=tokens * total * gated,
        ),
        name="gate",
    )(row, aux, gates, *tiles)
    return pair_next, out.transpose(1, 0, 2)


def solution(mesh):
    return jax.shard_map(
        functools.partial(body, count=mesh.shape["row"]),
        mesh=mesh,
        in_specs=(
            P(("groups", "row"), None, None),
            P(None, ("groups", "row"), None),
            P("groups"),
            P("groups"),
        )
        + (P(),) * 11,
        out_specs=(P(("groups", "row"), None, None), P("groups", "row", None)),
        check_vma=False,
    )
```

```python
import functools

import jax
import jax.numpy as jnp
from jax import lax
from jax.experimental import pallas as pl
from jax.experimental.pallas import tpu as pltpu
from jax.sharding import PartitionSpec as P

F32 = jnp.float32
BF16 = jnp.bfloat16
NT = (((1,), (1,)), ((), ()))
VMEM = pltpu.VMEM
SMEM = pltpu.SMEM
HBM = pltpu.HBM
LANES = 128


def whole(space):
    return pl.BlockSpec(memory_space=space)


def params(mib):
    return pltpu.CompilerParams(vmem_limit_bytes=mib * 1024 * 1024)


def fetch(sems, *pairs):
    copies = [pltpu.make_async_copy(a, b, sems.at[n]) for n, (a, b) in enumerate(pairs)]
    for copy in copies:
        copy.start()
    return copies


def finish(copies):
    for copy in copies:
        copy.wait()


def prepare_kernel(
    row_ref, depth_hbm, hom_hbm, scale_hbm, shift_hbm, src_hbm, tgt_hbm, depth_row_hbm, chain_hbm, chain_row_hbm,
    match_hbm, bias_hbm, gain_hbm, move_hbm, proj_hbm, gate_hbm, weight_hbm,
    mix_ref, item_ref, aux_ref, gates_ref,
    depth_ref, hom_ref, scale_ref, shift_ref, both_ref, depth_row_ref, chain_ref, chain_row_ref, vec_ref, sems,
):
    tokens, seqs, feats = hom_ref.shape
    pair_width = aux_ref.shape[1]
    total = depth_ref.shape[0]
    width = src_hbm.shape[0]
    half = width // 2
    gated = proj_hbm.shape[1]
    first_copies = fetch(
        sems,
        (hom_hbm, hom_ref),
        (depth_hbm, depth_ref),
        (scale_hbm, scale_ref),
        (shift_hbm, shift_ref),
        (src_hbm, both_ref.at[0:width]),
        (tgt_hbm, both_ref.at[width : 2 * width]),
        (chain_hbm, chain_ref),
        (depth_row_hbm, depth_row_ref),
        (chain_row_hbm, chain_row_ref),
        (match_hbm, vec_ref.at[0]),
        (bias_hbm, vec_ref.at[1]),
        (gain_hbm, vec_ref.at[2]),
        (move_hbm, vec_ref.at[3]),
        (proj_hbm, gates_ref.at[0]),
        (gate_hbm, gates_ref.at[1]),
        (weight_hbm, mix_ref.at[tokens * seqs : tokens * seqs + width * width]),
    )
    finish(first_copies[:6])
    values = hom_ref[...].reshape(tokens * seqs, feats)
    ones = jnp.full((feats, feats), 1.0 / feats, BF16)
    centre = values.astype(F32) - jnp.dot(values, ones, preferred_element_type=F32)
    square = centre * centre
    high = square.astype(BF16)
    low = (square - high.astype(F32)).astype(BF16)
    spread = jnp.dot(high, ones, preferred_element_type=F32) + jnp.dot(
        low, ones, preferred_element_type=F32
    )
    normed = (centre * lax.rsqrt(spread + 1e-05) * scale_ref[...] + shift_ref[...]).astype(BF16)
    turned = lax.dot_general(both_ref[width : 2 * width], normed, NT, preferred_element_type=F32)
    plain = lax.dot_general(normed, both_ref[0:width], NT, preferred_element_type=F32)
    first = row_ref[0] * tokens
    row_pos = lax.broadcasted_iota(jnp.int32, (seqs, width), 0)
    lane = lax.broadcasted_iota(jnp.int32, (half, 2 * seqs), 1)
    seq_pos = jnp.where(lane < seqs, lane, lane - seqs)
    for n in range(tokens):
        depth = depth_ref[first + n]
        rows = slice(n * seqs, (n + 1) * seqs)
        mix_ref[rows, 0:width] = jnp.where(row_pos < depth, plain[rows], 0.0).astype(BF16)
        joint = jnp.concatenate([turned[0:half, rows], turned[half:width, rows]], axis=1)
        item_ref[0, n * half : (n + 1) * half] = jnp.where(seq_pos < depth, joint, 0.0).astype(BF16)

    finish(first_copies[6:])
    same = lax.broadcasted_iota(jnp.int32, (total, total), 0) == lax.broadcasted_iota(
        jnp.int32, (total, total), 1
    )
    fill = jnp.ones((total, pair_width), BF16)

    def column(ref):
        diagonal = jnp.where(same, ref[...].astype(F32), 0.0).astype(BF16)
        return jnp.dot(diagonal, fill, preferred_element_type=F32)

    aux_ref[0:total] = 1.0 / jnp.maximum(column(depth_row_ref), 1.0)
    aux_ref[total : 2 * total] = column(chain_row_ref)
    for n in range(tokens):
        own = jnp.full((1, pair_width), depth_ref[first + n], jnp.int32).astype(F32)
        aux_ref[2 * total + n : 2 * total + n + 1] = 1.0 / jnp.maximum(own, 1.0)
        label = jnp.full((1, pair_width), chain_ref[first + n], jnp.int32).astype(F32)
        aux_ref[2 * total + 16 + n : 2 * total + 17 + n] = label
    for n in range(4):
        aux_ref[2 * total + 32 + n : 2 * total + 33 + n] = vec_ref[n]


def mix_kernel(factor, mix_ref, out_ref, wide_ref):
    half = factor // 2
    seqs = out_ref.shape[1] // factor
    width = mix_ref.shape[1]
    lefts = mix_ref.shape[0] - factor * factor
    tokens = lefts // seqs
    wide_ref[...] = mix_ref[lefts : lefts + factor * factor].astype(F32)

    def one(q, carry):
        pair = [wide_ref[pl.ds(q + t * half, factor, stride=factor), :] for t in (0, 1)]
        rhs = jnp.concatenate(pair, axis=1).astype(BF16)
        mixed = jnp.dot(mix_ref[0:lefts, 0:factor], rhs, preferred_element_type=F32).astype(BF16)
        for n in range(tokens):
            rows = slice(n * seqs, (n + 1) * seqs)
            cols = slice(n % 2 * width, (n % 2 + 1) * width)
            for t in (0, 1):
                spot = pl.ds(pl.multiple_of((2 * q + t) * seqs, seqs), seqs)
                out_ref[n // 2, spot, cols] = mixed[rows, t * width : (t + 1) * width]
        return carry

    lax.fori_loop(0, half, one, 0, unroll=4)


def join_kernel(*refs):
    spot = 0
    for piece in refs[:-1]:
        refs[-1][spot : spot + piece.shape[0]] = piece[...]
        spot += piece.shape[0]


def by_core(row, pair):
    return jnp.where((row & 1) == 1, pair[1], pair[0])


def spread_items(row, wide_ref, pieces, orders):
    for piece, pairs in zip(pieces, orders):
        size = piece.shape[1]
        for m, pair in enumerate(pairs):
            spot = pl.ds(pl.multiple_of((row ^ by_core(row, pair)) * size, size), size)
            wide_ref[spot, :] = piece[m].astype(F32)


def first_half_kernel(orders, row_ref, state_ref, aux_ref, *rest):
    pieces, (wide_ref, state_out, aux_out) = rest[:-3], rest[-3:]
    state_out[...] = state_ref[...]
    aux_out[...] = aux_ref[...]
    spread_items(row_ref[0], wide_ref, pieces, orders)


def pair_kernel(orders, row_ref, aux_ref, state_ref, y_ref, wide_in, *rest):
    pieces, (next_ref, same_ref, cross_ref, wide_ref, lhs_ref) = rest[:-5], rest[-5:]
    step = pl.program_id(0)
    block, total, width = state_ref.shape
    lanes = pieces[0].shape[2]
    count = 2 * same_ref.shape[0]
    tokens = total // count
    groups = wide_ref.shape[0] // total

    @pl.when(step == 0)
    def _():
        spread_items(row_ref[0], wide_ref, pieces, orders)

        def one(q, carry):
            cols = pl.ds(pl.multiple_of(q * lanes, lanes), lanes)
            lhs_ref[:, cols] = wide_ref[pl.ds(q, total, stride=groups), :].astype(BF16)
            return carry

        lax.fori_loop(0, groups, one, 0, unroll=4)

    base = 2 * total
    match = aux_ref[base + 32 : base + 33]
    bias = aux_ref[base + 33 : base + 34]
    done = []
    for t in range(block):
        if t % 2 == 0:
            prod = jnp.dot(lhs_ref[...], y_ref[step * (block // 2) + t // 2], preferred_element_type=F32)
        own = step * block + t
        inv_own = aux_ref[pl.ds(base + own, 1)]
        label = aux_ref[pl.ds(base + 16 + own, 1)]
        extra = jnp.where(aux_ref[total:base] == label, match, 0.0) + bias
        value = prod[:, t % 2 * width : (t % 2 + 1) * width] * jnp.maximum(aux_ref[0:total], inv_own) + extra
        value = state_ref[t].astype(F32) + value
        next_ref[t] = value.astype(BF16)
        done.append(value)
    size = block * tokens
    spot = pl.ds(pl.multiple_of(step * size, size), size)
    for core in (0, 1):

        @pl.when((row_ref[0] & 1) == core)
        def _():
            for d in range(count):
                rows = slice(d * tokens, (d + 1) * tokens)
                tile = jnp.concatenate([value[rows] for value in done], axis=0).astype(BF16)
                (same_ref if (d & 1) == core else cross_ref)[d // 2, spot, :] = tile


def pack_kernel(pairs, row_ref, same_ref, crossed_ref, *outs):
    chip = row_ref[0] >> 1
    for core in (0, 1):

        @pl.when((row_ref[0] & 1) == core)
        def _():
            for pair, out_ref in zip(pairs, outs):
                out_ref[core] = same_ref[chip ^ pair[core]]
                out_ref[1 - core] = crossed_ref[chip ^ pair[core]]


def gate_kernel(groups, row_ref, aux_ref, gates_ref, *rest):
    tiles, (out_hbm, wide_ref, done_ref, sems) = rest[: 2 * len(groups)], rest[-4:]
    tokens, total, gated = out_hbm.shape
    rows, width = tiles[0].shape[1:]
    chip = row_ref[0] >> 1
    band = 4 * tokens
    gain = aux_ref[2 * total + 34 : 2 * total + 35]
    shift = aux_ref[2 * total + 35 : 2 * total + 36]
    ones = jnp.full((width, width), 1.0 / width, BF16)
    none = jnp.zeros((width, width), BF16)
    means = jnp.concatenate(
        [jnp.concatenate([ones, none], axis=1), jnp.concatenate([none, ones], axis=1)], axis=0
    )
    weights = jnp.concatenate([gates_ref[0], gates_ref[1]], axis=1)
    copies = []
    for n, pairs in enumerate(groups):
        for m, pair in enumerate(pairs):
            source = chip ^ by_core(row_ref[0], pair)
            for core in (0, 1):
                spot = pl.ds(pl.multiple_of(((source & 1) * 2 + core) * rows, rows), rows)
                wide_ref[n, spot, :] = tiles[2 * n + m][core].astype(F32)
        place = source >> 1
        parts = [wide_ref[n, pl.ds(j, band, stride=tokens), :] for j in range(tokens)]
        half = tokens // 2
        pair = jnp.concatenate(
            [jnp.concatenate(parts[:half], axis=0), jnp.concatenate(parts[half:], axis=0)], axis=1
        )
        centre = pair - jnp.dot(pair.astype(BF16), means, preferred_element_type=F32)
        square = (centre * centre).astype(BF16)
        spread = jnp.dot(square, means, preferred_element_type=F32)
        scaled = centre * lax.rsqrt(spread + 1e-05)
        scaled = jnp.concatenate([scaled[:, 0:width], scaled[:, width : 2 * width]], axis=0)
        normed = (scaled * gain + shift).astype(BF16)
        mixed = jnp.dot(normed, weights, preferred_element_type=F32)
        result = (mixed[:, 0:gated] * (0.5 + 0.5 * jnp.tanh(0.5 * mixed[:, gated : 2 * gated]))).astype(BF16)
        for j in range(tokens):
            done_ref[n, j] = result[j * band : (j + 1) * band]
        copies.append(
            pltpu.make_async_copy(
                done_ref.at[n],
                out_hbm.at[:, pl.ds(pl.multiple_of(place * band, band), band), :],
                sems.at[n],
            )
        )
        copies[-1].start()
    finish(copies)


def fixed(*shape):
    return pl.BlockSpec(shape, lambda g: (0,) * len(shape))


def body(
    pairwise_state,
    homolog_embedding,
    alignment_depth,
    chain_labels,
    homolog_layer_scale,
    homolog_layer_shift,
    outer_source_matrix,
    outer_target_matrix,
    output_weight,
    output_bias,
    chain_match,
    pairwise_norm_gain,
    pairwise_norm_bias,
    input_projection_weight,
    input_gate_weight,
    *,
    count,
):
    tokens, total, width = pairwise_state.shape
    seqs, _, feats = homolog_embedding.shape
    factor = outer_source_matrix.shape[1]
    half = factor // 2
    inner = factor * seqs
    gated = input_projection_weight.shape[1]
    row = lax.axis_index("row").astype(jnp.int32).reshape(1)

    def swap(array, bits):
        bits = bits if isinstance(bits, tuple) else (bits, bits)
        return lax.ppermute(array, "row", [(r, r ^ bits[r & 1]) for r in range(count)])

    def staggered(items):
        cut = (len(items) + 1) // 2
        return list(zip(items, items[cut:] + items[:cut]))

    aux_rows = 2 * total + 40
    part = tokens * half
    mix_rows = tokens * seqs + factor * factor
    to_mix, item, aux, gates = pl.pallas_call(
        prepare_kernel,
        out_shape=(
            jax.ShapeDtypeStruct((mix_rows, width), BF16),
            jax.ShapeDtypeStruct((1, part, 2 * seqs), BF16),
            jax.ShapeDtypeStruct((aux_rows, width), F32),
            jax.ShapeDtypeStruct((2, width, gated), BF16),
        ),
        in_specs=[whole(SMEM)] + [whole(HBM)] * 16,
        out_specs=(whole(VMEM),) * 4,
        scratch_shapes=[
            SMEM((total,), jnp.int32),
            VMEM((tokens, seqs, feats), BF16),
            VMEM((1, feats), F32),
            VMEM((1, feats), F32),
            VMEM((2 * factor, feats), BF16),
            VMEM((1, total), jnp.int32),
            SMEM((total,), jnp.int32),
            VMEM((1, total), jnp.int32),
            VMEM((4, 1, width), F32),
            pltpu.SemaphoreType.DMA((16,)),
        ],
        name="prepare",
    )(
        row,
        alignment_depth,
        homolog_embedding.transpose(1, 0, 2),
        homolog_layer_scale.reshape(1, feats),
        homolog_layer_shift.reshape(1, feats),
        outer_source_matrix.T,
        outer_target_matrix.T,
        alignment_depth.reshape(1, total),
        chain_labels,
        chain_labels.reshape(1, total),
        chain_match.reshape(1, width),
        output_bias.reshape(1, width),
        pairwise_norm_gain.reshape(1, width),
        pairwise_norm_bias.reshape(1, width),
        input_projection_weight,
        input_gate_weight,
        output_weight,
    )

    y = pl.pallas_call(
        functools.partial(mix_kernel, factor),
        out_shape=jax.ShapeDtypeStruct((tokens // 2, inner, 2 * width), BF16),
        in_specs=[whole(VMEM)],
        out_specs=whole(VMEM),
        scratch_shapes=[VMEM((factor * factor, width), F32)],
        compiler_params=params(16),
        cost_estimate=pl.CostEstimate(
            flops=2 * tokens * seqs * factor * factor * width,
            bytes_accessed=2 * inner * tokens * width,
            transcendentals=0,
        ),
        name="mix",
    )(to_mix)

    def joined(*pieces):
        return pl.pallas_call(
            join_kernel,
            out_shape=jax.ShapeDtypeStruct((sum(x.shape[0] for x in pieces), part, 2 * seqs), BF16),
            in_specs=[whole(VMEM)] * len(pieces),
            out_specs=whole(VMEM),
            compiler_params=params(16),
            name="join",
        )(*pieces)

    chips = count // 2
    turn = staggered([4 * k for k in range(count // 4 - 1, 0, -1)])
    direct = [swap(item, pair) for pair in turn]
    own_came = swap(item, 2)
    own_early = swap(item, 1)
    *direct, own_came, own_early = lax.optimization_barrier((*direct, own_came, own_early))
    held = joined(*direct)
    came = swap(held, 2)
    kept, y = lax.optimization_barrier((held, y))
    early = swap(kept, 1)
    came, y = lax.optimization_barrier((came, y))
    own_late = swap(own_came, 1)
    late = swap(came, 1)

    def ranks(bits):
        return [(a ^ bits, b ^ bits) if bits in (0, 2) else (b ^ bits, a ^ bits) for a, b in turn]

    wide, state, aux = pl.pallas_call(
        functools.partial(
            first_half_kernel, [[(0, 0)], [(1, 1)], [(2, 2)], ranks(0), ranks(1), ranks(2)]
        ),
        out_shape=(
            jax.ShapeDtypeStruct((count * part, 2 * seqs), F32),
            jax.ShapeDtypeStruct((tokens, total, width), BF16),
            jax.ShapeDtypeStruct((aux_rows, width), F32),
        ),
        in_specs=[whole(SMEM)] + [whole(VMEM)] * 8,
        out_specs=(whole(VMEM),) * 3,
        compiler_params=params(16),
        name="first_half",
    )(row, pairwise_state, aux, item, own_early, own_came, held, early, came)

    block = 4
    tile = tokens * tokens
    pair_next, same, cross, _ = pl.pallas_call(
        functools.partial(pair_kernel, [[(3, 3)], ranks(3)]),
        grid=(tokens // block,),
        out_shape=(
            jax.ShapeDtypeStruct((tokens, total, width), BF16),
            jax.ShapeDtypeStruct((chips, tile, width), BF16),
            jax.ShapeDtypeStruct((chips, tile, width), BF16),
            jax.ShapeDtypeStruct((count * part, 2 * seqs), F32),
        ),
        in_specs=[whole(SMEM), whole(VMEM), pl.BlockSpec((block, total, width), lambda g: (g, 0, 0))]
        + [whole(VMEM)] * 4,
        out_specs=(pl.BlockSpec((block, total, width), lambda g: (g, 0, 0)),) + (whole(VMEM),) * 3,
        scratch_shapes=[VMEM((total, inner), BF16)],
        input_output_aliases={4: 3},
        compiler_params=params(16),
        cost_estimate=pl.CostEstimate(
            flops=2 * total * inner * tokens * width,
            bytes_accessed=2 * inner * tokens * width + 8 * tokens * total * width,
            transcendentals=0,
        ),
        name="pair",
    )(row, aux, state, y, wide, own_late, late)

    crossed = swap(cross, 1)
    others = staggered([(k, k - 1) for k in range(chips - 1, 1, -2)])
    others = [[(a[m], b[m]) for m in (0, 1)] for a, b in others]
    cut = (len(others) + 1) // 2
    first, last = others[:cut], [[(0, 0), (1, 1)]] + others[cut:]
    sends = [(0, 0)] + [pair for group in first for pair in group] + [(1, 1)]
    sends += [pair for group in others[cut:] for pair in group]
    tiles = pl.pallas_call(
        functools.partial(pack_kernel, sends),
        out_shape=(jax.ShapeDtypeStruct((2, tile, width), BF16),) * chips,
        in_specs=[whole(SMEM), whole(VMEM), whole(VMEM)],
        out_specs=(whole(VMEM),) * chips,
        compiler_params=params(16),
        name="pack",
    )(row, same, crossed)
    tiles = [tiles[0]] + [swap(t, (2 * a, 2 * b)) for t, (a, b) in zip(tiles[1:], sends[1:])]

    by_send = dict(zip(sends, tiles))

    def gate(groups, name, *before):
        given = [by_send[pair] for group in groups for pair in group]
        return pl.pallas_call(
            functools.partial(gate_kernel, groups),
            out_shape=jax.ShapeDtypeStruct((tokens, total, gated), BF16),
            in_specs=[whole(SMEM)] + [whole(VMEM)] * (2 + len(given)) + [whole(HBM)] * len(before),
            out_specs=whole(HBM),
            scratch_shapes=[
                VMEM((len(groups), 4 * tile, width), F32),
                VMEM((len(groups), tokens, 4 * tokens, gated), BF16),
                pltpu.SemaphoreType.DMA((len(groups),)),
            ],
            input_output_aliases={3 + len(given): 0} if before else {},
            compiler_params=params(24),
            cost_estimate=pl.CostEstimate(
                flops=2 * tokens * total * width * gated,
                bytes_accessed=tokens * total * (gated + 3 * width),
                transcendentals=tokens * total * gated // 2,
            ),
            name=name,
        )(row, aux, gates, *given, *before)

    out = gate(last, "gate_last", gate(first, "gate_first"))
    return pair_next, out.transpose(1, 0, 2)


def solution(mesh):
    return jax.shard_map(
        functools.partial(body, count=mesh.shape["row"]),
        mesh=mesh,
        in_specs=(
            P(("groups", "row"), None, None),
            P(None, ("groups", "row"), None),
            P("groups"),
            P("groups"),
        )
        + (P(),) * 11,
        out_specs=(P(("groups", "row"), None, None), P("groups", "row", None)),
        check_vma=False,
    )
```

```python
import functools

import jax
import jax.numpy as jnp
from jax import lax
from jax.experimental import pallas as pl
from jax.experimental.pallas import tpu as pltpu
from jax.sharding import PartitionSpec as P

F32 = jnp.float32
BF16 = jnp.bfloat16
NT = (((1,), (1,)), ((), ()))
VMEM = pltpu.VMEM
SMEM = pltpu.SMEM
HBM = pltpu.HBM
LANES = 128


def whole(space):
    return pl.BlockSpec(memory_space=space)


def params(mib):
    return pltpu.CompilerParams(vmem_limit_bytes=mib * 1024 * 1024)


def fetch(sems, *pairs):
    copies = [pltpu.make_async_copy(a, b, sems.at[n]) for n, (a, b) in enumerate(pairs)]
    for copy in copies:
        copy.start()
    return copies


def finish(copies):
    for copy in copies:
        copy.wait()


def prepare_kernel(
    row_ref, depth_hbm, hom_hbm, scale_hbm, shift_hbm, src_hbm, tgt_hbm, depth_row_hbm, chain_hbm, chain_row_hbm,
    match_hbm, bias_hbm, gain_hbm, move_hbm, proj_hbm, gate_hbm, weight_hbm,
    mix_ref, item_ref, aux_ref, gates_ref,
    depth_ref, hom_ref, scale_ref, shift_ref, both_ref, depth_row_ref, chain_ref, chain_row_ref, vec_ref, sems,
):
    tokens, seqs, feats = hom_ref.shape
    pair_width = aux_ref.shape[1]
    total = depth_ref.shape[0]
    width = src_hbm.shape[0]
    half = width // 2
    gated = proj_hbm.shape[1]
    first_copies = fetch(
        sems,
        (hom_hbm, hom_ref),
        (depth_hbm, depth_ref),
        (scale_hbm, scale_ref),
        (shift_hbm, shift_ref),
        (src_hbm, both_ref.at[0:width]),
        (tgt_hbm, both_ref.at[width : 2 * width]),
        (chain_hbm, chain_ref),
        (depth_row_hbm, depth_row_ref),
        (chain_row_hbm, chain_row_ref),
        (match_hbm, vec_ref.at[0]),
        (bias_hbm, vec_ref.at[1]),
        (gain_hbm, vec_ref.at[2]),
        (move_hbm, vec_ref.at[3]),
        (proj_hbm, gates_ref.at[0]),
        (gate_hbm, gates_ref.at[1]),
        (weight_hbm, mix_ref.at[tokens * seqs : tokens * seqs + width * width]),
    )
    finish(first_copies[:6])
    values = hom_ref[...].reshape(tokens * seqs, feats)
    ones = jnp.full((feats, feats), 1.0 / feats, BF16)
    centre = values.astype(F32) - jnp.dot(values, ones, preferred_element_type=F32)
    square = centre * centre
    high = square.astype(BF16)
    low = (square - high.astype(F32)).astype(BF16)
    spread = jnp.dot(high, ones, preferred_element_type=F32) + jnp.dot(
        low, ones, preferred_element_type=F32
    )
    normed = (centre * lax.rsqrt(spread + 1e-05) * scale_ref[...] + shift_ref[...]).astype(BF16)
    turned = lax.dot_general(both_ref[width : 2 * width], normed, NT, preferred_element_type=F32)
    plain = lax.dot_general(normed, both_ref[0:width], NT, preferred_element_type=F32)
    first = row_ref[0] * tokens
    row_pos = lax.broadcasted_iota(jnp.int32, (seqs, width), 0)
    lane = lax.broadcasted_iota(jnp.int32, (half, 2 * seqs), 1)
    seq_pos = jnp.where(lane < seqs, lane, lane - seqs)
    for n in range(tokens):
        depth = depth_ref[first + n]
        rows = slice(n * seqs, (n + 1) * seqs)
        mix_ref[rows, 0:width] = jnp.where(row_pos < depth, plain[rows], 0.0).astype(BF16)
        joint = jnp.concatenate([turned[0:half, rows], turned[half:width, rows]], axis=1)
        item_ref[0, n * half : (n + 1) * half] = jnp.where(seq_pos < depth, joint, 0.0).astype(BF16)

    finish(first_copies[6:])
    same = lax.broadcasted_iota(jnp.int32, (total, total), 0) == lax.broadcasted_iota(
        jnp.int32, (total, total), 1
    )
    fill = jnp.ones((total, pair_width), BF16)

    def column(ref):
        diagonal = jnp.where(same, ref[...].astype(F32), 0.0).astype(BF16)
        return jnp.dot(diagonal, fill, preferred_element_type=F32)

    aux_ref[0:total] = 1.0 / jnp.maximum(column(depth_row_ref), 1.0)
    aux_ref[total : 2 * total] = column(chain_row_ref)
    for n in range(tokens):
        own = jnp.full((1, pair_width), depth_ref[first + n], jnp.int32).astype(F32)
        aux_ref[2 * total + n : 2 * total + n + 1] = 1.0 / jnp.maximum(own, 1.0)
        label = jnp.full((1, pair_width), chain_ref[first + n], jnp.int32).astype(F32)
        aux_ref[2 * total + 16 + n : 2 * total + 17 + n] = label
    for n in range(4):
        aux_ref[2 * total + 32 + n : 2 * total + 33 + n] = vec_ref[n]


def mix_kernel(factor, mix_ref, out_ref, wide_ref):
    half = factor // 2
    seqs = out_ref.shape[1] // factor
    width = mix_ref.shape[1]
    lefts = mix_ref.shape[0] - factor * factor
    tokens = lefts // seqs
    wide_ref[...] = mix_ref[lefts : lefts + factor * factor].astype(F32)

    def one(q, carry):
        pair = [wide_ref[pl.ds(q + t * half, factor, stride=factor), :] for t in (0, 1)]
        rhs = jnp.concatenate(pair, axis=1).astype(BF16)
        mixed = jnp.dot(mix_ref[0:lefts, 0:factor], rhs, preferred_element_type=F32).astype(BF16)
        for n in range(tokens):
            rows = slice(n * seqs, (n + 1) * seqs)
            cols = slice(n % 2 * width, (n % 2 + 1) * width)
            for t in (0, 1):
                spot = pl.ds(pl.multiple_of((2 * q + t) * seqs, seqs), seqs)
                out_ref[n // 2, spot, cols] = mixed[rows, t * width : (t + 1) * width]
        return carry

    lax.fori_loop(0, half, one, 0, unroll=4)


def join_kernel(*refs):
    spot = 0
    for piece in refs[:-1]:
        refs[-1][spot : spot + piece.shape[0]] = piece[...]
        spot += piece.shape[0]


def by_core(row, pair):
    return jnp.where((row & 1) == 1, pair[1], pair[0])


def spread_items(row, wide_ref, pieces, orders):
    for piece, pairs in zip(pieces, orders):
        size = piece.shape[1]
        for m, pair in enumerate(pairs):
            spot = pl.ds(pl.multiple_of((row ^ by_core(row, pair)) * size, size), size)
            wide_ref[spot, :] = piece[m].astype(F32)


def first_half_kernel(orders, row_ref, state_ref, aux_ref, *rest):
    pieces, (wide_ref, state_out, aux_out) = rest[:-3], rest[-3:]
    state_out[...] = state_ref[...]
    aux_out[...] = aux_ref[...]
    spread_items(row_ref[0], wide_ref, pieces, orders)


def pair_kernel(orders, row_ref, aux_ref, state_ref, y_ref, wide_in, *rest):
    pieces, (next_ref, same_ref, cross_ref, wide_ref, lhs_ref) = rest[:-5], rest[-5:]
    step = pl.program_id(0)
    block, total, width = state_ref.shape
    lanes = pieces[0].shape[2]
    count = 2 * same_ref.shape[0]
    tokens = total // count
    groups = wide_ref.shape[0] // total

    @pl.when(step == 0)
    def _():
        spread_items(row_ref[0], wide_ref, pieces, orders)

        def one(q, carry):
            cols = pl.ds(pl.multiple_of(q * lanes, lanes), lanes)
            lhs_ref[:, cols] = wide_ref[pl.ds(q, total, stride=groups), :].astype(BF16)
            return carry

        lax.fori_loop(0, groups, one, 0, unroll=4)

    base = 2 * total
    match = aux_ref[base + 32 : base + 33]
    bias = aux_ref[base + 33 : base + 34]
    done = []
    for t in range(block):
        if t % 2 == 0:
            prod = jnp.dot(lhs_ref[...], y_ref[step * (block // 2) + t // 2], preferred_element_type=F32)
        own = step * block + t
        inv_own = aux_ref[pl.ds(base + own, 1)]
        label = aux_ref[pl.ds(base + 16 + own, 1)]
        extra = jnp.where(aux_ref[total:base] == label, match, 0.0) + bias
        value = prod[:, t % 2 * width : (t % 2 + 1) * width] * jnp.maximum(aux_ref[0:total], inv_own) + extra
        value = state_ref[t].astype(F32) + value
        next_ref[t] = value.astype(BF16)
        done.append(value)
    size = block * tokens
    spot = pl.ds(pl.multiple_of(step * size, size), size)
    for core in (0, 1):

        @pl.when((row_ref[0] & 1) == core)
        def _():
            for d in range(count):
                rows = slice(d * tokens, (d + 1) * tokens)
                tile = jnp.concatenate([value[rows] for value in done], axis=0).astype(BF16)
                (same_ref if (d & 1) == core else cross_ref)[d // 2, spot, :] = tile


def pack_kernel(pairs, row_ref, same_ref, crossed_ref, *outs):
    chip = row_ref[0] >> 1
    for core in (0, 1):

        @pl.when((row_ref[0] & 1) == core)
        def _():
            for pair, out_ref in zip(pairs, outs):
                out_ref[core] = same_ref[chip ^ pair[core]]
                out_ref[1 - core] = crossed_ref[chip ^ pair[core]]


def gate_kernel(groups, row_ref, aux_ref, gates_ref, *rest):
    tiles, (out_hbm, wide_ref, done_ref, sems) = rest[: 2 * len(groups)], rest[-4:]
    tokens, total, gated = out_hbm.shape
    rows, width = tiles[0].shape[1:]
    chip = row_ref[0] >> 1
    band = 4 * tokens
    gain = aux_ref[2 * total + 34 : 2 * total + 35]
    shift = aux_ref[2 * total + 35 : 2 * total + 36]
    ones = jnp.full((width, width), 1.0 / width, BF16)
    none = jnp.zeros((width, width), BF16)
    means = jnp.concatenate(
        [jnp.concatenate([ones, none], axis=1), jnp.concatenate([none, ones], axis=1)], axis=0
    )
    weights = jnp.concatenate([gates_ref[0], gates_ref[1]], axis=1)
    copies = []
    for n, pairs in enumerate(groups):
        for m, pair in enumerate(pairs):
            source = chip ^ by_core(row_ref[0], pair)
            for core in (0, 1):
                spot = pl.ds(pl.multiple_of(((source & 1) * 2 + core) * rows, rows), rows)
                wide_ref[n, spot, :] = tiles[2 * n + m][core].astype(F32)
        place = source >> 1
        parts = [wide_ref[n, pl.ds(j, band, stride=tokens), :] for j in range(tokens)]
        half = tokens // 2
        pair = jnp.concatenate(
            [jnp.concatenate(parts[:half], axis=0), jnp.concatenate(parts[half:], axis=0)], axis=1
        )
        centre = pair - jnp.dot(pair.astype(BF16), means, preferred_element_type=F32)
        square = (centre * centre).astype(BF16)
        spread = jnp.dot(square, means, preferred_element_type=F32)
        scaled = centre * lax.rsqrt(spread + 1e-05)
        scaled = jnp.concatenate([scaled[:, 0:width], scaled[:, width : 2 * width]], axis=0)
        normed = (scaled * gain + shift).astype(BF16)
        mixed = jnp.dot(normed, weights, preferred_element_type=F32)
        result = (mixed[:, 0:gated] * (0.5 + 0.5 * jnp.tanh(0.5 * mixed[:, gated : 2 * gated]))).astype(BF16)
        for j in range(tokens):
            done_ref[n, j] = result[j * band : (j + 1) * band]
        copies.append(
            pltpu.make_async_copy(
                done_ref.at[n],
                out_hbm.at[:, pl.ds(pl.multiple_of(place * band, band), band), :],
                sems.at[n],
            )
        )
        copies[-1].start()
    finish(copies)


def fixed(*shape):
    return pl.BlockSpec(shape, lambda g: (0,) * len(shape))


def body(
    pairwise_state,
    homolog_embedding,
    alignment_depth,
    chain_labels,
    homolog_layer_scale,
    homolog_layer_shift,
    outer_source_matrix,
    outer_target_matrix,
    output_weight,
    output_bias,
    chain_match,
    pairwise_norm_gain,
    pairwise_norm_bias,
    input_projection_weight,
    input_gate_weight,
    *,
    count,
):
    tokens, total, width = pairwise_state.shape
    seqs, _, feats = homolog_embedding.shape
    factor = outer_source_matrix.shape[1]
    half = factor // 2
    inner = factor * seqs
    gated = input_projection_weight.shape[1]
    row = lax.axis_index("row").astype(jnp.int32).reshape(1)

    def swap(array, bits):
        bits = bits if isinstance(bits, tuple) else (bits, bits)
        return lax.ppermute(array, "row", [(r, r ^ bits[r & 1]) for r in range(count)])

    def staggered(items):
        cut = (len(items) + 1) // 2
        return list(zip(items, items[cut:] + items[:cut]))

    aux_rows = 2 * total + 40
    part = tokens * half
    mix_rows = tokens * seqs + factor * factor
    to_mix, item, aux, gates = pl.pallas_call(
        prepare_kernel,
        out_shape=(
            jax.ShapeDtypeStruct((mix_rows, width), BF16),
            jax.ShapeDtypeStruct((1, part, 2 * seqs), BF16),
            jax.ShapeDtypeStruct((aux_rows, width), F32),
            jax.ShapeDtypeStruct((2, width, gated), BF16),
        ),
        in_specs=[whole(SMEM)] + [whole(HBM)] * 16,
        out_specs=(whole(VMEM),) * 4,
        scratch_shapes=[
            SMEM((total,), jnp.int32),
            VMEM((tokens, seqs, feats), BF16),
            VMEM((1, feats), F32),
            VMEM((1, feats), F32),
            VMEM((2 * factor, feats), BF16),
            VMEM((1, total), jnp.int32),
            SMEM((total,), jnp.int32),
            VMEM((1, total), jnp.int32),
            VMEM((4, 1, width), F32),
            pltpu.SemaphoreType.DMA((16,)),
        ],
        name="prepare",
    )(
        row,
        alignment_depth,
        homolog_embedding.transpose(1, 0, 2),
        homolog_layer_scale.reshape(1, feats),
        homolog_layer_shift.reshape(1, feats),
        outer_source_matrix.T,
        outer_target_matrix.T,
        alignment_depth.reshape(1, total),
        chain_labels,
        chain_labels.reshape(1, total),
        chain_match.reshape(1, width),
        output_bias.reshape(1, width),
        pairwise_norm_gain.reshape(1, width),
        pairwise_norm_bias.reshape(1, width),
        input_projection_weight,
        input_gate_weight,
        output_weight,
    )

    def mixed(to_mix):
        return pl.pallas_call(
            functools.partial(mix_kernel, factor),
            out_shape=jax.ShapeDtypeStruct((tokens // 2, inner, 2 * width), BF16),
            in_specs=[whole(VMEM)],
            out_specs=whole(VMEM),
            scratch_shapes=[VMEM((factor * factor, width), F32)],
            compiler_params=params(16),
            cost_estimate=pl.CostEstimate(
                flops=2 * tokens * seqs * factor * factor * width,
                bytes_accessed=2 * inner * tokens * width,
                transcendentals=0,
            ),
            name="mix",
        )(to_mix)

    def joined(*pieces):
        return pl.pallas_call(
            join_kernel,
            out_shape=jax.ShapeDtypeStruct((sum(x.shape[0] for x in pieces), part, 2 * seqs), BF16),
            in_specs=[whole(VMEM)] * len(pieces),
            out_specs=whole(VMEM),
            compiler_params=params(16),
            name="join",
        )(*pieces)

    chips = count // 2
    turn = staggered([4 * k for k in range(count // 4 - 1, 0, -1)])
    direct = [swap(item, pair) for pair in turn]
    own_came = swap(item, 2)
    own_early = swap(item, 1)
    came = [swap(d, 2) for d in direct]
    *direct, to_mix = lax.optimization_barrier((*direct, to_mix))
    y = mixed(to_mix)
    held = joined(*direct)
    held, y = lax.optimization_barrier((held, y))
    early = swap(held, 1)
    *came, own_came, own_early, y = lax.optimization_barrier((*came, own_came, own_early, y))
    came = joined(*came)
    own_late = swap(own_came, 1)
    late = swap(came, 1)

    def ranks(bits):
        return [(a ^ bits, b ^ bits) if bits in (0, 2) else (b ^ bits, a ^ bits) for a, b in turn]

    wide, state, aux = pl.pallas_call(
        functools.partial(
            first_half_kernel, [[(0, 0)], [(1, 1)], [(2, 2)], ranks(0), ranks(1), ranks(2)]
        ),
        out_shape=(
            jax.ShapeDtypeStruct((count * part, 2 * seqs), F32),
            jax.ShapeDtypeStruct((tokens, total, width), BF16),
            jax.ShapeDtypeStruct((aux_rows, width), F32),
        ),
        in_specs=[whole(SMEM)] + [whole(VMEM)] * 8,
        out_specs=(whole(VMEM),) * 3,
        compiler_params=params(16),
        name="first_half",
    )(row, pairwise_state, aux, item, own_early, own_came, held, early, came)

    block = 4
    tile = tokens * tokens
    pair_next, same, cross, _ = pl.pallas_call(
        functools.partial(pair_kernel, [[(3, 3)], ranks(3)]),
        grid=(tokens // block,),
        out_shape=(
            jax.ShapeDtypeStruct((tokens, total, width), BF16),
            jax.ShapeDtypeStruct((chips, tile, width), BF16),
            jax.ShapeDtypeStruct((chips, tile, width), BF16),
            jax.ShapeDtypeStruct((count * part, 2 * seqs), F32),
        ),
        in_specs=[whole(SMEM), whole(VMEM), pl.BlockSpec((block, total, width), lambda g: (g, 0, 0))]
        + [whole(VMEM)] * 4,
        out_specs=(pl.BlockSpec((block, total, width), lambda g: (g, 0, 0)),) + (whole(VMEM),) * 3,
        scratch_shapes=[VMEM((total, inner), BF16)],
        input_output_aliases={4: 3},
        compiler_params=params(16),
        cost_estimate=pl.CostEstimate(
            flops=2 * total * inner * tokens * width,
            bytes_accessed=2 * inner * tokens * width + 8 * tokens * total * width,
            transcendentals=0,
        ),
        name="pair",
    )(row, aux, state, y, wide, own_late, late)

    crossed = swap(cross, 1)
    falling = [(k, k - 1) for k in range(chips - 1, 1, -2)]
    inward = [falling[m // 2] if m % 2 == 0 else falling[-1 - m // 2] for m in range(len(falling))]
    mirrored = [inward[m ^ 1] if (m ^ 1) < len(inward) else inward[m] for m in range(len(inward))]
    others = [[(a[m], b[m]) for m in (0, 1)] for a, b in zip(inward, mirrored)]
    cut = (len(others) + 1) // 2
    first, last = others[:cut], [[(0, 0), (1, 1)]] + others[cut:]
    sends = [(0, 0)] + [pair for group in first for pair in group] + [(1, 1)]
    sends += [pair for group in others[cut:] for pair in group]
    tiles = pl.pallas_call(
        functools.partial(pack_kernel, sends),
        out_shape=(jax.ShapeDtypeStruct((2, tile, width), BF16),) * chips,
        in_specs=[whole(SMEM), whole(VMEM), whole(VMEM)],
        out_specs=(whole(VMEM),) * chips,
        compiler_params=params(16),
        name="pack",
    )(row, same, crossed)
    tiles = [tiles[0]] + [swap(t, (2 * a, 2 * b)) for t, (a, b) in zip(tiles[1:], sends[1:])]

    by_send = dict(zip(sends, tiles))

    def gate(groups, name, *before):
        given = [by_send[pair] for group in groups for pair in group]
        return pl.pallas_call(
            functools.partial(gate_kernel, groups),
            out_shape=jax.ShapeDtypeStruct((tokens, total, gated), BF16),
            in_specs=[whole(SMEM)] + [whole(VMEM)] * (2 + len(given)) + [whole(HBM)] * len(before),
            out_specs=whole(HBM),
            scratch_shapes=[
                VMEM((len(groups), 4 * tile, width), F32),
                VMEM((len(groups), tokens, 4 * tokens, gated), BF16),
                pltpu.SemaphoreType.DMA((len(groups),)),
            ],
            input_output_aliases={3 + len(given): 0} if before else {},
            compiler_params=params(24),
            cost_estimate=pl.CostEstimate(
                flops=2 * tokens * total * width * gated,
                bytes_accessed=tokens * total * (gated + 3 * width),
                transcendentals=tokens * total * gated // 2,
            ),
            name=name,
        )(row, aux, gates, *given, *before)

    out = gate(last, "gate_last", gate(first, "gate_first"))
    return pair_next, out.transpose(1, 0, 2)


def solution(mesh):
    return jax.shard_map(
        functools.partial(body, count=mesh.shape["row"]),
        mesh=mesh,
        in_specs=(
            P(("groups", "row"), None, None),
            P(None, ("groups", "row"), None),
            P("groups"),
            P("groups"),
        )
        + (P(),) * 11,
        out_specs=(P(("groups", "row"), None, None), P("groups", "row", None)),
        check_vma=False,
    )
```

```python
import functools

import jax
import jax.numpy as jnp
from jax import lax
from jax.experimental import pallas as pl
from jax.experimental.pallas import tpu as pltpu
from jax.sharding import PartitionSpec as P

F32 = jnp.float32
BF16 = jnp.bfloat16
NT = (((1,), (1,)), ((), ()))
VMEM = pltpu.VMEM
SMEM = pltpu.SMEM
HBM = pltpu.HBM
LANES = 128


def whole(space):
    return pl.BlockSpec(memory_space=space)


def params(mib):
    return pltpu.CompilerParams(vmem_limit_bytes=mib * 1024 * 1024)


def fetch(sems, *pairs):
    copies = [pltpu.make_async_copy(a, b, sems.at[n]) for n, (a, b) in enumerate(pairs)]
    for copy in copies:
        copy.start()
    return copies


def finish(copies):
    for copy in copies:
        copy.wait()


def prepare_kernel(
    row_ref, depth_hbm, hom_hbm, scale_hbm, shift_hbm, src_hbm, tgt_hbm, depth_row_hbm, chain_hbm, chain_row_hbm,
    match_hbm, bias_hbm, gain_hbm, move_hbm, proj_hbm, gate_hbm, weight_hbm,
    mix_ref, item_ref, aux_ref, gates_ref,
    depth_ref, hom_ref, scale_ref, shift_ref, both_ref, depth_row_ref, chain_ref, chain_row_ref, vec_ref, sems,
):
    tokens, seqs, feats = hom_ref.shape
    pair_width = aux_ref.shape[1]
    total = depth_ref.shape[0]
    width = src_hbm.shape[0]
    half = width // 2
    gated = proj_hbm.shape[1]
    first_copies = fetch(
        sems,
        (hom_hbm, hom_ref),
        (depth_hbm, depth_ref),
        (scale_hbm, scale_ref),
        (shift_hbm, shift_ref),
        (src_hbm, both_ref.at[0:width]),
        (tgt_hbm, both_ref.at[width : 2 * width]),
        (chain_hbm, chain_ref),
        (depth_row_hbm, depth_row_ref),
        (chain_row_hbm, chain_row_ref),
        (match_hbm, vec_ref.at[0]),
        (bias_hbm, vec_ref.at[1]),
        (gain_hbm, vec_ref.at[2]),
        (move_hbm, vec_ref.at[3]),
        (proj_hbm, gates_ref.at[0]),
        (gate_hbm, gates_ref.at[1]),
        (weight_hbm, mix_ref.at[tokens * seqs : tokens * seqs + width * width]),
    )
    finish(first_copies[:6])
    values = hom_ref[...].reshape(tokens * seqs, feats)
    ones = jnp.full((feats, feats), 1.0 / feats, BF16)
    centre = values.astype(F32) - jnp.dot(values, ones, preferred_element_type=F32)
    square = centre * centre
    high = square.astype(BF16)
    low = (square - high.astype(F32)).astype(BF16)
    spread = jnp.dot(high, ones, preferred_element_type=F32) + jnp.dot(
        low, ones, preferred_element_type=F32
    )
    normed = (centre * lax.rsqrt(spread + 1e-05) * scale_ref[...] + shift_ref[...]).astype(BF16)
    turned = lax.dot_general(both_ref[width : 2 * width], normed, NT, preferred_element_type=F32)
    plain = lax.dot_general(normed, both_ref[0:width], NT, preferred_element_type=F32)
    first = row_ref[0] * tokens
    row_pos = lax.broadcasted_iota(jnp.int32, (seqs, width), 0)
    lane = lax.broadcasted_iota(jnp.int32, (half, 2 * seqs), 1)
    seq_pos = jnp.where(lane < seqs, lane, lane - seqs)
    for n in range(tokens):
        depth = depth_ref[first + n]
        rows = slice(n * seqs, (n + 1) * seqs)
        mix_ref[rows, 0:width] = jnp.where(row_pos < depth, plain[rows], 0.0).astype(BF16)
        joint = jnp.concatenate([turned[0:half, rows], turned[half:width, rows]], axis=1)
        item_ref[0, n * half : (n + 1) * half] = jnp.where(seq_pos < depth, joint, 0.0).astype(BF16)

    finish(first_copies[6:])
    same = lax.broadcasted_iota(jnp.int32, (total, total), 0) == lax.broadcasted_iota(
        jnp.int32, (total, total), 1
    )
    fill = jnp.ones((total, pair_width), BF16)

    def column(ref):
        diagonal = jnp.where(same, ref[...].astype(F32), 0.0).astype(BF16)
        return jnp.dot(diagonal, fill, preferred_element_type=F32)

    aux_ref[0:total] = 1.0 / jnp.maximum(column(depth_row_ref), 1.0)
    aux_ref[total : 2 * total] = column(chain_row_ref)
    for n in range(tokens):
        own = jnp.full((1, pair_width), depth_ref[first + n], jnp.int32).astype(F32)
        aux_ref[2 * total + n : 2 * total + n + 1] = 1.0 / jnp.maximum(own, 1.0)
        label = jnp.full((1, pair_width), chain_ref[first + n], jnp.int32).astype(F32)
        aux_ref[2 * total + 16 + n : 2 * total + 17 + n] = label
    for n in range(4):
        aux_ref[2 * total + 32 + n : 2 * total + 33 + n] = vec_ref[n]


def mix_kernel(factor, mix_ref, out_ref, wide_ref):
    half = factor // 2
    seqs = out_ref.shape[1] // factor
    width = mix_ref.shape[1]
    lefts = mix_ref.shape[0] - factor * factor
    tokens = lefts // seqs
    wide_ref[...] = mix_ref[lefts : lefts + factor * factor].astype(F32)

    def one(q, carry):
        pair = [wide_ref[pl.ds(q + t * half, factor, stride=factor), :] for t in (0, 1)]
        rhs = jnp.concatenate(pair, axis=1).astype(BF16)
        mixed = jnp.dot(mix_ref[0:lefts, 0:factor], rhs, preferred_element_type=F32).astype(BF16)
        for n in range(tokens):
            rows = slice(n * seqs, (n + 1) * seqs)
            cols = slice(n % 2 * width, (n % 2 + 1) * width)
            for t in (0, 1):
                spot = pl.ds(pl.multiple_of((2 * q + t) * seqs, seqs), seqs)
                out_ref[n // 2, spot, cols] = mixed[rows, t * width : (t + 1) * width]
        return carry

    lax.fori_loop(0, half, one, 0, unroll=4)


def join_kernel(*refs):
    spot = 0
    for piece in refs[:-1]:
        refs[-1][spot : spot + piece.shape[0]] = piece[...]
        spot += piece.shape[0]


def by_core(row, pair):
    return jnp.where((row & 1) == 1, pair[1], pair[0])


def spread_items(row, wide_ref, pieces, orders):
    for piece, pairs in zip(pieces, orders):
        size = piece.shape[1]
        for m, pair in enumerate(pairs):
            spot = pl.ds(pl.multiple_of((row ^ by_core(row, pair)) * size, size), size)
            wide_ref[spot, :] = piece[m].astype(F32)


def first_half_kernel(orders, row_ref, state_ref, aux_ref, *rest):
    pieces, (wide_ref, state_out, aux_out) = rest[:-3], rest[-3:]
    state_out[...] = state_ref[...]
    aux_out[...] = aux_ref[...]
    spread_items(row_ref[0], wide_ref, pieces, orders)


def pair_kernel(orders, row_ref, aux_ref, state_ref, y_ref, wide_in, *rest):
    pieces, (next_ref, same_ref, cross_ref, wide_ref, lhs_ref) = rest[:-5], rest[-5:]
    step = pl.program_id(0)
    block, total, width = state_ref.shape
    lanes = pieces[0].shape[2]
    count = 2 * same_ref.shape[0]
    tokens = total // count
    groups = wide_ref.shape[0] // total

    @pl.when(step == 0)
    def _():
        spread_items(row_ref[0], wide_ref, pieces, orders)

        def one(q, carry):
            cols = pl.ds(pl.multiple_of(q * lanes, lanes), lanes)
            lhs_ref[:, cols] = wide_ref[pl.ds(q, total, stride=groups), :].astype(BF16)
            return carry

        lax.fori_loop(0, groups, one, 0, unroll=4)

    base = 2 * total
    match = aux_ref[base + 32 : base + 33]
    bias = aux_ref[base + 33 : base + 34]
    done = []
    for t in range(block):
        if t % 2 == 0:
            prod = jnp.dot(lhs_ref[...], y_ref[step * (block // 2) + t // 2], preferred_element_type=F32)
        own = step * block + t
        inv_own = aux_ref[pl.ds(base + own, 1)]
        label = aux_ref[pl.ds(base + 16 + own, 1)]
        extra = jnp.where(aux_ref[total:base] == label, match, 0.0) + bias
        value = prod[:, t % 2 * width : (t % 2 + 1) * width] * jnp.maximum(aux_ref[0:total], inv_own) + extra
        value = state_ref[t].astype(F32) + value
        next_ref[t] = value.astype(BF16)
        done.append(value)
    size = block * tokens
    spot = pl.ds(pl.multiple_of(step * size, size), size)
    for core in (0, 1):

        @pl.when((row_ref[0] & 1) == core)
        def _():
            for d in range(count):
                rows = slice(d * tokens, (d + 1) * tokens)
                tile = jnp.concatenate([value[rows] for value in done], axis=0).astype(BF16)
                (same_ref if (d & 1) == core else cross_ref)[d // 2, spot, :] = tile


def pack_kernel(pairs, row_ref, same_ref, crossed_ref, *outs):
    chip = row_ref[0] >> 1
    for core in (0, 1):

        @pl.when((row_ref[0] & 1) == core)
        def _():
            for pair, out_ref in zip(pairs, outs):
                out_ref[core] = same_ref[chip ^ pair[core]]
                out_ref[1 - core] = crossed_ref[chip ^ pair[core]]


def gate_kernel(groups, row_ref, aux_ref, gates_ref, *rest):
    tiles, (out_hbm, wide_ref, done_ref, sems) = rest[: 2 * len(groups)], rest[-4:]
    tokens, total, gated = out_hbm.shape
    rows, width = tiles[0].shape[1:]
    chip = row_ref[0] >> 1
    band = 4 * tokens
    gain = aux_ref[2 * total + 34 : 2 * total + 35]
    shift = aux_ref[2 * total + 35 : 2 * total + 36]
    ones = jnp.full((width, width), 1.0 / width, BF16)
    none = jnp.zeros((width, width), BF16)
    means = jnp.concatenate(
        [jnp.concatenate([ones, none], axis=1), jnp.concatenate([none, ones], axis=1)], axis=0
    )
    weights = jnp.concatenate([gates_ref[0], gates_ref[1]], axis=1)
    copies = []
    for n, pairs in enumerate(groups):
        for m, pair in enumerate(pairs):
            source = chip ^ by_core(row_ref[0], pair)
            for core in (0, 1):
                spot = pl.ds(pl.multiple_of(((source & 1) * 2 + core) * rows, rows), rows)
                wide_ref[n, spot, :] = tiles[2 * n + m][core].astype(F32)
        place = source >> 1
        parts = [wide_ref[n, pl.ds(j, band, stride=tokens), :] for j in range(tokens)]
        half = tokens // 2
        pair = jnp.concatenate(
            [jnp.concatenate(parts[:half], axis=0), jnp.concatenate(parts[half:], axis=0)], axis=1
        )
        centre = pair - jnp.dot(pair.astype(BF16), means, preferred_element_type=F32)
        square = (centre * centre).astype(BF16)
        spread = jnp.dot(square, means, preferred_element_type=F32)
        scaled = centre * lax.rsqrt(spread + 1e-05)
        scaled = jnp.concatenate([scaled[:, 0:width], scaled[:, width : 2 * width]], axis=0)
        normed = (scaled * gain + shift).astype(BF16)
        mixed = jnp.dot(normed, weights, preferred_element_type=F32)
        result = (mixed[:, 0:gated] * (0.5 + 0.5 * jnp.tanh(0.5 * mixed[:, gated : 2 * gated]))).astype(BF16)
        for j in range(tokens):
            done_ref[n, j] = result[j * band : (j + 1) * band]
        copies.append(
            pltpu.make_async_copy(
                done_ref.at[n],
                out_hbm.at[:, pl.ds(pl.multiple_of(place * band, band), band), :],
                sems.at[n],
            )
        )
        copies[-1].start()
    finish(copies)


def fixed(*shape):
    return pl.BlockSpec(shape, lambda g: (0,) * len(shape))


def body(
    pairwise_state,
    homolog_embedding,
    alignment_depth,
    chain_labels,
    homolog_layer_scale,
    homolog_layer_shift,
    outer_source_matrix,
    outer_target_matrix,
    output_weight,
    output_bias,
    chain_match,
    pairwise_norm_gain,
    pairwise_norm_bias,
    input_projection_weight,
    input_gate_weight,
    *,
    count,
):
    tokens, total, width = pairwise_state.shape
    seqs, _, feats = homolog_embedding.shape
    factor = outer_source_matrix.shape[1]
    half = factor // 2
    inner = factor * seqs
    gated = input_projection_weight.shape[1]
    row = lax.axis_index("row").astype(jnp.int32).reshape(1)

    def swap(array, bits):
        bits = bits if isinstance(bits, tuple) else (bits, bits)
        return lax.ppermute(array, "row", [(r, r ^ bits[r & 1]) for r in range(count)])

    def staggered(items):
        cut = (len(items) + 1) // 2
        return list(zip(items, items[cut:] + items[:cut]))

    aux_rows = 2 * total + 40
    part = tokens * half
    mix_rows = tokens * seqs + factor * factor
    to_mix, item, aux, gates = pl.pallas_call(
        prepare_kernel,
        out_shape=(
            jax.ShapeDtypeStruct((mix_rows, width), BF16),
            jax.ShapeDtypeStruct((1, part, 2 * seqs), BF16),
            jax.ShapeDtypeStruct((aux_rows, width), F32),
            jax.ShapeDtypeStruct((2, width, gated), BF16),
        ),
        in_specs=[whole(SMEM)] + [whole(HBM)] * 16,
        out_specs=(whole(VMEM),) * 4,
        scratch_shapes=[
            SMEM((total,), jnp.int32),
            VMEM((tokens, seqs, feats), BF16),
            VMEM((1, feats), F32),
            VMEM((1, feats), F32),
            VMEM((2 * factor, feats), BF16),
            VMEM((1, total), jnp.int32),
            SMEM((total,), jnp.int32),
            VMEM((1, total), jnp.int32),
            VMEM((4, 1, width), F32),
            pltpu.SemaphoreType.DMA((16,)),
        ],
        name="prepare",
    )(
        row,
        alignment_depth,
        homolog_embedding.transpose(1, 0, 2),
        homolog_layer_scale.reshape(1, feats),
        homolog_layer_shift.reshape(1, feats),
        outer_source_matrix.T,
        outer_target_matrix.T,
        alignment_depth.reshape(1, total),
        chain_labels,
        chain_labels.reshape(1, total),
        chain_match.reshape(1, width),
        output_bias.reshape(1, width),
        pairwise_norm_gain.reshape(1, width),
        pairwise_norm_bias.reshape(1, width),
        input_projection_weight,
        input_gate_weight,
        output_weight,
    )

    def mixed(to_mix):
        return pl.pallas_call(
            functools.partial(mix_kernel, factor),
            out_shape=jax.ShapeDtypeStruct((tokens // 2, inner, 2 * width), BF16),
            in_specs=[whole(VMEM)],
            out_specs=whole(VMEM),
            scratch_shapes=[VMEM((factor * factor, width), F32)],
            compiler_params=params(16),
            cost_estimate=pl.CostEstimate(
                flops=2 * tokens * seqs * factor * factor * width,
                bytes_accessed=2 * inner * tokens * width,
                transcendentals=0,
            ),
            name="mix",
        )(to_mix)

    def joined(*pieces):
        return pl.pallas_call(
            join_kernel,
            out_shape=jax.ShapeDtypeStruct((sum(x.shape[0] for x in pieces), part, 2 * seqs), BF16),
            in_specs=[whole(VMEM)] * len(pieces),
            out_specs=whole(VMEM),
            compiler_params=params(16),
            name="join",
        )(*pieces)

    chips = count // 2
    turn = staggered([4 * k for k in range(count // 4 - 1, 0, -1)])
    direct = [swap(item, pair) for pair in turn]
    own_came = swap(item, 2)
    own_early = swap(item, 1)
    staged = pl.pallas_call(
        join_kernel,
        out_shape=jax.ShapeDtypeStruct(to_mix.shape, BF16),
        in_specs=[whole(VMEM)],
        out_specs=whole(VMEM),
        compiler_params=params(16),
        name="stage",
    )(to_mix)
    direct[0], staged = lax.optimization_barrier((direct[0], staged))
    came = [swap(d, 2) for d in direct]
    *direct, staged = lax.optimization_barrier((*direct, staged))
    y = mixed(staged)
    held = joined(*direct)
    held, y = lax.optimization_barrier((held, y))
    early = swap(held, 1)
    *came, own_came, own_early, y = lax.optimization_barrier((*came, own_came, own_early, y))
    came = joined(*came)
    own_late = swap(own_came, 1)
    late = swap(came, 1)

    def ranks(bits):
        return [(a ^ bits, b ^ bits) if bits in (0, 2) else (b ^ bits, a ^ bits) for a, b in turn]

    wide, state, aux = pl.pallas_call(
        functools.partial(
            first_half_kernel, [[(0, 0)], [(1, 1)], [(2, 2)], ranks(0), ranks(1), ranks(2)]
        ),
        out_shape=(
            jax.ShapeDtypeStruct((count * part, 2 * seqs), F32),
            jax.ShapeDtypeStruct((tokens, total, width), BF16),
            jax.ShapeDtypeStruct((aux_rows, width), F32),
        ),
        in_specs=[whole(SMEM)] + [whole(VMEM)] * 8,
        out_specs=(whole(VMEM),) * 3,
        compiler_params=params(16),
        name="first_half",
    )(row, pairwise_state, aux, item, own_early, own_came, held, early, came)

    block = 4
    tile = tokens * tokens
    pair_next, same, cross, _ = pl.pallas_call(
        functools.partial(pair_kernel, [[(3, 3)], ranks(3)]),
        grid=(tokens // block,),
        out_shape=(
            jax.ShapeDtypeStruct((tokens, total, width), BF16),
            jax.ShapeDtypeStruct((chips, tile, width), BF16),
            jax.ShapeDtypeStruct((chips, tile, width), BF16),
            jax.ShapeDtypeStruct((count * part, 2 * seqs), F32),
        ),
        in_specs=[whole(SMEM), whole(VMEM), pl.BlockSpec((block, total, width), lambda g: (g, 0, 0))]
        + [whole(VMEM)] * 4,
        out_specs=(pl.BlockSpec((block, total, width), lambda g: (g, 0, 0)),) + (whole(VMEM),) * 3,
        scratch_shapes=[VMEM((total, inner), BF16)],
        input_output_aliases={4: 3},
        compiler_params=params(16),
        cost_estimate=pl.CostEstimate(
            flops=2 * total * inner * tokens * width,
            bytes_accessed=2 * inner * tokens * width + 8 * tokens * total * width,
            transcendentals=0,
        ),
        name="pair",
    )(row, aux, state, y, wide, own_late, late)

    crossed = swap(cross, 1)
    falling = [(k, k - 1) for k in range(chips - 1, 1, -2)]
    inward = [falling[m // 2] if m % 2 == 0 else falling[-1 - m // 2] for m in range(len(falling))]
    mirrored = [inward[m ^ 1] if (m ^ 1) < len(inward) else inward[m] for m in range(len(inward))]
    others = [[(a[m], b[m]) for m in (0, 1)] for a, b in zip(inward, mirrored)]
    cut = (len(others) + 1) // 2
    first, last = others[:cut], [[(0, 0), (1, 1)]] + others[cut:]
    sends = [(0, 0)] + [pair for group in first for pair in group] + [(1, 1)]
    sends += [pair for group in others[cut:] for pair in group]
    tiles = pl.pallas_call(
        functools.partial(pack_kernel, sends),
        out_shape=(jax.ShapeDtypeStruct((2, tile, width), BF16),) * chips,
        in_specs=[whole(SMEM), whole(VMEM), whole(VMEM)],
        out_specs=(whole(VMEM),) * chips,
        compiler_params=params(16),
        name="pack",
    )(row, same, crossed)
    tiles = [tiles[0]] + [swap(t, (2 * a, 2 * b)) for t, (a, b) in zip(tiles[1:], sends[1:])]

    by_send = dict(zip(sends, tiles))

    def gate(groups, name, *before):
        given = [by_send[pair] for group in groups for pair in group]
        return pl.pallas_call(
            functools.partial(gate_kernel, groups),
            out_shape=jax.ShapeDtypeStruct((tokens, total, gated), BF16),
            in_specs=[whole(SMEM)] + [whole(VMEM)] * (2 + len(given)) + [whole(HBM)] * len(before),
            out_specs=whole(HBM),
            scratch_shapes=[
                VMEM((len(groups), 4 * tile, width), F32),
                VMEM((len(groups), tokens, 4 * tokens, gated), BF16),
                pltpu.SemaphoreType.DMA((len(groups),)),
            ],
            input_output_aliases={3 + len(given): 0} if before else {},
            compiler_params=params(24),
            cost_estimate=pl.CostEstimate(
                flops=2 * tokens * total * width * gated,
                bytes_accessed=tokens * total * (gated + 3 * width),
                transcendentals=tokens * total * gated // 2,
            ),
            name=name,
        )(row, aux, gates, *given, *before)

    out = gate(last, "gate_last", gate(first, "gate_first"))
    return pair_next, out.transpose(1, 0, 2)


def solution(mesh):
    return jax.shard_map(
        functools.partial(body, count=mesh.shape["row"]),
        mesh=mesh,
        in_specs=(
            P(("groups", "row"), None, None),
            P(None, ("groups", "row"), None),
            P("groups"),
            P("groups"),
        )
        + (P(),) * 11,
        out_specs=(P(("groups", "row"), None, None), P("groups", "row", None)),
        check_vma=False,
    )
```
